512 devices in a mesh: gx: 32 (over z, y_hi), gy: 4 (over x), gz: 4 (over y_lo, core).
Axes of the slice: x: 4, y: 4 (y_hi: 2, y_lo: 2; y = y_hi * 2 + y_lo), z: 16, core: 2. Of those that a mesh axis runs over, the one named last changes fastest.
Arguments:
- field: bfloat16 [32, 96, 32, 512], P(None, 'gx', 'gy', 'gz'), may hold values from -6 to 6
- cotangent: bfloat16 [32, 96, 32, 512], P(None, 'gx', 'gy', 'gz'), may hold values from -6 to 6
- cosmology: float32 [2], replicated, may hold values from -1 to 1
- lift_weight: float32 [2, 256], replicated, may hold values from -4 to 4
- lift_bias: float32 [256], replicated, may hold values from -3 to 3
- style_weight: float32 [256, 32], replicated, may hold values from -0.375 to 0.375
- style_bias: float32 [32], replicated, may hold values from -2 to 2
- kernel: float32 [32, 32, 3, 3, 3], replicated, may hold values from -0.21875 to 0.21875
- offset: float32 [32], replicated, may hold values from -3 to 3
Outputs:
- grad_field: bfloat16 [32, 96, 32, 512], P(None, 'gx', 'gy', 'gz')
- grad_kernel: float32 [32, 32, 3, 3, 3], replicated
- grad_offset: float32 [32], replicated
- grad_lift: float32 [2, 256], replicated
- grad_liftbias: float32 [256], replicated
- grad_style: float32 [256, 32], replicated
- grad_stylebias: float32 [32], replicated
The draws below stay inside these ranges and needn't reach their ends.
All inputs are finite; a program needn't handle non-finite values.
Results may differ from the reference program's by a relative error of at most 0.013.
Values may be sent and summed in bfloat16 or wider, within the bound.
No kernel may reach another device: no remote copies, remote signals or barrier semaphores. Data moves between devices by JAX's collectives and lax.ppermute only.
A program may use at most 64 MiB of HBM per device.

```python
import jax
import jax.numpy as jnp
from jax import lax

C = 32
HID = 256
NPAR = 2
CX = 3
NX = 96
NY = 32
NZ = 512


def steps_of(key, shape, split, smallest, largest):
    level = 1.0
    for axis_at, shards_of in split:
        steps = jax.random.uniform(jax.random.fold_in(jax.random.fold_in(key, 6), axis_at), (shards_of,), jnp.float32, smallest / len(split), largest / len(split))
        level = level * jnp.repeat(jnp.exp(steps), shape[axis_at] // shards_of).reshape((-1,) + (1,) * (len(shape) - 1 - axis_at))
    return level


def normal_values(own_key, shape, spread, limit, cuts=(), kind=jnp.bfloat16):
    array = spread * jax.random.normal(own_key, shape, jnp.float32)
    if cuts:
        array = array * steps_of(own_key, shape, cuts, -0.22, 0.18)
    return jnp.clip(array, -limit, limit).astype(kind)


def setup_inputs(seed: int = 0) -> dict:
    arg_keys = jax.random.split(jax.random.key(seed), 10)
    field = normal_values(arg_keys[0], (C, NX, NY, NZ), 1.0, 6.0, ((1, 32), (2, 4), (3, 4)))
    cotangent = normal_values(arg_keys[1], (C, NX, NY, NZ), 1.0, 6.0, ((1, 32), (2, 4), (3, 4)))
    cosmology = jnp.clip(jax.random.uniform(arg_keys[2], (NPAR,), jnp.float32, -1.0, 1.0), -1.0, 1.0)
    lift_weight = normal_values(arg_keys[3], (NPAR, HID), NPAR ** -0.5, 4.0, (), jnp.float32)
    lift_bias = normal_values(arg_keys[4], (HID,), 0.5, 3.0, (), jnp.float32)
    style_weight = normal_values(arg_keys[5], (HID, C), HID ** -0.5, 0.375, (), jnp.float32)
    style_bias = normal_values(arg_keys[6], (C,), 0.3, 2.0, (), jnp.float32)
    kernel = normal_values(arg_keys[7], (C, C, 3, 3, 3), (C * 27) ** -0.5, 0.21875, (), jnp.float32)
    offset = normal_values(arg_keys[8], (C,), 0.5, 3.0, (), jnp.float32)
    return {"field": field, "cotangent": cotangent, "cosmology": cosmology, "lift_weight": lift_weight, "lift_bias": lift_bias, "style_weight": style_weight, "style_bias": style_bias, "kernel": kernel, "offset": offset}


demod_eps = 1e-06
clip_eps = 1e-06

def silu_slope(values):
    logistic = jax.nn.sigmoid(values)
    return logistic * (1.0 + values * (1.0 - logistic))

def modulate(cosmology, lift_weight, lift_bias, style_weight, style_bias, kernel):
    lifted = jnp.dot(cosmology[None, :], lift_weight, precision=lax.Precision.HIGHEST)[0] + lift_bias
    hidden = jax.nn.silu(lifted)
    styles = jnp.dot(hidden[None, :], style_weight, precision=lax.Precision.HIGHEST)[0] + style_bias + 1.0
    modded = kernel * styles[None, :, None, None, None]
    inv_norm = lax.rsqrt(lax.optimization_barrier(jnp.sum(modded * modded, axis=(1, 2, 3, 4))) + demod_eps)
    scaled = (modded * inv_norm[:, None, None, None, None]).astype(jnp.bfloat16)
    return (lifted, hidden, styles, modded, inv_norm, scaled)

def param_backward(sums_kernel, sums_offset, cosmology, style_weight, kernel, lifted, hidden, styles, modded, inv_norm):
    projected = lax.optimization_barrier(jnp.sum(sums_kernel * modded, axis=(1, 2, 3, 4)))
    mod_grad = inv_norm[:, None, None, None, None] * (sums_kernel - modded * (inv_norm * inv_norm * projected)[:, None, None, None, None])
    kernel_raw = mod_grad * styles[None, :, None, None, None]
    styles_grad = lax.optimization_barrier(jnp.sum(mod_grad * kernel, axis=(0, 2, 3, 4)))
    hidden_grad = jnp.dot(style_weight, styles_grad[:, None], precision=lax.Precision.HIGHEST)[:, 0]
    lifted_grad = hidden_grad * silu_slope(lifted)
    style_raw = hidden[:, None] * styles_grad[None, :]
    lift_raw = cosmology[:, None] * lifted_grad[None, :]
    members = (kernel_raw, sums_offset, lift_raw, lifted_grad, style_raw, styles_grad)
    square_sum = sum((jnp.sum(member * member) for member in members))
    entries = sum((member.size for member in members))
    factor = jnp.minimum(1.0, lax.rsqrt(square_sum / entries + clip_eps))
    return tuple((factor * member for member in members))

def conv_valid(operand, filters):
    return lax.conv_general_dilated(operand[None].astype(jnp.float32), filters.astype(jnp.float32), (1, 1, 1), 'VALID', dimension_numbers=('NCDHW', 'OIDHW', 'NCDHW'), precision=lax.Precision.HIGHEST)[0]

def weight_conv(operand, upstream):
    result = lax.conv_general_dilated(operand[None].astype(jnp.float32), upstream[None].astype(jnp.float32), (1, 1, 1), 'VALID', dimension_numbers=('CNDHW', 'IODHW', 'NCDHW'), precision=lax.Precision.HIGHEST)
    return jnp.transpose(result, (1, 0, 2, 3, 4))

def reference(field, cotangent, cosmology, lift_weight, lift_bias, style_weight, style_bias, kernel, offset):
    lifted, hidden, styles, modded, inv_norm, scaled = modulate(cosmology, lift_weight, lift_bias, style_weight, style_bias, kernel)
    flipped = jnp.transpose(scaled[:, :, ::-1, ::-1, ::-1], (1, 0, 2, 3, 4))
    padded = jnp.pad(field, ((0, 0), (1, 1), (1, 1), (1, 1)), mode='wrap')
    slab_count = NX // CX

    def forward_slab(slab_index):
        first_plane = (slab_index * CX).astype(jnp.int32)
        slab_block = lax.dynamic_slice_in_dim(padded, first_plane, CX + 2, 1)
        preact = conv_valid(slab_block, scaled) + offset[:, None, None, None]
        slab_cotan = lax.dynamic_slice_in_dim(cotangent, first_plane, CX, 1)
        upstream = (slab_cotan.astype(jnp.float32) * silu_slope(preact)).astype(jnp.bfloat16)
        part_kernel = weight_conv(slab_block, upstream)
        part_offset = lax.optimization_barrier(jnp.sum(upstream.astype(jnp.float32), axis=(1, 2, 3)))
        return (upstream, part_kernel, part_offset)
    upstreams, kernel_parts, offset_parts = lax.map(forward_slab, jnp.arange(slab_count, dtype=jnp.int32))
    upstream_all = jnp.moveaxis(upstreams, 0, 1).reshape(C, NX, NY, NZ)
    grad_pad = jnp.pad(upstream_all, ((0, 0), (1, 1), (1, 1), (1, 1)), mode='wrap')

    def input_slab(slab_index):
        first_plane = (slab_index * CX).astype(jnp.int32)
        slab_block = lax.dynamic_slice_in_dim(grad_pad, first_plane, CX + 2, 1)
        return conv_valid(slab_block, flipped).astype(jnp.bfloat16)
    grad_slabs = lax.map(input_slab, jnp.arange(slab_count, dtype=jnp.int32))
    grad_field = jnp.moveaxis(grad_slabs, 0, 1).reshape(C, NX, NY, NZ)
    sums_kernel = lax.optimization_barrier(jnp.sum(kernel_parts, axis=0))
    sums_offset = lax.optimization_barrier(jnp.sum(offset_parts, axis=0))
    grad_kernel, grad_offset, grad_lift, grad_liftbias, grad_style, grad_stylebias = param_backward(sums_kernel, sums_offset, cosmology, style_weight, kernel, lifted, hidden, styles, modded, inv_norm)
    return (grad_field, grad_kernel, grad_offset, grad_lift, grad_liftbias, grad_style, grad_stylebias)
```

```python
import numpy as np
import jax
import jax.numpy as jnp
from jax import lax
from jax.experimental import pallas as pl
from jax.experimental.pallas import tpu as pltpu
from jax.sharding import PartitionSpec as P

demod_eps = 1e-06
clip_eps = 1e-06

C = 32
TAPS = 27
PITCH = 132
PLANE = 14 * 128
OUT = 11 * 128
GRAD = 9 * 128
FIELD_ROWS = 7 * 12 * C
COT_ROWS = 5 * 10 * C
f32 = jnp.float32
bf16 = jnp.bfloat16
VMEM = pl.BlockSpec(memory_space=pltpu.VMEM)


def call(kernel, outs, n_in, flops=0, limit=40):
    return pl.pallas_call(
        kernel,
        out_shape=outs,
        in_specs=[VMEM] * n_in,
        out_specs=[VMEM] * len(outs),
        cost_estimate=pl.CostEstimate(flops=flops, bytes_accessed=1 << 20, transcendentals=0),
        compiler_params=pltpu.CompilerParams(vmem_limit_bytes=limit * 1024 * 1024),
    )


def shape(*dims, dtype=bf16):
    return jax.ShapeDtypeStruct(dims, dtype)


def split_kernel(field_ref, cot_ref, perm_ref, low_ref, high_ref, mid_ref):
    def rows(ref, x):
        block = ref[:, x].astype(f32).reshape(C * 8, 128).astype(bf16)
        moved = jnp.dot(perm_ref[...], block, preferred_element_type=f32)
        return moved.astype(bf16).reshape(8, C, 128)

    f0, f1, f2 = (rows(field_ref, x) for x in range(3))
    c0, c1, c2 = (rows(cot_ref, x) for x in range(3))
    low_ref[0], low_ref[1], low_ref[2] = f0, f1, c0
    high_ref[0], high_ref[1], high_ref[2] = f1, f2, c2
    mid_ref[0] = c1


def planes(low_ref, high_ref, mid_ref, left_ref, right_ref):
    field = (
        (left_ref, 0), (left_ref, 1), (low_ref, 0), (low_ref, 1), (high_ref, 1), (right_ref, 0), (right_ref, 1),
    )
    cot = ((left_ref, 2), (low_ref, 2), (mid_ref, 0), (high_ref, 2), (right_ref, 2))
    return field, cot


def pack_kernel(low_ref, high_ref, mid_ref, left_ref, right_ref, up_ref, down_ref):
    field, cot = planes(low_ref, high_ref, mid_ref, left_ref, right_ref)
    for n, (ref, at) in enumerate(field):
        up_ref[2 * n : 2 * n + 2] = ref[at, 6:8]
        down_ref[2 * n : 2 * n + 2] = ref[at, 0:2]
    for n, (ref, at) in enumerate(cot):
        up_ref[14 + n] = ref[at, 7]
        down_ref[14 + n] = ref[at, 0]


def gather_kernel(
    low_ref, high_ref, mid_ref, left_ref, right_ref, up_ref, down_ref, pick_ref,
    field_out, cot_out, hi_ref, lo_ref,
):
    field, cot = planes(low_ref, high_ref, mid_ref, left_ref, right_ref)
    for n, (ref, at) in enumerate(field):
        field_out[n, 0:2] = up_ref[2 * n : 2 * n + 2]
        field_out[n, 2:10] = ref[at]
        field_out[n, 10:12] = down_ref[2 * n : 2 * n + 2]
    for n, (ref, at) in enumerate(cot):
        cot_out[n, 0] = up_ref[14 + n]
        cot_out[n, 1:9] = ref[at]
        cot_out[n, 9] = down_ref[14 + n]

    def faces(pick, rows):
        return lax.dot_general(
            pick, rows, (((1,), (1,)), ((), ())), preferred_element_type=f32
        ).astype(bf16)

    frows = field_out[...].reshape(FIELD_ROWS, 128)
    crows = cot_out[...].reshape(COT_ROWS, 128)
    hi_ref[:, :FIELD_ROWS] = faces(pick_ref[0], frows)
    lo_ref[:, :FIELD_ROWS] = faces(pick_ref[1], frows)
    hi_ref[:, FIELD_ROWS:] = faces(pick_ref[2], crows)
    lo_ref[:, FIELD_ROWS:] = faces(pick_ref[3], crows)


def silu_slope(values):
    logistic = jax.nn.sigmoid(values)
    return logistic * (1.0 + values * (1.0 - logistic))


def conv_kernel(
    field_ref, cot_ref, before_ref, after_ref, place_ref, mask_ref, fwd_ref, bwd_ref, offset_ref,
    grad_ref, sums_ref,
    edge, plane, cols, cot_flat, up, ucols, total,
):
    def placed(faces, place):
        return lax.dot_general(
            faces, place, (((0,), (0,)), ((), ())), preferred_element_type=f32
        )

    edge[:FIELD_ROWS] = (
        placed(before_ref[:, :FIELD_ROWS], place_ref[0]) + placed(after_ref[:, :FIELD_ROWS], place_ref[1])
    ).astype(bf16)
    edge[FIELD_ROWS:] = (
        placed(before_ref[:, FIELD_ROWS:], place_ref[2]) + placed(after_ref[:, FIELD_ROWS:], place_ref[3])
    ).astype(bf16)

    @pl.loop(0, 7)
    def _(x):
        pieces = []
        for y in range(12):
            sides = edge[pl.ds(pl.multiple_of((x * 12 + y) * C, C), C), :]
            pieces += [sides[:, 0:2], field_ref[x, y], sides[:, 2:4]]
        plane[...] = jnp.concatenate(
            pieces + [jnp.zeros((C, PLANE - 12 * PITCH), bf16)], axis=1
        )
        for t in range(9):
            at = (t // 3) * PITCH + t % 3
            cols[x, t * C : (t + 1) * C, :] = plane[:, at : at + OUT]

    total[...] = jnp.zeros_like(total)

    @pl.loop(0, 5)
    def _(x):
        pieces = []
        for y in range(10):
            sides = edge[pl.ds(pl.multiple_of(FIELD_ROWS + (x * 10 + y) * C, C), C), :]
            pieces += [sides[:, 0:1], cot_ref[x, y], sides[:, 1:2], jnp.zeros((C, 2), bf16)]
        pieces.append(jnp.zeros((C, OUT - 10 * PITCH), bf16))
        beside = jnp.concatenate(pieces, axis=1).astype(f32)
        block = cols[pl.ds(x, 3)].reshape(3 * 9 * C, OUT)
        preact = jnp.dot(fwd_ref[...], block, preferred_element_type=f32) + offset_ref[...]
        upstream = (beside * silu_slope(preact)).astype(bf16)
        up[:, :OUT] = upstream
        up[:, OUT:] = jnp.zeros((C, 128), bf16)
        for t in range(9):
            at = (t // 3) * PITCH + t % 3
            ucols[x, t * C : (t + 1) * C, :] = up[:, at : at + GRAD]

        @pl.when((x >= 1) & (x <= 3))
        def _():
            own = upstream.astype(f32) * mask_ref[...]
            total[:, 864:] += jnp.sum(own, axis=1, keepdims=True)
            total[:, :864] += lax.dot_general(
                own.astype(bf16), block, (((1,), (1,)), ((), ())), preferred_element_type=f32
            )

    for s in range(4):
        for l in range(8):
            at = (s * 8 + l) * 8
            if l < 7:
                sums_ref[at : at + 8] = total[8 * s : 8 * s + 8, 128 * l : 128 * l + 128]
            else:
                sums_ref[at : at + 8] = jnp.zeros((8, 128), f32)

    @pl.loop(0, 3)
    def _(x):
        block = ucols[pl.ds(x, 3)].reshape(3 * 9 * C, GRAD)
        grad = jnp.dot(bwd_ref[...], block, preferred_element_type=f32).astype(bf16)
        for y in range(8):
            grad_ref[x, y] = grad[:, y * PITCH : y * PITCH + 128]


def constants():
    perm = np.zeros((256, 256), np.float32)
    for y in range(8):
        for c in range(C):
            perm[y * C + c, c * 8 + y] = 1
    pick = np.zeros((4, 8, 128), np.float32)
    pick[0, 0, 126] = pick[0, 1, 127] = 1
    pick[1, 0, 0] = pick[1, 1, 1] = 1
    pick[2, 0, 127] = 1
    pick[3, 0, 0] = 1
    place = np.zeros((4, 8, 128), np.float32)
    place[0, 0, 0] = place[0, 1, 1] = 1
    place[1, 0, 2] = place[1, 1, 3] = 1
    place[2, 0, 0] = 1
    place[3, 0, 1] = 1
    mask = np.zeros((1, OUT), np.float32)
    for y in range(1, 9):
        mask[0, y * PITCH + 1 : y * PITCH + 129] = 1
    return (
        jnp.asarray(perm, bf16), jnp.asarray(pick, bf16), jnp.asarray(place, bf16), jnp.asarray(mask, f32),
    )


def shifts(axis):
    n = lax.axis_size(axis)
    ahead = [(i, (i + 1) % n) for i in range(n)]
    return ahead, [(j, i) for i, j in ahead]


def modulate(cosmology, lift_weight, lift_bias, style_weight, style_bias, kernel):
    lifted = (
        jnp.dot(cosmology[None, :], lift_weight, precision=lax.Precision.HIGHEST)[0] + lift_bias
    )
    hidden = jax.nn.silu(lifted)
    styles = (
        jnp.dot(hidden[None, :], style_weight, precision=lax.Precision.HIGHEST)[0]
        + style_bias
        + 1.0
    )
    modded = kernel * styles[None, None, :]
    inv_norm = lax.rsqrt(jnp.sum(modded * modded, axis=(0, 2)) + demod_eps)
    scaled = (modded * inv_norm[None, :, None]).astype(bf16)
    return (lifted, hidden, styles, modded, inv_norm, scaled)


def param_backward(
    sums_kernel, sums_offset, cosmology, style_weight, kernel, lifted, hidden, styles, modded, inv_norm
):
    projected = jnp.sum(sums_kernel * modded, axis=(0, 2))
    mod_grad = inv_norm[None, :, None] * (
        sums_kernel - modded * (inv_norm * inv_norm * projected)[None, :, None]
    )
    kernel_raw = mod_grad * styles[None, None, :]
    styles_grad = jnp.sum(mod_grad * kernel, axis=(0, 1))
    hidden_grad = jnp.dot(style_weight, styles_grad[:, None], precision=lax.Precision.HIGHEST)[:, 0]
    lifted_grad = hidden_grad * silu_slope(lifted)
    style_raw = hidden[:, None] * styles_grad[None, :]
    lift_raw = cosmology[:, None] * lifted_grad[None, :]
    members = (kernel_raw, sums_offset, lift_raw, lifted_grad, style_raw, styles_grad)
    square_sum = sum((jnp.sum(member * member) for member in members))
    entries = sum((member.size for member in members))
    factor = jnp.minimum(1.0, lax.rsqrt(square_sum / entries + clip_eps))
    return tuple((factor * member for member in members))


def summed(sums):
    part = jnp.sum(lax.all_to_all(sums.reshape(16, 16, 128), ("gy", "gz"), 0, 0, tiled=True), axis=0)
    spread = jnp.broadcast_to(part[None], (32, 16, 128))
    part = jnp.sum(lax.all_to_all(spread, "gx", 0, 0, tiled=True), axis=0)
    spread = jnp.broadcast_to(part[None], (16, 16, 128))
    return lax.all_to_all(spread, ("gy", "gz"), 0, 0, tiled=True)


def body(
    field, cotangent, cosmology, lift_weight, lift_bias, style_weight, style_bias, kernel, offset
):
    perm, pick, place, mask = constants()
    low, high, mid = call(
        split_kernel, [shape(3, 8, C, 128), shape(3, 8, C, 128), shape(1, 8, C, 128)], 3
    )(field, cotangent, perm)
    ahead, back = shifts("gx")
    left = lax.ppermute(high, "gx", ahead)
    right = lax.ppermute(low, "gx", back)

    taps = jnp.transpose(kernel, (2, 3, 4, 0, 1)).reshape(TAPS, C, C)
    lifted, hidden, styles, modded, inv_norm, scaled = modulate(
        cosmology, lift_weight, lift_bias, style_weight, style_bias, taps
    )
    fwd = jnp.transpose(scaled, (1, 0, 2)).reshape(C, TAPS * C)
    bwd = jnp.transpose(scaled[::-1], (2, 0, 1)).reshape(C, TAPS * C)

    rows = (low, high, mid, left, right)
    up, down = call(pack_kernel, [shape(19, C, 128), shape(19, C, 128)], 5)(*rows)
    ahead, back = shifts("gy")
    up = lax.ppermute(up, "gy", ahead)
    down = lax.ppermute(down, "gy", back)

    field_rows, cot_rows, hi, lo = call(
        gather_kernel,
        [
            shape(7, 12, C, 128), shape(5, 10, C, 128),
            shape(8, FIELD_ROWS + COT_ROWS), shape(8, FIELD_ROWS + COT_ROWS),
        ],
        8,
    )(*rows, up, down, pick)
    ahead, back = shifts("gz")
    before = lax.ppermute(hi, "gz", ahead)
    after = lax.ppermute(lo, "gz", back)

    grad_rows, sums = pl.pallas_call(
        conv_kernel,
        out_shape=[shape(3, 8, C, 128), shape(256, 128, dtype=f32)],
        in_specs=[VMEM] * 9,
        out_specs=[VMEM] * 2,
        scratch_shapes=[
            pltpu.VMEM((FIELD_ROWS + COT_ROWS, 128), bf16),
            pltpu.VMEM((C, PLANE), bf16),
            pltpu.VMEM((7, 9 * C, OUT), bf16),
            pltpu.VMEM((C, OUT), bf16),
            pltpu.VMEM((C, OUT + 128), bf16),
            pltpu.VMEM((5, 9 * C, GRAD), bf16),
            pltpu.VMEM((C, 896), f32),
        ],
        cost_estimate=pl.CostEstimate(flops=700_000_000, bytes_accessed=4 << 20, transcendentals=0),
        compiler_params=pltpu.CompilerParams(vmem_limit_bytes=48 * 1024 * 1024),
    )(field_rows, cot_rows, before, after, place, mask, fwd, bwd, offset[:, None])
    grad_field = jnp.transpose(grad_rows, (2, 0, 1, 3))

    sums = summed(sums).reshape(4, 8, 8, 128).transpose(0, 2, 1, 3).reshape(C, 1024)
    sums_kernel = sums[:, : TAPS * C].reshape(C, TAPS, C).transpose(1, 0, 2)
    sums_offset = sums[:, TAPS * C]
    kernel_out, grad_offset, grad_lift, grad_liftbias, grad_style, grad_stylebias = param_backward(
        sums_kernel, sums_offset, cosmology, style_weight, taps, lifted, hidden, styles, modded, inv_norm
    )
    grad_kernel = jnp.transpose(kernel_out.reshape(3, 3, 3, C, C), (3, 4, 0, 1, 2))
    return (
        grad_field, grad_kernel, grad_offset, grad_lift, grad_liftbias, grad_style, grad_stylebias,
    )


def solution(mesh):
    placed = (P(None, "gx", "gy", "gz"),) * 2 + (P(),) * 7
    return jax.shard_map(
        body,
        mesh=mesh,
        in_specs=placed,
        out_specs=(P(None, "gx", "gy", "gz"),) + (P(),) * 6,
        check_vma=False,
    )
```

```python
import numpy as np
import jax
import jax.numpy as jnp
from jax import lax
from jax.experimental import pallas as pl
from jax.experimental.pallas import tpu as pltpu
from jax.sharding import Mesh, PartitionSpec as P

demod_eps = 1e-06
clip_eps = 1e-06

C = 32
TAPS = 27
PITCH = 132
PLANE = 14 * 128
OUT = 11 * 128
GRAD = 9 * 128
FIELD_ROWS = 7 * 12 * C
COT_ROWS = 5 * 10 * C
f32 = jnp.float32
bf16 = jnp.bfloat16
VMEM = pl.BlockSpec(memory_space=pltpu.VMEM)


def call(kernel, outs, n_in, flops=0, limit=40):
    return pl.pallas_call(
        kernel,
        out_shape=outs,
        in_specs=[VMEM] * n_in,
        out_specs=[VMEM] * len(outs),
        cost_estimate=pl.CostEstimate(flops=flops, bytes_accessed=1 << 20, transcendentals=0),
        compiler_params=pltpu.CompilerParams(vmem_limit_bytes=limit * 1024 * 1024),
    )


def shape(*dims, dtype=bf16):
    return jax.ShapeDtypeStruct(dims, dtype)


def select(dims, row_axis, lane_axis, lanes):
    row = lax.broadcasted_iota(jnp.int32, dims, row_axis)
    lane = lax.broadcasted_iota(jnp.int32, dims, lane_axis)
    hit = jnp.zeros(dims, f32)
    for n, at in enumerate(lanes):
        if at is not None:
            hit = jnp.where((row == n) & (lane == at), 1.0, hit)
    return hit.astype(bf16)


def split_kernel(field_hbm, cot_hbm, low_ref, high_ref, mid_ref, field_ref, cot_ref, sems):
    fetches = (
        pltpu.make_async_copy(field_hbm, field_ref, sems.at[0]),
        pltpu.make_async_copy(cot_hbm, cot_ref, sems.at[1]),
    )
    for fetch in fetches:
        fetch.start()
    to = lax.broadcasted_iota(jnp.int32, (256, 256), 0)
    of = lax.broadcasted_iota(jnp.int32, (256, 256), 1)
    perm = jnp.where((of & 7) * C + (of >> 3) == to, 1.0, 0.0).astype(bf16)

    def rows(ref, x):
        block = ref[:, x].astype(f32).reshape(C * 8, 128).astype(bf16)
        return jnp.dot(perm, block, preferred_element_type=f32).astype(bf16).reshape(8, C, 128)

    fetches[0].wait()
    f0, f1, f2 = (rows(field_ref, x) for x in range(3))
    low_ref[0], low_ref[1] = f0, f1
    high_ref[0], high_ref[1] = f1, f2
    fetches[1].wait()
    c0, c1, c2 = (rows(cot_ref, x) for x in range(3))
    low_ref[2], high_ref[2], mid_ref[0] = c0, c2, c1


def planes(low_ref, high_ref, mid_ref, left_ref, right_ref):
    field = (
        (left_ref, 0), (left_ref, 1), (low_ref, 0), (low_ref, 1), (high_ref, 1), (right_ref, 0), (right_ref, 1),
    )
    cot = ((left_ref, 2), (low_ref, 2), (mid_ref, 0), (high_ref, 2), (right_ref, 2))
    return field, cot


def pack_kernel(low_ref, high_ref, mid_ref, left_ref, right_ref, up_ref, down_ref):
    field, cot = planes(low_ref, high_ref, mid_ref, left_ref, right_ref)
    for n, (ref, at) in enumerate(field):
        up_ref[2 * n : 2 * n + 2] = ref[at, 6:8]
        down_ref[2 * n : 2 * n + 2] = ref[at, 0:2]
    for n, (ref, at) in enumerate(cot):
        up_ref[14 + n] = ref[at, 7]
        down_ref[14 + n] = ref[at, 0]


def gather_kernel(
    low_ref, high_ref, mid_ref, left_ref, right_ref, up_ref, down_ref, field_out, cot_out, faces_ref
):
    field, cot = planes(low_ref, high_ref, mid_ref, left_ref, right_ref)
    for n, (ref, at) in enumerate(field):
        field_out[n, 0:2] = up_ref[2 * n : 2 * n + 2]
        field_out[n, 2:10] = ref[at]
        field_out[n, 10:12] = down_ref[2 * n : 2 * n + 2]
    for n, (ref, at) in enumerate(cot):
        cot_out[n, 0] = up_ref[14 + n]
        cot_out[n, 1:9] = ref[at]
        cot_out[n, 9] = down_ref[14 + n]

    def faces(lanes, rows):
        pick = select((8, 128), 0, 1, lanes)
        return lax.dot_general(
            pick, rows, (((1,), (1,)), ((), ())), preferred_element_type=f32
        )

    both = faces((126, 127, 0, 1), field_out[...].reshape(FIELD_ROWS, 128))
    beside = faces((None, None, None, None, 127, 0), cot_out[...].reshape(COT_ROWS, 128))
    both = jnp.concatenate([both[:, :COT_ROWS] + beside, both[:, COT_ROWS:]], axis=1).astype(bf16)
    for n in range(4):
        faces_ref[n] = both


def silu_slope(values):
    logistic = jax.nn.sigmoid(values)
    return logistic * (1.0 + values * (1.0 - logistic))


def conv_kernel(
    field_ref, cot_ref, faces_ref, fwd_ref, bwd_ref, offset_ref,
    grad_ref, sums_ref,
    edge, plane, cols, up, ucols, total,
):
    me = lax.axis_index("gz")
    before, after = lax.rem(me + 3, 4), lax.rem(me + 1, 4)

    def placed(lanes_before, lanes_after, count):
        return sum(
            lax.dot_general(
                faces_ref[at, :, :count], select((8, 128), 0, 1, lanes),
                (((0,), (0,)), ((), ())), preferred_element_type=f32,
            )
            for at, lanes in ((before, lanes_before), (after, lanes_after))
        ).astype(bf16)

    none = (None,) * 4
    edge[:FIELD_ROWS] = placed((0, 1), (None, None, 2, 3), FIELD_ROWS)
    edge[FIELD_ROWS:] = placed(none + (0,), none + (None, 1), COT_ROWS)
    lane = lax.broadcasted_iota(jnp.int32, (1, OUT), 1)
    own_lanes = jnp.zeros((1, OUT), f32)
    for y in range(1, 9):
        own_lanes = jnp.where((lane > y * PITCH) & (lane <= y * PITCH + 128), 1.0, own_lanes)

    @pl.loop(0, 7)
    def _(x):
        pieces = []
        for y in range(12):
            sides = edge[pl.ds(pl.multiple_of((x * 12 + y) * C, C), C), :]
            pieces += [sides[:, 0:2], field_ref[x, y], sides[:, 2:4]]
        plane[...] = jnp.concatenate(
            pieces + [jnp.zeros((C, PLANE - 12 * PITCH), bf16)], axis=1
        )
        for t in range(9):
            at = (t // 3) * PITCH + t % 3
            cols[x, t * C : (t + 1) * C, :] = plane[:, at : at + OUT]

    total[...] = jnp.zeros_like(total)

    @pl.loop(0, 5)
    def _(x):
        pieces = []
        for y in range(10):
            sides = edge[pl.ds(pl.multiple_of(FIELD_ROWS + (x * 10 + y) * C, C), C), :]
            pieces += [sides[:, 0:1], cot_ref[x, y], sides[:, 1:2], jnp.zeros((C, 2), bf16)]
        pieces.append(jnp.zeros((C, OUT - 10 * PITCH), bf16))
        beside = jnp.concatenate(pieces, axis=1).astype(f32)
        block = cols[pl.ds(x, 3)].reshape(3 * 9 * C, OUT)
        preact = jnp.dot(fwd_ref[...], block, preferred_element_type=f32) + offset_ref[...]
        upstream = (beside * silu_slope(preact)).astype(bf16)
        up[:, :OUT] = upstream
        up[:, OUT:] = jnp.zeros((C, 128), bf16)
        for t in range(9):
            at = (t // 3) * PITCH + t % 3
            ucols[x, t * C : (t + 1) * C, :] = up[:, at : at + GRAD]

        @pl.when((x >= 1) & (x <= 3))
        def _():
            own = upstream.astype(f32) * own_lanes
            total[:, 864:] += jnp.sum(own, axis=1, keepdims=True)
            total[:, :864] += lax.dot_general(
                own.astype(bf16), block, (((1,), (1,)), ((), ())), preferred_element_type=f32
            )

    for s in range(4):
        for l in range(8):
            at = (s * 8 + l) * 8
            if l < 7:
                sums_ref[at : at + 8] = total[8 * s : 8 * s + 8, 128 * l : 128 * l + 128]
            else:
                sums_ref[at : at + 8] = jnp.zeros((8, 128), f32)

    @pl.loop(0, 3)
    def _(x):
        block = ucols[pl.ds(x, 3)].reshape(3 * 9 * C, GRAD)
        grad = jnp.dot(bwd_ref[...], block, preferred_element_type=f32).astype(bf16)
        for y in range(8):
            grad_ref[x, y] = grad[:, y * PITCH : y * PITCH + 128]


def tail_kernel(
    sums_ref, kernel_ref, modded_ref, styles_ref, inv_ref, lifted_ref, hidden_ref, weight_ref, cosmology_ref,
    kernel_out, offset_out, lift_out, bias_out, style_out, sbias_out,
):
    def total(values):
        return jnp.sum(jnp.sum(values, axis=1, keepdims=True), axis=0, keepdims=True)

    sums = jnp.concatenate(
        [
            jnp.concatenate([sums_ref[(s * 8 + l) * 8 : (s * 8 + l) * 8 + 8] for s in range(4)], axis=0)
            for l in range(7)
        ],
        axis=1,
    )
    kernel, modded, styles, inv = kernel_ref[...], modded_ref[...], styles_ref[...], inv_ref[...]
    eye = jnp.where(
        lax.broadcasted_iota(jnp.int32, (C, C), 0) == lax.broadcasted_iota(jnp.int32, (C, C), 1), 1.0, 0.0
    )
    offset = jnp.sum(sums[:, TAPS * C : TAPS * C + C] * eye, axis=0, keepdims=True)
    projected = jnp.sum(sums * modded, axis=1, keepdims=True)
    mod_grad = inv * (sums - modded * (inv * inv * projected))
    raw = mod_grad * styles
    lanes = jnp.sum(mod_grad * kernel, axis=0, keepdims=True)
    folded = sum(lanes[:, 128 * l : 128 * l + 128] for l in range(7))
    row = sum(folded[:, C * n : C * n + C] for n in range(4))
    column = jnp.sum(row * eye, axis=1, keepdims=True)
    lifted_grad = jnp.sum(weight_ref[...] * column, axis=0, keepdims=True) * silu_slope(lifted_ref[...])
    style_raw = column * hidden_ref[...]
    lift_raw = cosmology_ref[...] * lifted_grad
    squares = sum(total(v * v) for v in (raw, offset, lift_raw, lifted_grad, style_raw, row))
    entries = TAPS * C * C + C + lift_raw.size + lifted_grad.size + style_raw.size + C
    factor = jnp.minimum(1.0, lax.rsqrt(squares / entries + clip_eps))
    raw = raw * factor
    for t in range(TAPS):
        kernel_out[t] = raw[:, C * t : C * t + C]
    offset_out[...] = offset * factor
    lift_out[...] = lift_raw * factor
    bias_out[...] = lifted_grad * factor
    style_out[...] = style_raw * factor
    sbias_out[...] = row * factor


def shifts(axis):
    n = lax.axis_size(axis)
    ahead = [(i, (i + 1) % n) for i in range(n)]
    return ahead, [(j, i) for i, j in ahead]


def modulate(cosmology, lift_weight, lift_bias, style_weight, style_bias, kernel):
    lifted = (
        jnp.dot(cosmology[None, :], lift_weight, precision=lax.Precision.HIGHEST)[0] + lift_bias
    )
    hidden = jax.nn.silu(lifted)
    styles = (
        jnp.dot(hidden[None, :], style_weight, precision=lax.Precision.HIGHEST)[0]
        + style_bias
        + 1.0
    )
    modded = kernel * styles[None, None, :]
    inv_norm = lax.rsqrt(jnp.sum(modded * modded, axis=(0, 2)) + demod_eps)
    scaled = (modded * inv_norm[None, :, None]).astype(bf16)
    return (lifted, hidden, styles, modded, inv_norm, scaled)


def summed(sums):
    flat = ("ghi", "gy", "gz")
    part = jnp.sum(lax.all_to_all(sums.reshape(32, 8, 128), flat, 0, 0, tiled=True), axis=0)
    spread = jnp.broadcast_to(part[None], (16, 8, 128))
    part = jnp.sum(lax.all_to_all(spread, "glong", 0, 0, tiled=True), axis=0)
    spread = jnp.broadcast_to(part[None], (32, 8, 128))
    return lax.all_to_all(spread, flat, 0, 0, tiled=True).reshape(256, 128)


def body(
    field, cotangent, cosmology, lift_weight, lift_bias, style_weight, style_bias, kernel, offset
):
    low, high, mid = pl.pallas_call(
        split_kernel,
        out_shape=[shape(3, 8, C, 128), shape(3, 8, C, 128), shape(1, 8, C, 128)],
        in_specs=[pl.BlockSpec(memory_space=pltpu.HBM)] * 2,
        out_specs=[VMEM] * 3,
        scratch_shapes=[
            pltpu.VMEM((C, 3, 8, 128), bf16), pltpu.VMEM((C, 3, 8, 128), bf16), pltpu.SemaphoreType.DMA((2,)),
        ],
    )(field, cotangent)
    ahead, back = shifts(("glong", "ghi"))
    left = lax.ppermute(high, ("glong", "ghi"), ahead)
    right = lax.ppermute(low, ("glong", "ghi"), back)

    taps = jnp.transpose(kernel, (2, 3, 4, 0, 1)).reshape(TAPS, C, C)
    lifted, hidden, styles, modded, inv_norm, scaled = modulate(
        cosmology, lift_weight, lift_bias, style_weight, style_bias, taps
    )
    fwd = jnp.transpose(scaled, (1, 0, 2)).reshape(C, TAPS * C)
    bwd = jnp.transpose(scaled[::-1], (2, 0, 1)).reshape(C, TAPS * C)

    rows = (low, high, mid, left, right)
    up, down = call(pack_kernel, [shape(19, C, 128), shape(19, C, 128)], 5)(*rows)
    ahead, back = shifts("gy")
    up = lax.ppermute(up, "gy", ahead)
    down = lax.ppermute(down, "gy", back)

    field_rows, cot_rows, faces = call(
        gather_kernel, [shape(7, 12, C, 128), shape(5, 10, C, 128), shape(4, 8, FIELD_ROWS)], 7
    )(*rows, up, down)
    faces = lax.all_to_all(faces, "gz", 0, 0, tiled=True)

    grad_rows, sums = pl.pallas_call(
        conv_kernel,
        out_shape=[shape(3, 8, C, 128), shape(256, 128, dtype=f32)],
        in_specs=[VMEM] * 6,
        out_specs=[VMEM] * 2,
        scratch_shapes=[
            pltpu.VMEM((FIELD_ROWS + COT_ROWS, 128), bf16),
            pltpu.VMEM((C, PLANE), bf16),
            pltpu.VMEM((7, 9 * C, OUT), bf16),
            pltpu.VMEM((C, OUT + 128), bf16),
            pltpu.VMEM((5, 9 * C, GRAD), bf16),
            pltpu.VMEM((C, 896), f32),
        ],
        cost_estimate=pl.CostEstimate(flops=700_000_000, bytes_accessed=4 << 20, transcendentals=0),
        compiler_params=pltpu.CompilerParams(vmem_limit_bytes=48 * 1024 * 1024),
    )(field_rows, cot_rows, faces, fwd, bwd, offset[:, None])
    grad_field = jnp.transpose(grad_rows, (2, 0, 1, 3))

    packed = jnp.pad(jnp.transpose(taps, (1, 0, 2)).reshape(C, TAPS * C), ((0, 0), (0, C)))
    styles_row = jnp.pad(jnp.tile(styles, TAPS), (0, C))[None, :]
    kernel_out, grad_offset, grad_lift, grad_liftbias, grad_style, grad_stylebias = call(
        tail_kernel,
        [
            shape(TAPS, C, C, dtype=f32), shape(1, C, dtype=f32), shape(2, 256, dtype=f32),
            shape(1, 256, dtype=f32), shape(C, 256, dtype=f32), shape(1, C, dtype=f32),
        ],
        9,
    )(
        summed(sums), packed, packed * styles_row, styles_row, inv_norm[:, None], lifted[None, :],
        hidden[None, :], style_weight.T, cosmology[:, None],
    )
    grad_kernel = jnp.transpose(kernel_out.reshape(3, 3, 3, C, C), (3, 4, 0, 1, 2))
    return (
        grad_field, grad_kernel, grad_offset[0], grad_lift, grad_liftbias[0], grad_style.T, grad_stylebias[0],
    )


def solution(mesh):
    cut = Mesh(mesh.devices.reshape(16, 2, 4, 4), ("glong", "ghi", "gy", "gz"))
    grid = P(None, ("glong", "ghi"), "gy", "gz")
    return jax.shard_map(
        body, mesh=cut, in_specs=(grid,) * 2 + (P(),) * 7, out_specs=(grid,) + (P(),) * 6, check_vma=False
    )
```

```python
import numpy as np
import jax
import jax.numpy as jnp
from jax import lax
from jax.experimental import pallas as pl
from jax.experimental.pallas import tpu as pltpu
from jax.sharding import Mesh, PartitionSpec as P

demod_eps = 1e-06
clip_eps = 1e-06

C = 32
TAPS = 27
EDGE = 6
FIELD_LANES = 12 * 8 * C
COT_LANES = 10 * 8 * C
OUT = 10 * 128
OWN = 8 * 128
f32 = jnp.float32
bf16 = jnp.bfloat16
VMEM = pl.BlockSpec(memory_space=pltpu.VMEM)


def call(kernel, outs, n_in, flops=0, limit=24, scratch=()):
    return pl.pallas_call(
        kernel,
        out_shape=outs,
        in_specs=[VMEM] * n_in,
        out_specs=[VMEM] * len(outs),
        scratch_shapes=list(scratch),
        cost_estimate=pl.CostEstimate(flops=flops, bytes_accessed=1 << 20, transcendentals=0),
        compiler_params=pltpu.CompilerParams(vmem_limit_bytes=limit * 1024 * 1024),
    )


def shape(*dims, dtype=bf16):
    return jax.ShapeDtypeStruct(dims, dtype)


def select(dims, row_axis, lane_axis, lanes):
    row = lax.broadcasted_iota(jnp.int32, dims, row_axis)
    lane = lax.broadcasted_iota(jnp.int32, dims, lane_axis)
    hit = jnp.zeros(dims, f32)
    for n, at in enumerate(lanes):
        if at is not None:
            hit = jnp.where((row == n) & (lane == at), 1.0, hit)
    return hit.astype(bf16)


def split_kernel(field_hbm, cot_hbm, low_ref, high_ref, mid_ref, field_ref, cot_ref, sems):
    fetches = (
        pltpu.make_async_copy(field_hbm, field_ref, sems.at[0]),
        pltpu.make_async_copy(cot_hbm, cot_ref, sems.at[1]),
    )
    for fetch in fetches:
        fetch.start()
    to = lax.broadcasted_iota(jnp.int32, (256, 256), 0)
    of = lax.broadcasted_iota(jnp.int32, (256, 256), 1)
    perm = jnp.where((of & 7) * C + (of >> 3) == to, 1.0, 0.0).astype(bf16)

    def rows(ref, x):
        block = ref[:, x].astype(f32).reshape(C * 8, 128).astype(bf16)
        return jnp.dot(perm, block, preferred_element_type=f32).astype(bf16).reshape(8, C, 128)

    fetches[0].wait()
    f0, f1, f2 = (rows(field_ref, x) for x in range(3))
    low_ref[0], low_ref[1] = f0, f1
    high_ref[0], high_ref[1] = f1, f2
    fetches[1].wait()
    c0, c1, c2 = (rows(cot_ref, x) for x in range(3))
    low_ref[2], high_ref[2], mid_ref[0] = c0, c2, c1


def planes(low_ref, high_ref, mid_ref, left_ref, right_ref):
    field = (
        (left_ref, 0), (left_ref, 1), (low_ref, 0), (low_ref, 1), (high_ref, 1), (right_ref, 0), (right_ref, 1),
    )
    cot = ((left_ref, 2), (low_ref, 2), (mid_ref, 0), (high_ref, 2), (right_ref, 2))
    return field, cot


def pack_kernel(low_ref, high_ref, mid_ref, left_ref, right_ref, up_ref, down_ref):
    field, cot = planes(low_ref, high_ref, mid_ref, left_ref, right_ref)
    for n, (ref, at) in enumerate(field):
        up_ref[2 * n : 2 * n + 2] = ref[at, 6:8]
        down_ref[2 * n : 2 * n + 2] = ref[at, 0:2]
    for n, (ref, at) in enumerate(cot):
        up_ref[14 + n] = ref[at, 7]
        down_ref[14 + n] = ref[at, 0]


def gather_kernel(
    low_ref, high_ref, mid_ref, left_ref, right_ref, up_ref, down_ref, field_out, cot_out, faces_ref
):
    field, cot = planes(low_ref, high_ref, mid_ref, left_ref, right_ref)
    for n, (ref, at) in enumerate(field):
        for y in range(12):
            if y < 2:
                row = up_ref[2 * n + y]
            elif y < 10:
                row = ref[at, y - 2]
            else:
                row = down_ref[2 * n + y - 10]
            field_out[y, n] = row
    field_out[:, 7:] = jnp.zeros((12, 1, C, 128), bf16)
    for n, (ref, at) in enumerate(cot):
        for y in range(10):
            cot_out[y, n] = up_ref[14 + n] if y == 0 else down_ref[14 + n] if y == 9 else ref[at, y - 1]
    cot_out[:, 5:] = jnp.zeros((10, 3, C, 128), bf16)

    def faces(lanes, rows):
        pick = select((8, 128), 0, 1, lanes)
        return lax.dot_general(
            pick, rows, (((1,), (1,)), ((), ())), preferred_element_type=f32
        )

    both = faces((126, 127, 0, 1), field_out[...].reshape(FIELD_LANES, 128))
    beside = faces((None, None, None, None, 127, 0), cot_out[...].reshape(COT_LANES, 128))
    both = jnp.concatenate([both[:, :COT_LANES] + beside, both[:, COT_LANES:]], axis=1).astype(bf16)
    for n in range(4):
        faces_ref[n] = both


def silu_slope(values):
    logistic = jax.nn.sigmoid(values)
    return logistic * (1.0 + values * (1.0 - logistic))


def conv_kernel(
    field_ref, cot_ref, faces_ref, fwd_ref, offset_ref, sums_ref, up_ref, rim_ref, halo, shifted, edge, total
):
    me = lax.axis_index("gz")
    before, after = lax.rem(me + 3, 4), lax.rem(me + 1, 4)

    def across(rows, place):
        return lax.dot_general(rows, place, (((0,), (0,)), ((), ())), preferred_element_type=f32)

    halo[...] = (
        across(faces_ref[before], select((8, 128), 0, 1, (None, 0)))
        + across(faces_ref[after], select((8, 128), 0, 1, (None, None, 127)))
    ).astype(bf16)
    lane = lax.broadcasted_iota(jnp.int32, (C, 128), 1)

    @pl.loop(0, 7)
    def _(x):
        for y in range(12):
            row = field_ref[y, x]
            ends = halo[pl.ds(pl.multiple_of((y * 8 + x) * C, C), C), :]
            at = slice(y * 128, y * 128 + 128)
            shifted[0, x, :, at] = jnp.where(lane == 0, ends, pltpu.roll(row, 1, 1))
            shifted[1, x, :, at] = row
            shifted[2, x, :, at] = jnp.where(lane == 127, ends, pltpu.roll(row, 127, 1))

    def spread(at, count, moves):
        rows = jnp.concatenate(
            [faces_ref[at, :, y * 256 : y * 256 + 256].astype(f32) for y in range(count)], axis=0
        ).astype(bf16)
        row = lax.broadcasted_iota(jnp.int32, (count * 8, 128), 0)
        to = lax.broadcasted_iota(jnp.int32, (count * 8, 128), 1)
        place = jnp.zeros((count * 8, 128), f32)
        for k, n in moves:
            place = jnp.where(((row & 7) == k) & (to == (row >> 3) * EDGE + n), 1.0, place)
        return across(rows, place.astype(bf16))

    rim = spread(before, 12, ((0, 0), (1, 1))) + spread(me, 12, ((2, 2), (1, 3))) + spread(after, 12, ((2, 4), (3, 5)))
    for t in range(9):
        shift = (t // 3) * EDGE + t % 3
        edge[t] = (pltpu.roll(rim, 128 - shift, 1) if shift else rim).astype(bf16)
    rim_cot = spread(before, 10, ((4, 0),)) + spread(after, 10, ((5, 3),))
    block = jnp.concatenate(
        [
            jnp.concatenate([edge[t, (x + a) * C : (x + a) * C + C] for a in range(3) for t in range(9)], axis=0)
            for x in range(5)
        ],
        axis=1,
    )
    preact = jnp.dot(fwd_ref[...], block, preferred_element_type=f32) + offset_ref[...]
    slope = silu_slope(preact)
    for x in range(5):
        rim_ref[x] = (rim_cot[x * C : x * C + C] * slope[:, x * 128 : x * 128 + 128]).astype(bf16)

    total[...] = jnp.zeros_like(total)

    @pl.loop(0, 5)
    def _(x):
        beside = jnp.concatenate([cot_ref[y, x] for y in range(10)], axis=1).astype(f32)
        block = jnp.concatenate(
            [shifted[c, x + a, :, b * 128 : b * 128 + OUT] for a in range(3) for b in range(3) for c in range(3)],
            axis=0,
        )
        preact = jnp.dot(fwd_ref[...], block, preferred_element_type=f32) + offset_ref[...]
        upstream = (beside * silu_slope(preact)).astype(bf16)
        up_ref[x] = upstream

        @pl.when((x >= 1) & (x <= 3))
        def _():
            own = upstream[:, 128 : 128 + OWN]
            total[:, 864:] += jnp.sum(own.astype(f32), axis=1, keepdims=True)
            total[:, :864] += lax.dot_general(
                own, block[:, 128 : 128 + OWN], (((1,), (1,)), ((), ())), preferred_element_type=f32
            )

    for s in range(4):
        for l in range(8):
            at = (s * 8 + l) * 8
            if l < 7:
                sums_ref[at : at + 8] = total[8 * s : 8 * s + 8, 128 * l : 128 * l + 128]
            else:
                sums_ref[at : at + 8] = jnp.zeros((8, 128), f32)


def grad_kernel_body(up_ref, rim_ref, bwd_ref, grad_ref, shifted):
    lane = lax.broadcasted_iota(jnp.int32, (C, 128), 1)

    @pl.loop(0, 5)
    def _(x):
        rim = rim_ref[x].astype(f32)
        for y in range(10):
            at = slice(y * 128, y * 128 + 128)
            row = up_ref[x, :, at].astype(f32)
            low, high = rim[:, y * EDGE : y * EDGE + 1], rim[:, y * EDGE + 3 : y * EDGE + 4]
            shifted[0, x, :, at] = jnp.where(lane == 0, low, pltpu.roll(row, 1, 1)).astype(bf16)
            shifted[1, x, :, at] = up_ref[x, :, at]
            shifted[2, x, :, at] = jnp.where(lane == 127, high, pltpu.roll(row, 127, 1)).astype(bf16)

    @pl.loop(0, 3)
    def _(x):
        block = jnp.concatenate(
            [shifted[c, x + a, :, b * 128 : b * 128 + OWN] for a in range(3) for b in range(3) for c in range(3)],
            axis=0,
        )
        grad = jnp.dot(bwd_ref[...], block, preferred_element_type=f32).astype(bf16)
        for y in range(8):
            grad_ref[x, y] = grad[:, y * 128 : y * 128 + 128]


def tail_kernel(
    sums_ref, kernel_ref, modded_ref, styles_ref, inv_ref, lifted_ref, hidden_ref, weight_ref, cosmology_ref,
    kernel_out, offset_out, lift_out, bias_out, style_out, sbias_out,
):
    def total(values):
        return jnp.sum(jnp.sum(values, axis=1, keepdims=True), axis=0, keepdims=True)

    sums = jnp.concatenate(
        [
            jnp.concatenate([sums_ref[(s * 8 + l) * 8 : (s * 8 + l) * 8 + 8] for s in range(4)], axis=0)
            for l in range(7)
        ],
        axis=1,
    )
    kernel, modded, styles, inv = kernel_ref[...], modded_ref[...], styles_ref[...], inv_ref[...]
    eye = jnp.where(
        lax.broadcasted_iota(jnp.int32, (C, C), 0) == lax.broadcasted_iota(jnp.int32, (C, C), 1), 1.0, 0.0
    )
    offset = jnp.sum(sums[:, TAPS * C : TAPS * C + C] * eye, axis=0, keepdims=True)
    projected = jnp.sum(sums * modded, axis=1, keepdims=True)
    mod_grad = inv * (sums - modded * (inv * inv * projected))
    raw = mod_grad * styles
    lanes = jnp.sum(mod_grad * kernel, axis=0, keepdims=True)
    folded = sum(lanes[:, 128 * l : 128 * l + 128] for l in range(7))
    row = sum(folded[:, C * n : C * n + C] for n in range(4))
    column = jnp.sum(row * eye, axis=1, keepdims=True)
    lifted_grad = jnp.sum(weight_ref[...] * column, axis=0, keepdims=True) * silu_slope(lifted_ref[...])
    style_raw = column * hidden_ref[...]
    lift_raw = cosmology_ref[...] * lifted_grad
    squares = sum(total(v * v) for v in (raw, offset, lift_raw, lifted_grad, style_raw, row))
    entries = TAPS * C * C + C + lift_raw.size + lifted_grad.size + style_raw.size + C
    factor = jnp.minimum(1.0, lax.rsqrt(squares / entries + clip_eps))
    raw = raw * factor
    for t in range(TAPS):
        kernel_out[t] = raw[:, C * t : C * t + C]
    offset_out[...] = offset * factor
    lift_out[...] = lift_raw * factor
    bias_out[...] = lifted_grad * factor
    style_out[...] = style_raw * factor
    sbias_out[...] = row * factor


def shifts(axis):
    n = lax.axis_size(axis)
    ahead = [(i, (i + 1) % n) for i in range(n)]
    return ahead, [(j, i) for i, j in ahead]


def modulate(cosmology, lift_weight, lift_bias, style_weight, style_bias, kernel):
    lifted = (
        jnp.dot(cosmology[None, :], lift_weight, precision=lax.Precision.HIGHEST)[0] + lift_bias
    )
    hidden = jax.nn.silu(lifted)
    styles = (
        jnp.dot(hidden[None, :], style_weight, precision=lax.Precision.HIGHEST)[0]
        + style_bias
        + 1.0
    )
    modded = kernel * styles[None, None, :]
    inv_norm = lax.rsqrt(jnp.sum(modded * modded, axis=(0, 2)) + demod_eps)
    scaled = (modded * inv_norm[None, :, None]).astype(bf16)
    return (lifted, hidden, styles, modded, inv_norm, scaled)


def summed(sums):
    flat = ("ghi", "gy", "gz")
    part = jnp.sum(lax.all_to_all(sums.reshape(32, 8, 128), flat, 0, 0, tiled=True), axis=0)
    spread = jnp.broadcast_to(part[None], (16, 8, 128))
    part = jnp.sum(lax.all_to_all(spread, "glong", 0, 0, tiled=True), axis=0)
    spread = jnp.broadcast_to(part[None], (32, 8, 128))
    return lax.all_to_all(spread, flat, 0, 0, tiled=True).reshape(256, 128)


def body(
    field, cotangent, cosmology, lift_weight, lift_bias, style_weight, style_bias, kernel, offset
):
    low, high, mid = pl.pallas_call(
        split_kernel,
        out_shape=[shape(3, 8, C, 128), shape(3, 8, C, 128), shape(1, 8, C, 128)],
        in_specs=[pl.BlockSpec(memory_space=pltpu.HBM)] * 2,
        out_specs=[VMEM] * 3,
        scratch_shapes=[
            pltpu.VMEM((C, 3, 8, 128), bf16), pltpu.VMEM((C, 3, 8, 128), bf16), pltpu.SemaphoreType.DMA((2,)),
        ],
    )(field, cotangent)
    ahead, back = shifts(("glong", "ghi"))
    left = lax.ppermute(high, ("glong", "ghi"), ahead)
    right = lax.ppermute(low, ("glong", "ghi"), back)

    taps = jnp.transpose(kernel, (2, 3, 4, 0, 1)).reshape(TAPS, C, C)
    lifted, hidden, styles, modded, inv_norm, scaled = modulate(
        cosmology, lift_weight, lift_bias, style_weight, style_bias, taps
    )
    fwd = jnp.transpose(scaled, (1, 0, 2)).reshape(C, TAPS * C)
    bwd = jnp.transpose(scaled[::-1], (2, 0, 1)).reshape(C, TAPS * C)

    rows = (low, high, mid, left, right)
    up, down = call(pack_kernel, [shape(19, C, 128), shape(19, C, 128)], 5)(*rows)
    ahead, back = shifts("gy")
    up = lax.ppermute(up, "gy", ahead)
    down = lax.ppermute(down, "gy", back)

    field_rows, cot_rows, faces = call(
        gather_kernel, [shape(12, 8, C, 128), shape(10, 8, C, 128), shape(4, 8, FIELD_LANES)], 7
    )(*rows, up, down)
    faces = lax.all_to_all(faces, "gz", 0, 0, tiled=True)

    sums, upstream, rim = call(
        conv_kernel,
        [shape(256, 128, dtype=f32), shape(5, C, OUT), shape(5, C, 128)],
        5,
        flops=540_000_000,
        scratch=[
            pltpu.VMEM((FIELD_LANES, 128), bf16),
            pltpu.VMEM((3, 7, C, 12 * 128), bf16),
            pltpu.VMEM((9, 8 * C, 128), bf16),
            pltpu.VMEM((C, 896), f32),
        ],
    )(field_rows, cot_rows, faces, fwd, offset[:, None])
    (grad_rows,) = call(
        grad_kernel_body,
        [shape(3, 8, C, 128)],
        3,
        flops=170_000_000,
        scratch=[pltpu.VMEM((3, 5, C, OUT), bf16)],
    )(upstream, rim, bwd)
    grad_field = jnp.transpose(grad_rows, (2, 0, 1, 3))

    packed = jnp.pad(jnp.transpose(taps, (1, 0, 2)).reshape(C, TAPS * C), ((0, 0), (0, C)))
    styles_row = jnp.pad(jnp.tile(styles, TAPS), (0, C))[None, :]
    kernel_out, grad_offset, grad_lift, grad_liftbias, grad_style, grad_stylebias = call(
        tail_kernel,
        [
            shape(TAPS, C, C, dtype=f32), shape(1, C, dtype=f32), shape(2, 256, dtype=f32),
            shape(1, 256, dtype=f32), shape(C, 256, dtype=f32), shape(1, C, dtype=f32),
        ],
        9,
    )(
        summed(sums), packed, packed * styles_row, styles_row, inv_norm[:, None], lifted[None, :],
        hidden[None, :], style_weight.T, cosmology[:, None],
    )
    grad_kernel = jnp.transpose(kernel_out.reshape(3, 3, 3, C, C), (3, 4, 0, 1, 2))
    return (
        grad_field, grad_kernel, grad_offset[0], grad_lift, grad_liftbias[0], grad_style.T, grad_stylebias[0],
    )


def solution(mesh):
    cut = Mesh(mesh.devices.reshape(16, 2, 4, 4), ("glong", "ghi", "gy", "gz"))
    grid = P(None, ("glong", "ghi"), "gy", "gz")
    return jax.shard_map(
        body, mesh=cut, in_specs=(grid,) * 2 + (P(),) * 7, out_specs=(grid,) + (P(),) * 6, check_vma=False
    )
```

```python
import numpy as np
import jax
import jax.numpy as jnp
from jax import lax
from jax.experimental import pallas as pl
from jax.experimental.pallas import tpu as pltpu
from jax.sharding import Mesh, PartitionSpec as P

demod_eps = 1e-06
clip_eps = 1e-06

C = 32
TAPS = 27
EDGE = 6
FIELD_LANES = 12 * 8 * C
COT_LANES = 10 * 8 * C
OUT = 10 * 128
OWN = 8 * 128
f32 = jnp.float32
bf16 = jnp.bfloat16
VMEM = pl.BlockSpec(memory_space=pltpu.VMEM)


def call(kernel, outs, n_in, flops=0, limit=24, scratch=()):
    return pl.pallas_call(
        kernel,
        out_shape=outs,
        in_specs=[VMEM] * n_in,
        out_specs=[VMEM] * len(outs),
        scratch_shapes=list(scratch),
        cost_estimate=pl.CostEstimate(flops=flops, bytes_accessed=1 << 20, transcendentals=0),
        compiler_params=pltpu.CompilerParams(vmem_limit_bytes=limit * 1024 * 1024),
    )


def shape(*dims, dtype=bf16):
    return jax.ShapeDtypeStruct(dims, dtype)


def select(dims, row_axis, lane_axis, lanes):
    row = lax.broadcasted_iota(jnp.int32, dims, row_axis)
    lane = lax.broadcasted_iota(jnp.int32, dims, lane_axis)
    hit = jnp.zeros(dims, f32)
    for n, at in enumerate(lanes):
        if at is not None:
            hit = jnp.where((row == n) & (lane == at), 1.0, hit)
    return hit.astype(bf16)


def split_kernel(field_hbm, cot_hbm, low_ref, high_ref, mid_ref, field_ref, cot_ref, sems):
    fetches = (
        pltpu.make_async_copy(field_hbm, field_ref, sems.at[0]),
        pltpu.make_async_copy(cot_hbm, cot_ref, sems.at[1]),
    )
    for fetch in fetches:
        fetch.start()
    to = lax.broadcasted_iota(jnp.int32, (256, 256), 0)
    of = lax.broadcasted_iota(jnp.int32, (256, 256), 1)
    perm = jnp.where((of & 7) * C + (of >> 3) == to, 1.0, 0.0).astype(bf16)

    def rows(ref, x):
        block = ref[:, x].astype(f32).reshape(C * 8, 128).astype(bf16)
        return jnp.dot(perm, block, preferred_element_type=f32).astype(bf16).reshape(8, C, 128)

    fetches[0].wait()
    f0, f1, f2 = (rows(field_ref, x) for x in range(3))
    low_ref[0], low_ref[1] = f0, f1
    high_ref[0], high_ref[1] = f1, f2
    fetches[1].wait()
    c0, c1, c2 = (rows(cot_ref, x) for x in range(3))
    low_ref[2], high_ref[2], mid_ref[0] = c0, c2, c1


def planes(low_ref, high_ref, mid_ref, left_ref, right_ref):
    field = (
        (left_ref, 0), (left_ref, 1), (low_ref, 0), (low_ref, 1), (high_ref, 1), (right_ref, 0), (right_ref, 1),
    )
    cot = ((left_ref, 2), (low_ref, 2), (mid_ref, 0), (high_ref, 2), (right_ref, 2))
    return field, cot


def pack_kernel(low_ref, high_ref, mid_ref, left_ref, right_ref, _, up_ref, down_ref):
    field, cot = planes(low_ref, high_ref, mid_ref, left_ref, right_ref)
    for n, (ref, at) in enumerate(field):
        up_ref[2 * n : 2 * n + 2] = ref[at, 6:8]
        down_ref[2 * n : 2 * n + 2] = ref[at, 0:2]
    for n, (ref, at) in enumerate(cot):
        up_ref[14 + n] = ref[at, 7]
        down_ref[14 + n] = ref[at, 0]


def gather_kernel(
    low_ref, high_ref, mid_ref, left_ref, right_ref, up_ref, down_ref, field_out, cot_out, faces_ref
):
    field, cot = planes(low_ref, high_ref, mid_ref, left_ref, right_ref)
    for n, (ref, at) in enumerate(field):
        for y in range(12):
            if y < 2:
                row = up_ref[2 * n + y]
            elif y < 10:
                row = ref[at, y - 2]
            else:
                row = down_ref[2 * n + y - 10]
            field_out[y, n] = row
    field_out[:, 7:] = jnp.zeros((12, 1, C, 128), bf16)
    for n, (ref, at) in enumerate(cot):
        for y in range(10):
            cot_out[y, n] = up_ref[14 + n] if y == 0 else down_ref[14 + n] if y == 9 else ref[at, y - 1]
    cot_out[:, 5:] = jnp.zeros((10, 3, C, 128), bf16)

    def faces(lanes, rows):
        pick = select((8, 128), 0, 1, lanes)
        return lax.dot_general(
            pick, rows, (((1,), (1,)), ((), ())), preferred_element_type=f32
        )

    both = faces((126, 127, 0, 1), field_out[...].reshape(FIELD_LANES, 128))
    beside = faces((None, None, None, None, 127, 0), cot_out[...].reshape(COT_LANES, 128))
    both = jnp.concatenate([both[:, :COT_LANES] + beside, both[:, COT_LANES:]], axis=1).astype(bf16)
    for n in range(4):
        faces_ref[n] = both


def silu_slope(values):
    logistic = jax.nn.sigmoid(values)
    return logistic * (1.0 + values * (1.0 - logistic))


def row_taps(ref, x, width):
    return jnp.concatenate(
        [ref[c, x, :, b * 128 : b * 128 + width] for b in range(3) for c in range(3)], axis=0
    )


def conv_kernel(
    field_ref, cot_ref, faces_ref, fwd_ref, offset_ref,
    sums_ref, up_ref, rim_ref,
    halo, shifted, edge, acc, own, total,
):
    me = lax.axis_index("gz")
    before, after = lax.rem(me + 3, 4), lax.rem(me + 1, 4)

    def across(rows, place):
        return lax.dot_general(rows, place, (((0,), (0,)), ((), ())), preferred_element_type=f32)

    sides = [faces_ref[at].astype(f32) for at in (before, me, after)]
    halo[...] = across(
        jnp.concatenate([sides[0], sides[2]], axis=0).astype(bf16),
        select((16, 128), 0, 1, (None, 0) + (None,) * 8 + (127,)),
    ).astype(bf16)
    lane = lax.broadcasted_iota(jnp.int32, (C, 128), 1)
    acc[...] = jnp.zeros_like(acc)

    @pl.loop(0, 7)
    def _(x):
        for y in range(12):
            row = field_ref[y, x]
            ends = halo[pl.ds(pl.multiple_of((y * 8 + x) * C, C), C), :]
            at = slice(y * 128, y * 128 + 128)
            shifted[0, x, :, at] = jnp.where(lane == 0, ends, pltpu.roll(row, 1, 1))
            shifted[1, x, :, at] = row
            shifted[2, x, :, at] = jnp.where(lane == 127, ends, pltpu.roll(row, 127, 1))
        part = jnp.dot(fwd_ref[...], row_taps(shifted, x, OUT), preferred_element_type=f32)
        for a in range(3):
            acc[x + 2 - a] += part[a * C : a * C + C]

    def spread(count, moves):
        rows = jnp.concatenate(
            [side[:, y * 256 : y * 256 + 256] for side in sides for y in range(count)], axis=0
        ).astype(bf16)
        row = lax.broadcasted_iota(jnp.int32, (count * 24, 128), 0)
        to = lax.broadcasted_iota(jnp.int32, (count * 24, 128), 1)
        place = jnp.zeros((count * 24, 128), f32)
        for n, (side, k, m) in enumerate(moves):
            y = (row >> 3) - side * count
            hit = ((row & 7) == k) & (to == y * EDGE + m) & (y >= 0) & (y < count)
            place = jnp.where(hit, 1.0, place)
        return across(rows, place.astype(bf16))

    rim = spread(12, ((0, 0, 0), (0, 1, 1), (1, 2, 2), (1, 1, 3), (2, 2, 4), (2, 3, 5)))
    for t in range(9):
        shift = (t // 3) * EDGE + t % 3
        edge[t] = (pltpu.roll(rim, 128 - shift, 1) if shift else rim).astype(bf16)
    rim_cot = spread(10, ((0, 4, 0), (2, 5, 3)))
    block = jnp.concatenate(
        [jnp.concatenate([edge[t, x * C : x * C + C] for t in range(9)], axis=0) for x in range(7)], axis=1
    )
    part = jnp.dot(fwd_ref[...], block, preferred_element_type=f32)
    offset = offset_ref[...]
    for x in range(5):
        preact = offset + sum(
            part[a * C : a * C + C, (x + a) * 128 : (x + a) * 128 + 128] for a in range(3)
        )
        rim_ref[x] = (rim_cot[x * C : x * C + C] * silu_slope(preact)).astype(bf16)

    own[...] = jnp.zeros_like(own)
    total[...] = jnp.zeros_like(total)

    @pl.loop(0, 5)
    def _(x):
        beside = jnp.concatenate([cot_ref[y, x] for y in range(10)], axis=1).astype(f32)
        upstream = (beside * silu_slope(acc[x + 2] + offset)).astype(bf16)
        up_ref[x] = upstream

        @pl.when((x >= 1) & (x <= 3))
        def _():
            own[x + 1] = upstream[:, 128 : 128 + OWN]

    @pl.loop(1, 6)
    def _(x):
        left = jnp.concatenate([own[x + 1 - a] for a in range(3)], axis=0)
        right = jnp.concatenate(
            [shifted[c, x, :, b * 128 + 128 : b * 128 + 128 + OWN] for b in range(3) for c in range(3)], axis=0
        )
        total[...] += lax.dot_general(left, right, (((1,), (1,)), ((), ())), preferred_element_type=f32)

    offsets = sum(jnp.sum(own[x].astype(f32), axis=1, keepdims=True) for x in range(2, 5))
    packed = jnp.concatenate(
        [total[a * C : a * C + C] for a in range(3)] + [jnp.broadcast_to(offsets, (C, C))], axis=1
    )
    for s in range(4):
        for l in range(8):
            at = (s * 8 + l) * 8
            if l < 7:
                sums_ref[at : at + 8] = packed[8 * s : 8 * s + 8, 128 * l : 128 * l + 128]
            else:
                sums_ref[at : at + 8] = jnp.zeros((8, 128), f32)


def grad_kernel_body(up_ref, rim_ref, bwd_ref, grad_ref, shifted, acc):
    lane = lax.broadcasted_iota(jnp.int32, (C, 128), 1)
    acc[...] = jnp.zeros_like(acc)

    @pl.loop(0, 5)
    def _(x):
        rim = rim_ref[x].astype(f32)
        for y in range(10):
            at = slice(y * 128, y * 128 + 128)
            row = up_ref[x, :, at]
            low = jnp.broadcast_to(rim[:, y * EDGE : y * EDGE + 1], (C, 128)).astype(bf16)
            high = jnp.broadcast_to(rim[:, y * EDGE + 3 : y * EDGE + 4], (C, 128)).astype(bf16)
            shifted[0, 0, :, at] = jnp.where(lane == 0, low, pltpu.roll(row, 1, 1))
            shifted[1, 0, :, at] = row
            shifted[2, 0, :, at] = jnp.where(lane == 127, high, pltpu.roll(row, 127, 1))
        part = jnp.dot(bwd_ref[...], row_taps(shifted, 0, OWN), preferred_element_type=f32)
        for a in range(3):
            acc[x + 2 - a] += part[a * C : a * C + C]

    to = lax.broadcasted_iota(jnp.int32, (256, 256), 0)
    of = lax.broadcasted_iota(jnp.int32, (256, 256), 1)
    perm = jnp.where((to & 7) * C + (to >> 3) == of, 1.0, 0.0).astype(bf16)
    for x in range(3):
        rows = jnp.concatenate(
            [acc[x + 2, :, y * 128 : y * 128 + 128] for y in range(8)], axis=0
        ).astype(bf16)
        moved = jnp.dot(perm, rows, preferred_element_type=f32)
        grad_ref[:, x] = moved.reshape(C, 8, 128).astype(bf16)


def identity():
    return jnp.where(
        lax.broadcasted_iota(jnp.int32, (C, C), 0) == lax.broadcasted_iota(jnp.int32, (C, C), 1), 1.0, 0.0
    )


def modulate_kernel(
    cosmology_ref, lift_ref, bias_ref, weight_ref, sbias_ref, taps_ref, offset_ref,
    fwd_ref, bwd_ref, kernel_ref, modded_ref, styles_ref, inv_ref, lifted_ref, hidden_ref, params_ref, column_ref,
):
    first, second = cosmology_ref[:, 0:1], cosmology_ref[:, 1:2]
    lifted = first * lift_ref[0:1] + second * lift_ref[1:2] + bias_ref[...]
    hidden = lifted * jax.nn.sigmoid(lifted)
    eye = identity()
    column = jnp.sum(weight_ref[...] * hidden, axis=1, keepdims=True)
    styles = jnp.sum(column * eye, axis=0, keepdims=True) + sbias_ref[...] + 1.0
    kernel = jnp.concatenate([taps_ref[t] for t in range(TAPS)] + [jnp.zeros((C, C), f32)], axis=1)
    styles = jnp.concatenate([styles] * TAPS + [jnp.zeros((1, C), f32)], axis=1)
    modded = kernel * styles
    inv = lax.rsqrt(jnp.sum(modded * modded, axis=1, keepdims=True) + demod_eps)
    scaled = (modded * inv).astype(bf16)
    for a in range(3):
        fwd_ref[a * C : a * C + C] = scaled[:, a * 288 : a * 288 + 288]
    turned = scaled.astype(f32).T
    for a in range(3):
        bwd_ref[a * C : a * C + C] = jnp.concatenate(
            [turned[(26 - a * 9 - t) * C : (27 - a * 9 - t) * C] for t in range(9)], axis=1
        ).astype(bf16)
    kernel_ref[...] = kernel
    modded_ref[...] = modded
    styles_ref[...] = styles
    inv_ref[...] = inv
    lifted_ref[...] = lifted
    hidden_ref[...] = hidden
    params_ref[...] = jnp.concatenate([first, second], axis=0)
    column_ref[...] = jnp.sum(offset_ref[...] * eye, axis=1, keepdims=True)


def total_kernel(parts_ref, spread_ref):
    part = jnp.sum(parts_ref[...], axis=0)
    for n in range(spread_ref.shape[0]):
        spread_ref[n] = part


def tail_kernel(
    sums_ref, kernel_ref, modded_ref, styles_ref, inv_ref, lifted_ref, hidden_ref, weight_ref, cosmology_ref,
    kernel_out, offset_out, lift_out, bias_out, style_out, sbias_out,
):
    def total(values):
        return jnp.sum(jnp.sum(values, axis=1, keepdims=True), axis=0, keepdims=True)

    sums = jnp.concatenate(
        [
            jnp.concatenate([sums_ref[(s * 8 + l) * 8 : (s * 8 + l) * 8 + 8] for s in range(4)], axis=0)
            for l in range(7)
        ],
        axis=1,
    )
    kernel, modded, styles, inv = kernel_ref[...], modded_ref[...], styles_ref[...], inv_ref[...]
    eye = identity()
    offset = jnp.sum(sums[:, TAPS * C : TAPS * C + C] * eye, axis=0, keepdims=True)
    projected = jnp.sum(sums * modded, axis=1, keepdims=True)
    mod_grad = inv * (sums - modded * (inv * inv * projected))
    raw = mod_grad * styles
    lanes = jnp.sum(mod_grad * kernel, axis=0, keepdims=True)
    folded = sum(lanes[:, 128 * l : 128 * l + 128] for l in range(7))
    row = sum(folded[:, C * n : C * n + C] for n in range(4))
    column = jnp.sum(row * eye, axis=1, keepdims=True)
    lifted_grad = jnp.sum(weight_ref[...] * column, axis=0, keepdims=True) * silu_slope(lifted_ref[...])
    style_raw = column * hidden_ref[...]
    lift_raw = cosmology_ref[...] * lifted_grad
    squares = sum(total(v * v) for v in (raw, offset, lift_raw, lifted_grad, style_raw, row))
    entries = TAPS * C * C + C + lift_raw.size + lifted_grad.size + style_raw.size + C
    factor = jnp.minimum(1.0, lax.rsqrt(squares / entries + clip_eps))
    raw = raw * factor
    for t in range(TAPS):
        kernel_out[t] = raw[:, C * t : C * t + C]
    offset_out[...] = offset * factor
    lift_out[...] = lift_raw * factor
    bias_out[...] = lifted_grad * factor
    style_out[...] = style_raw * factor
    sbias_out[...] = row * factor


def shifts(axis):
    n = lax.axis_size(axis)
    ahead = [(i, (i + 1) % n) for i in range(n)]
    return ahead, [(j, i) for i, j in ahead]


def summed(sums):
    flat = ("ghi", "gy", "gz")
    parts = lax.all_to_all(sums.reshape(32, 8, 128), flat, 0, 0, tiled=True)
    (spread,) = call(total_kernel, [shape(16, 8, 128, dtype=f32)], 1, limit=4)(parts)
    parts = lax.all_to_all(spread, "glong", 0, 0, tiled=True)
    (spread,) = call(total_kernel, [shape(32, 8, 128, dtype=f32)], 1, limit=4)(parts)
    return lax.all_to_all(spread, flat, 0, 0, tiled=True).reshape(256, 128)


def body(
    field, cotangent, cosmology, lift_weight, lift_bias, style_weight, style_bias, kernel, offset
):
    low, high, mid = pl.pallas_call(
        split_kernel,
        out_shape=[shape(3, 8, C, 128), shape(3, 8, C, 128), shape(1, 8, C, 128)],
        in_specs=[pl.BlockSpec(memory_space=pltpu.HBM)] * 2,
        out_specs=[VMEM] * 3,
        scratch_shapes=[
            pltpu.VMEM((C, 3, 8, 128), bf16), pltpu.VMEM((C, 3, 8, 128), bf16), pltpu.SemaphoreType.DMA((2,)),
        ],
        compiler_params=pltpu.CompilerParams(vmem_limit_bytes=4 * 1024 * 1024),
    )(*(pltpu.with_memory_space_constraint(block, pltpu.HBM) for block in (field, cotangent)))
    ahead, back = shifts(("glong", "ghi"))
    left = lax.ppermute(high, ("glong", "ghi"), ahead)
    right = lax.ppermute(low, ("glong", "ghi"), back)

    taps = jnp.transpose(kernel, (2, 3, 4, 0, 1)).reshape(TAPS, C, C)
    fwd, bwd, packed, modded, styles, inv_norm, lifted, hidden, params, column = call(
        modulate_kernel,
        [
            shape(3 * C, 9 * C), shape(3 * C, 9 * C), shape(C, 896, dtype=f32), shape(C, 896, dtype=f32),
            shape(1, 896, dtype=f32), shape(C, 1, dtype=f32), shape(1, 256, dtype=f32), shape(1, 256, dtype=f32),
            shape(2, 1, dtype=f32), shape(C, 1, dtype=f32),
        ],
        7,
        limit=8,
    )(
        cosmology[None, :], lift_weight, lift_bias[None, :], style_weight.T, style_bias[None, :], taps,
        offset[None, :],
    )

    rows = (low, high, mid, left, right)
    up, down = call(pack_kernel, [shape(19, C, 128), shape(19, C, 128)], 6, limit=8)(*rows, column)
    ahead, back = shifts("gy")
    up = lax.ppermute(up, "gy", ahead)
    down = lax.ppermute(down, "gy", back)

    field_rows, cot_rows, faces = call(
        gather_kernel, [shape(12, 8, C, 128), shape(10, 8, C, 128), shape(4, 8, FIELD_LANES)], 7
    )(*rows, up, down)
    faces = lax.all_to_all(faces, "gz", 0, 0, tiled=True)

    sums, upstream, rim = call(
        conv_kernel,
        [shape(256, 128, dtype=f32), shape(5, C, OUT), shape(5, C, 128)],
        5,
        flops=540_000_000,
        scratch=[
            pltpu.VMEM((FIELD_LANES, 128), bf16),
            pltpu.VMEM((3, 7, C, 12 * 128), bf16),
            pltpu.VMEM((9, 8 * C, 128), bf16),
            pltpu.VMEM((9, C, OUT), f32),
            pltpu.VMEM((7, C, OWN), bf16),
            pltpu.VMEM((3 * C, 9 * C), f32),
        ],
    )(field_rows, cot_rows, faces, fwd, column)
    (grad_field,) = call(
        grad_kernel_body,
        [shape(C, 3, 8, 128)],
        3,
        flops=170_000_000,
        scratch=[pltpu.VMEM((3, 1, C, OUT), bf16), pltpu.VMEM((7, C, OWN), f32)],
    )(upstream, rim, bwd)

    kernel_out, grad_offset, grad_lift, grad_liftbias, grad_style, grad_stylebias = call(
        tail_kernel,
        [
            shape(TAPS, C, C, dtype=f32), shape(1, C, dtype=f32), shape(2, 256, dtype=f32),
            shape(1, 256, dtype=f32), shape(C, 256, dtype=f32), shape(1, C, dtype=f32),
        ],
        9,
        limit=8,
    )(
        summed(sums), packed, modded, styles, inv_norm, lifted, hidden, style_weight.T, params,
    )
    grad_kernel = jnp.transpose(kernel_out.reshape(3, 3, 3, C, C), (3, 4, 0, 1, 2))
    return (
        grad_field, grad_kernel, grad_offset[0], grad_lift, grad_liftbias[0], grad_style.T, grad_stylebias[0],
    )


def solution(mesh):
    cut = Mesh(mesh.devices.reshape(16, 2, 4, 4), ("glong", "ghi", "gy", "gz"))
    grid = P(None, ("glong", "ghi"), "gy", "gz")
    return jax.shard_map(
        body, mesh=cut, in_specs=(grid,) * 2 + (P(),) * 7, out_specs=(grid,) + (P(),) * 6, check_vma=False
    )
```

```python
import numpy as np
import jax
import jax.numpy as jnp
from jax import lax
from jax.experimental import pallas as pl
from jax.experimental.pallas import tpu as pltpu
from jax.sharding import Mesh, PartitionSpec as P

demod_eps = 1e-06
clip_eps = 1e-06

C = 32
TAPS = 27
EDGE = 6
FIELD_LANES = 12 * 8 * C
COT_LANES = 10 * 8 * C
OUT = 10 * 128
OWN = 8 * 128
f32 = jnp.float32
bf16 = jnp.bfloat16
VMEM = pl.BlockSpec(memory_space=pltpu.VMEM)


def call(kernel, outs, n_in, flops=0, limit=24, scratch=()):
    return pl.pallas_call(
        kernel,
        out_shape=outs,
        in_specs=[VMEM] * n_in,
        out_specs=[VMEM] * len(outs),
        scratch_shapes=list(scratch),
        cost_estimate=pl.CostEstimate(flops=flops, bytes_accessed=1 << 20, transcendentals=0),
        compiler_params=pltpu.CompilerParams(vmem_limit_bytes=limit * 1024 * 1024),
    )


def shape(*dims, dtype=bf16):
    return jax.ShapeDtypeStruct(dims, dtype)


def select(dims, row_axis, lane_axis, lanes):
    row = lax.broadcasted_iota(jnp.int32, dims, row_axis)
    lane = lax.broadcasted_iota(jnp.int32, dims, lane_axis)
    hit = jnp.zeros(dims, f32)
    for n, at in enumerate(lanes):
        if at is not None:
            hit = jnp.where((row == n) & (lane == at), 1.0, hit)
    return hit.astype(bf16)


def split_kernel(field_hbm, cot_hbm, low_ref, high_ref, mid_ref, field_ref, cot_ref, sems):
    fetches = (
        pltpu.make_async_copy(field_hbm, field_ref, sems.at[0]),
        pltpu.make_async_copy(cot_hbm, cot_ref, sems.at[1]),
    )
    for fetch in fetches:
        fetch.start()
    to = lax.broadcasted_iota(jnp.int32, (256, 256), 0)
    of = lax.broadcasted_iota(jnp.int32, (256, 256), 1)
    perm = jnp.where((of & 7) * C + (of >> 3) == to, 1.0, 0.0).astype(bf16)

    def rows(ref, x):
        block = ref[:, x].astype(f32).reshape(C * 8, 128).astype(bf16)
        return jnp.dot(perm, block, preferred_element_type=f32).astype(bf16).reshape(8, C, 128)

    fetches[0].wait()
    f0, f1, f2 = (rows(field_ref, x) for x in range(3))
    low_ref[0], low_ref[1] = f0, f1
    high_ref[0], high_ref[1] = f1, f2
    fetches[1].wait()
    c0, c1, c2 = (rows(cot_ref, x) for x in range(3))
    low_ref[2], high_ref[2], mid_ref[0] = c0, c2, c1


def planes(low_ref, high_ref, mid_ref, left_ref, right_ref):
    field = (
        (left_ref, 0), (left_ref, 1), (low_ref, 0), (low_ref, 1), (high_ref, 1), (right_ref, 0), (right_ref, 1),
    )
    cot = ((left_ref, 2), (low_ref, 2), (mid_ref, 0), (high_ref, 2), (right_ref, 2))
    return field, cot


def pack_kernel(low_ref, high_ref, mid_ref, left_ref, right_ref, _, up_ref, down_ref):
    field, cot = planes(low_ref, high_ref, mid_ref, left_ref, right_ref)
    for n, (ref, at) in enumerate(field):
        up_ref[2 * n : 2 * n + 2] = ref[at, 6:8]
        down_ref[2 * n : 2 * n + 2] = ref[at, 0:2]
    for n, (ref, at) in enumerate(cot):
        up_ref[14 + n] = ref[at, 7]
        down_ref[14 + n] = ref[at, 0]


def gather_kernel(
    low_ref, high_ref, mid_ref, left_ref, right_ref, up_ref, down_ref, field_out, cot_out, faces_ref
):
    field, cot = planes(low_ref, high_ref, mid_ref, left_ref, right_ref)
    for n, (ref, at) in enumerate(field):
        for y in range(12):
            if y < 2:
                row = up_ref[2 * n + y]
            elif y < 10:
                row = ref[at, y - 2]
            else:
                row = down_ref[2 * n + y - 10]
            field_out[y, n] = row
    field_out[:, 7:] = jnp.zeros((12, 1, C, 128), bf16)
    for n, (ref, at) in enumerate(cot):
        for y in range(10):
            cot_out[y, n] = up_ref[14 + n] if y == 0 else down_ref[14 + n] if y == 9 else ref[at, y - 1]
    cot_out[:, 5:] = jnp.zeros((10, 3, C, 128), bf16)

    def faces(lanes, rows):
        pick = select((8, 128), 0, 1, lanes)
        return lax.dot_general(
            pick, rows, (((1,), (1,)), ((), ())), preferred_element_type=f32
        )

    both = faces((126, 127, 0, 1), field_out[...].reshape(FIELD_LANES, 128))
    beside = faces((None, None, None, None, 127, 0), cot_out[...].reshape(COT_LANES, 128))
    both = jnp.concatenate([both[:, :COT_LANES] + beside, both[:, COT_LANES:]], axis=1).astype(bf16)
    for n in range(4):
        faces_ref[n] = both


def silu_slope(values):
    logistic = jax.nn.sigmoid(values)
    return logistic * (1.0 + values * (1.0 - logistic))


def row_taps(ref, x, width):
    return jnp.concatenate(
        [ref[c, x, :, b * 128 : b * 128 + width] for b in range(3) for c in range(3)], axis=0
    )


def conv_kernel(
    field_ref, cot_ref, faces_ref, fwd_ref, offset_ref,
    sums_ref, up_ref, rim_ref,
    halo, shifted, edge, acc,
):
    me = lax.axis_index("gz")
    before, after = lax.rem(me + 3, 4), lax.rem(me + 1, 4)

    def across(rows, place):
        return lax.dot_general(rows, place, (((0,), (0,)), ((), ())), preferred_element_type=f32)

    sides = [faces_ref[at].astype(f32) for at in (before, me, after)]
    halo[...] = across(
        jnp.concatenate([sides[0], sides[2]], axis=0).astype(bf16),
        select((16, 128), 0, 1, (None, 0) + (None,) * 8 + (127,)),
    ).astype(bf16)
    lane = lax.broadcasted_iota(jnp.int32, (C, 128), 1)
    for x in range(7):
        for y in range(12):
            row = field_ref[y, x]
            ends = halo[(y * 8 + x) * C : (y * 8 + x) * C + C, :]
            at = slice(y * 128, y * 128 + 128)
            shifted[0, x, :, at] = jnp.where(lane == 0, ends, pltpu.roll(row, 1, 1))
            shifted[1, x, :, at] = row
            shifted[2, x, :, at] = jnp.where(lane == 127, ends, pltpu.roll(row, 127, 1))
        part = jnp.dot(fwd_ref[...], row_taps(shifted, x, OUT), preferred_element_type=f32)
        for a in range(3):
            if 0 <= x - a < 5:
                if a == 0:
                    acc[x] = part[:C]
                else:
                    acc[x - a] += part[a * C : a * C + C]

    def spread(count, moves):
        rows = jnp.concatenate(
            [side[:, y * 256 : y * 256 + 256] for side in sides for y in range(count)], axis=0
        ).astype(bf16)
        row = lax.broadcasted_iota(jnp.int32, (count * 24, 128), 0)
        to = lax.broadcasted_iota(jnp.int32, (count * 24, 128), 1)
        place = jnp.zeros((count * 24, 128), f32)
        for n, (side, k, m) in enumerate(moves):
            y = (row >> 3) - side * count
            hit = ((row & 7) == k) & (to == y * EDGE + m) & (y >= 0) & (y < count)
            place = jnp.where(hit, 1.0, place)
        return across(rows, place.astype(bf16))

    rim = spread(12, ((0, 0, 0), (0, 1, 1), (1, 2, 2), (1, 1, 3), (2, 2, 4), (2, 3, 5)))
    for t in range(9):
        shift = (t // 3) * EDGE + t % 3
        edge[t] = (pltpu.roll(rim, 128 - shift, 1) if shift else rim).astype(bf16)
    rim_cot = spread(10, ((0, 4, 0), (2, 5, 3)))
    block = jnp.concatenate(
        [jnp.concatenate([edge[t, x * C : x * C + C] for t in range(9)], axis=0) for x in range(7)], axis=1
    )
    part = jnp.dot(fwd_ref[...], block, preferred_element_type=f32)
    offset = offset_ref[...]
    for x in range(5):
        preact = offset + sum(
            part[a * C : a * C + C, (x + a) * 128 : (x + a) * 128 + 128] for a in range(3)
        )
        rim_ref[x] = (rim_cot[x * C : x * C + C] * silu_slope(preact)).astype(bf16)

    ups = []
    for x in range(5):
        beside = jnp.concatenate([cot_ref[y, x] for y in range(10)], axis=1).astype(f32)
        upstream = (beside * silu_slope(acc[x] + offset)).astype(bf16)
        up_ref[x] = upstream
        ups.append(upstream[:, 128 : 128 + OWN] if 1 <= x <= 3 else jnp.zeros((C, OWN), bf16))

    left = jnp.concatenate(
        [
            jnp.concatenate([ups[x - a] if 0 <= x - a < 5 else ups[0] for a in range(3)], axis=0)
            for x in range(1, 6)
        ],
        axis=1,
    )
    right = jnp.concatenate(
        [
            jnp.concatenate(
                [shifted[c, x, :, b * 128 + 128 : b * 128 + 128 + OWN] for b in range(3) for c in range(3)], axis=0
            )
            for x in range(1, 6)
        ],
        axis=1,
    )
    total = lax.dot_general(left, right, (((1,), (1,)), ((), ())), preferred_element_type=f32)

    offsets = sum(jnp.sum(ups[x].astype(f32), axis=1, keepdims=True) for x in range(1, 4))
    packed = jnp.concatenate(
        [total[a * C : a * C + C] for a in range(3)] + [jnp.broadcast_to(offsets, (C, C))], axis=1
    )
    for s in range(4):
        for l in range(8):
            at = (s * 8 + l) * 8
            if l < 7:
                sums_ref[at : at + 8] = packed[8 * s : 8 * s + 8, 128 * l : 128 * l + 128]
            else:
                sums_ref[at : at + 8] = jnp.zeros((8, 128), f32)


def grad_kernel_body(up_ref, rim_ref, bwd_ref, grad_ref, shifted, acc):
    lane = lax.broadcasted_iota(jnp.int32, (C, 128), 1)
    for x in range(5):
        rim = rim_ref[x].astype(f32)
        for y in range(10):
            at = slice(y * 128, y * 128 + 128)
            row = up_ref[x, :, at]
            low = jnp.broadcast_to(rim[:, y * EDGE : y * EDGE + 1], (C, 128)).astype(bf16)
            high = jnp.broadcast_to(rim[:, y * EDGE + 3 : y * EDGE + 4], (C, 128)).astype(bf16)
            shifted[0, x, :, at] = jnp.where(lane == 0, low, pltpu.roll(row, 1, 1))
            shifted[1, x, :, at] = row
            shifted[2, x, :, at] = jnp.where(lane == 127, high, pltpu.roll(row, 127, 1))
        part = jnp.dot(bwd_ref[...], row_taps(shifted, x, OWN), preferred_element_type=f32)
        for a in range(3):
            if 0 <= x - a < 3:
                if a == 0:
                    acc[x] = part[:C]
                else:
                    acc[x - a] += part[a * C : a * C + C]

    to = lax.broadcasted_iota(jnp.int32, (256, 256), 0)
    of = lax.broadcasted_iota(jnp.int32, (256, 256), 1)
    perm = jnp.where((to & 7) * C + (to >> 3) == of, 1.0, 0.0).astype(bf16)
    for x in range(3):
        rows = jnp.concatenate(
            [acc[x, :, y * 128 : y * 128 + 128] for y in range(8)], axis=0
        ).astype(bf16)
        moved = jnp.dot(perm, rows, preferred_element_type=f32)
        grad_ref[:, x] = moved.reshape(C, 8, 128).astype(bf16)


def identity():
    return jnp.where(
        lax.broadcasted_iota(jnp.int32, (C, C), 0) == lax.broadcasted_iota(jnp.int32, (C, C), 1), 1.0, 0.0
    )


def modulate_kernel(
    cosmology_ref, lift_ref, bias_ref, weight_ref, sbias_ref, taps_ref, offset_ref,
    fwd_ref, bwd_ref, kernel_ref, modded_ref, styles_ref, inv_ref, lifted_ref, hidden_ref, params_ref, column_ref,
):
    first, second = cosmology_ref[:, 0:1], cosmology_ref[:, 1:2]
    lifted = first * lift_ref[0:1] + second * lift_ref[1:2] + bias_ref[...]
    hidden = lifted * jax.nn.sigmoid(lifted)
    eye = identity()
    column = jnp.sum(weight_ref[...] * hidden, axis=1, keepdims=True)
    styles = jnp.sum(column * eye, axis=0, keepdims=True) + sbias_ref[...] + 1.0
    kernel = jnp.concatenate([taps_ref[t] for t in range(TAPS)] + [jnp.zeros((C, C), f32)], axis=1)
    styles = jnp.concatenate([styles] * TAPS + [jnp.zeros((1, C), f32)], axis=1)
    modded = kernel * styles
    inv = lax.rsqrt(jnp.sum(modded * modded, axis=1, keepdims=True) + demod_eps)
    scaled = (modded * inv).astype(bf16)
    for a in range(3):
        fwd_ref[a * C : a * C + C] = scaled[:, a * 288 : a * 288 + 288]
    turned = scaled.astype(f32).T
    for a in range(3):
        bwd_ref[a * C : a * C + C] = jnp.concatenate(
            [turned[(26 - a * 9 - t) * C : (27 - a * 9 - t) * C] for t in range(9)], axis=1
        ).astype(bf16)
    kernel_ref[...] = kernel
    modded_ref[...] = modded
    styles_ref[...] = styles
    inv_ref[...] = inv
    lifted_ref[...] = lifted
    hidden_ref[...] = hidden
    params_ref[...] = jnp.concatenate([first, second], axis=0)
    column_ref[...] = jnp.sum(offset_ref[...] * eye, axis=1, keepdims=True)


def total_kernel(parts_ref, spread_ref):
    part = jnp.sum(parts_ref[...], axis=0)
    for n in range(spread_ref.shape[0]):
        spread_ref[n] = part


def tail_kernel(
    sums_ref, kernel_ref, modded_ref, styles_ref, inv_ref, lifted_ref, hidden_ref, weight_ref, cosmology_ref,
    kernel_out, offset_out, lift_out, bias_out, style_out, sbias_out,
):
    def total(values):
        return jnp.sum(jnp.sum(values, axis=1, keepdims=True), axis=0, keepdims=True)

    sums = jnp.concatenate(
        [
            jnp.concatenate([sums_ref[(s * 8 + l) * 8 : (s * 8 + l) * 8 + 8] for s in range(4)], axis=0)
            for l in range(7)
        ],
        axis=1,
    )
    kernel, modded, styles, inv = kernel_ref[...], modded_ref[...], styles_ref[...], inv_ref[...]
    eye = identity()
    offset = jnp.sum(sums[:, TAPS * C : TAPS * C + C] * eye, axis=0, keepdims=True)
    projected = jnp.sum(sums * modded, axis=1, keepdims=True)
    mod_grad = inv * (sums - modded * (inv * inv * projected))
    raw = mod_grad * styles
    lanes = jnp.sum(mod_grad * kernel, axis=0, keepdims=True)
    folded = sum(lanes[:, 128 * l : 128 * l + 128] for l in range(7))
    row = sum(folded[:, C * n : C * n + C] for n in range(4))
    column = jnp.sum(row * eye, axis=1, keepdims=True)
    lifted_grad = jnp.sum(weight_ref[...] * column, axis=0, keepdims=True) * silu_slope(lifted_ref[...])
    style_raw = column * hidden_ref[...]
    lift_raw = cosmology_ref[...] * lifted_grad
    squares = sum(total(v * v) for v in (raw, offset, lift_raw, lifted_grad, style_raw, row))
    entries = TAPS * C * C + C + lift_raw.size + lifted_grad.size + style_raw.size + C
    factor = jnp.minimum(1.0, lax.rsqrt(squares / entries + clip_eps))
    raw = raw * factor
    for t in range(TAPS):
        kernel_out[t] = raw[:, C * t : C * t + C]
    offset_out[...] = offset * factor
    lift_out[...] = lift_raw * factor
    bias_out[...] = lifted_grad * factor
    style_out[...] = style_raw * factor
    sbias_out[...] = row * factor


def shifts(axis):
    n = lax.axis_size(axis)
    ahead = [(i, (i + 1) % n) for i in range(n)]
    return ahead, [(j, i) for i, j in ahead]


def summed(sums):
    flat = ("ghi", "gy", "gz")
    parts = lax.all_to_all(sums.reshape(32, 8, 128), flat, 0, 0, tiled=True)
    (spread,) = call(total_kernel, [shape(16, 8, 128, dtype=f32)], 1, limit=4)(parts)
    parts = lax.all_to_all(spread, "glong", 0, 0, tiled=True)
    (spread,) = call(total_kernel, [shape(32, 8, 128, dtype=f32)], 1, limit=4)(parts)
    return lax.all_to_all(spread, flat, 0, 0, tiled=True).reshape(256, 128)


def body(
    field, cotangent, cosmology, lift_weight, lift_bias, style_weight, style_bias, kernel, offset
):
    low, high, mid = pl.pallas_call(
        split_kernel,
        out_shape=[shape(3, 8, C, 128), shape(3, 8, C, 128), shape(1, 8, C, 128)],
        in_specs=[pl.BlockSpec(memory_space=pltpu.HBM)] * 2,
        out_specs=[VMEM] * 3,
        scratch_shapes=[
            pltpu.VMEM((C, 3, 8, 128), bf16), pltpu.VMEM((C, 3, 8, 128), bf16), pltpu.SemaphoreType.DMA((2,)),
        ],
        compiler_params=pltpu.CompilerParams(vmem_limit_bytes=4 * 1024 * 1024),
    )(*(pltpu.with_memory_space_constraint(block, pltpu.HBM) for block in (field, cotangent)))
    ahead, back = shifts(("glong", "ghi"))
    left = lax.ppermute(high, ("glong", "ghi"), ahead)
    right = lax.ppermute(low, ("glong", "ghi"), back)

    taps = jnp.transpose(kernel, (2, 3, 4, 0, 1)).reshape(TAPS, C, C)
    fwd, bwd, packed, modded, styles, inv_norm, lifted, hidden, params, column = call(
        modulate_kernel,
        [
            shape(3 * C, 9 * C), shape(3 * C, 9 * C), shape(C, 896, dtype=f32), shape(C, 896, dtype=f32),
            shape(1, 896, dtype=f32), shape(C, 1, dtype=f32), shape(1, 256, dtype=f32), shape(1, 256, dtype=f32),
            shape(2, 1, dtype=f32), shape(C, 1, dtype=f32),
        ],
        7,
        limit=8,
    )(
        cosmology[None, :], lift_weight, lift_bias[None, :], style_weight.T, style_bias[None, :], taps,
        offset[None, :],
    )

    rows = (low, high, mid, left, right)
    up, down = call(pack_kernel, [shape(19, C, 128), shape(19, C, 128)], 6, limit=8)(*rows, column)
    ahead, back = shifts("gy")
    up = lax.ppermute(up, "gy", ahead)
    down = lax.ppermute(down, "gy", back)

    field_rows, cot_rows, faces = call(
        gather_kernel, [shape(12, 8, C, 128), shape(10, 8, C, 128), shape(4, 8, FIELD_LANES)], 7
    )(*rows, up, down)
    faces = lax.all_to_all(faces, "gz", 0, 0, tiled=True)

    sums, upstream, rim = call(
        conv_kernel,
        [shape(256, 128, dtype=f32), shape(5, C, OUT), shape(5, C, 128)],
        5,
        flops=540_000_000,
        scratch=[
            pltpu.VMEM((FIELD_LANES, 128), bf16),
            pltpu.VMEM((3, 7, C, 12 * 128), bf16),
            pltpu.VMEM((9, 8 * C, 128), bf16),
            pltpu.VMEM((5, C, OUT), f32),
        ],
    )(field_rows, cot_rows, faces, fwd, column)
    (grad_field,) = call(
        grad_kernel_body,
        [shape(C, 3, 8, 128)],
        3,
        flops=170_000_000,
        scratch=[pltpu.VMEM((3, 5, C, OUT), bf16), pltpu.VMEM((3, C, OWN), f32)],
    )(upstream, rim, bwd)

    kernel_out, grad_offset, grad_lift, grad_liftbias, grad_style, grad_stylebias = call(
        tail_kernel,
        [
            shape(TAPS, C, C, dtype=f32), shape(1, C, dtype=f32), shape(2, 256, dtype=f32),
            shape(1, 256, dtype=f32), shape(C, 256, dtype=f32), shape(1, C, dtype=f32),
        ],
        9,
        limit=8,
    )(
        summed(sums), packed, modded, styles, inv_norm, lifted, hidden, style_weight.T, params,
    )
    grad_kernel = jnp.transpose(kernel_out.reshape(3, 3, 3, C, C), (3, 4, 0, 1, 2))
    return (
        grad_field, grad_kernel, grad_offset[0], grad_lift, grad_liftbias[0], grad_style.T, grad_stylebias[0],
    )


def solution(mesh):
    cut = Mesh(mesh.devices.reshape(16, 2, 4, 4), ("glong", "ghi", "gy", "gz"))
    grid = P(None, ("glong", "ghi"), "gy", "gz")
    return jax.shard_map(
        body, mesh=cut, in_specs=(grid,) * 2 + (P(),) * 7, out_specs=(grid,) + (P(),) * 6, check_vma=False
    )
```

```python
import numpy as np
import jax
import jax.numpy as jnp
from jax import lax
from jax.experimental import pallas as pl
from jax.experimental.pallas import tpu as pltpu
from jax.sharding import Mesh, PartitionSpec as P

demod_eps = 1e-06
clip_eps = 1e-06

C = 32
TAPS = 27
EDGE = 6
FIELD_LANES = 12 * 8 * C
COT_LANES = 10 * 8 * C
OUT = 10 * 128
OWN = 8 * 128
f32 = jnp.float32
bf16 = jnp.bfloat16
VMEM = pl.BlockSpec(memory_space=pltpu.VMEM)


def call(kernel, outs, n_in, flops=0, limit=24, scratch=()):
    return pl.pallas_call(
        kernel,
        out_shape=outs,
        in_specs=[VMEM] * n_in,
        out_specs=[VMEM] * len(outs),
        scratch_shapes=list(scratch),
        cost_estimate=pl.CostEstimate(flops=flops, bytes_accessed=1 << 20, transcendentals=0),
        compiler_params=pltpu.CompilerParams(vmem_limit_bytes=limit * 1024 * 1024),
    )


def shape(*dims, dtype=bf16):
    return jax.ShapeDtypeStruct(dims, dtype)


def select(dims, row_axis, lane_axis, lanes):
    row = lax.broadcasted_iota(jnp.int32, dims, row_axis)
    lane = lax.broadcasted_iota(jnp.int32, dims, lane_axis)
    hit = jnp.zeros(dims, f32)
    for n, at in enumerate(lanes):
        if at is not None:
            hit = jnp.where((row == n) & (lane == at), 1.0, hit)
    return hit.astype(bf16)


def split_kernel(field_hbm, cot_hbm, low_ref, high_ref, mid_ref, field_ref, cot_ref, sems):
    fetches = (
        pltpu.make_async_copy(field_hbm, field_ref, sems.at[0]),
        pltpu.make_async_copy(cot_hbm, cot_ref, sems.at[1]),
    )
    for fetch in fetches:
        fetch.start()
    to = lax.broadcasted_iota(jnp.int32, (256, 256), 0)
    of = lax.broadcasted_iota(jnp.int32, (256, 256), 1)
    perm = jnp.where((of & 7) * C + (of >> 3) == to, 1.0, 0.0).astype(bf16)

    def rows(ref, x):
        block = ref[:, x].astype(f32).reshape(C * 8, 128).astype(bf16)
        return jnp.dot(perm, block, preferred_element_type=f32).astype(bf16).reshape(8, C, 128)

    fetches[0].wait()
    f0, f1, f2 = (rows(field_ref, x) for x in range(3))
    low_ref[0], low_ref[1] = f0, f1
    high_ref[0], high_ref[1] = f1, f2
    fetches[1].wait()
    c0, c1, c2 = (rows(cot_ref, x) for x in range(3))
    low_ref[2], high_ref[2], mid_ref[0] = c0, c2, c1


def planes(low_ref, high_ref, mid_ref, left_ref, right_ref):
    field = (
        (left_ref, 0), (left_ref, 1), (low_ref, 0), (low_ref, 1), (high_ref, 1), (right_ref, 0), (right_ref, 1),
    )
    cot = ((left_ref, 2), (low_ref, 2), (mid_ref, 0), (high_ref, 2), (right_ref, 2))
    return field, cot


def pack_kernel(low_ref, high_ref, mid_ref, left_ref, right_ref, _, up_ref, down_ref):
    field, cot = planes(low_ref, high_ref, mid_ref, left_ref, right_ref)
    for n, (ref, at) in enumerate(field):
        up_ref[2 * n : 2 * n + 2] = ref[at, 6:8]
        down_ref[2 * n : 2 * n + 2] = ref[at, 0:2]
    for n, (ref, at) in enumerate(cot):
        up_ref[14 + n] = ref[at, 7]
        down_ref[14 + n] = ref[at, 0]


def gather_kernel(
    low_ref, high_ref, mid_ref, left_ref, right_ref, up_ref, down_ref, field_out, cot_out, faces_ref
):
    field, cot = planes(low_ref, high_ref, mid_ref, left_ref, right_ref)
    for n, (ref, at) in enumerate(field):
        for y in range(12):
            if y < 2:
                row = up_ref[2 * n + y]
            elif y < 10:
                row = ref[at, y - 2]
            else:
                row = down_ref[2 * n + y - 10]
            field_out[y, n] = row
    field_out[:, 7:] = jnp.zeros((12, 1, C, 128), bf16)
    for n, (ref, at) in enumerate(cot):
        for y in range(10):
            cot_out[y, n] = up_ref[14 + n] if y == 0 else down_ref[14 + n] if y == 9 else ref[at, y - 1]
    cot_out[:, 5:] = jnp.zeros((10, 3, C, 128), bf16)

    def faces(lanes, rows):
        pick = select((8, 128), 0, 1, lanes)
        return lax.dot_general(
            pick, rows, (((1,), (1,)), ((), ())), preferred_element_type=f32
        )

    both = faces((126, 127, None, 0, 1, None), field_out[...].reshape(FIELD_LANES, 128))
    beside = faces((None, None, 127, None, None, 0), cot_out[...].reshape(COT_LANES, 128))
    both = jnp.concatenate([both[:, :COT_LANES] + beside, both[:, COT_LANES:]], axis=1)

    def chunk(first):
        return jnp.concatenate(
            [both[first : first + 4, y * 256 : y * 256 + 256] for y in range(12)], axis=0
        ).astype(bf16)

    me = lax.axis_index("gz")
    high = chunk(0)
    faces_ref[me] = high
    faces_ref[lax.rem(me + 1, 4)] = high
    faces_ref[lax.rem(me + 2, 4)] = jnp.zeros_like(high)
    faces_ref[lax.rem(me + 3, 4)] = chunk(3)


def silu_slope(values):
    logistic = jax.nn.sigmoid(values)
    return logistic * (1.0 + values * (1.0 - logistic))


def row_taps(ref, x, width):
    return jnp.concatenate(
        [ref[c, x, :, b * 128 : b * 128 + width] for b in range(3) for c in range(3)], axis=0
    )


def conv_kernel(
    field_ref, cot_ref, faces_ref, fwd_ref, offset_ref,
    sums_ref, up_ref, rim_ref,
    halo, shifted, edge, acc,
):
    me = lax.axis_index("gz")
    before, after = lax.rem(me + 3, 4), lax.rem(me + 1, 4)

    def across(rows, place):
        return lax.dot_general(rows, place, (((0,), (0,)), ((), ())), preferred_element_type=f32)

    sides = jnp.concatenate([faces_ref[at] for at in (before, me, after)], axis=0)
    row = lax.broadcasted_iota(jnp.int32, (144, 128), 0)
    to = lax.broadcasted_iota(jnp.int32, (144, 128), 1)

    def spread(moves):
        place = jnp.zeros((144, 128), f32)
        for side, k, m in moves:
            y = (row >> 2) - side * 12
            hit = ((row & 3) == k) & (to == y * EDGE + m) & (y >= 0) & (y < 12)
            place = jnp.where(hit, 1.0, place)
        return across(sides, place.astype(bf16))

    rim = spread(((0, 0, 0), (0, 1, 1), (1, 3, 2), (1, 1, 3), (2, 0, 4), (2, 1, 5)))
    rim_cot = spread(((0, 2, 0), (2, 2, 3)))

    row = lax.broadcasted_iota(jnp.int32, (128, 12 * 128), 0)
    to = lax.broadcasted_iota(jnp.int32, (128, 12 * 128), 1)
    at = (to >> 7) * EDGE
    place = jnp.where(((to & 127) == 0) & (row == at + 1) | ((to & 127) == 127) & (row == at + 4), 1.0, 0.0)
    halo[...] = jnp.dot(rim.astype(bf16), place.astype(bf16), preferred_element_type=f32).astype(bf16)
    lane = lax.broadcasted_iota(jnp.int32, (C, 128), 1)
    for x in range(7):
        for y in range(12):
            row = field_ref[y, x]
            at = slice(y * 128, y * 128 + 128)
            ends = halo[x * C : x * C + C, at]
            shifted[0, x, :, at] = jnp.where(lane == 0, ends, pltpu.roll(row, 1, 1))
            shifted[1, x, :, at] = row
            shifted[2, x, :, at] = jnp.where(lane == 127, ends, pltpu.roll(row, 127, 1))
        part = jnp.dot(fwd_ref[...], row_taps(shifted, x, OUT), preferred_element_type=f32)
        for a in range(3):
            if 0 <= x - a < 5:
                if a == 0:
                    acc[x] = part[:C]
                else:
                    acc[x - a] += part[a * C : a * C + C]

    for t in range(9):
        shift = (t // 3) * EDGE + t % 3
        edge[t] = (pltpu.roll(rim, 128 - shift, 1) if shift else rim).astype(bf16)
    block = jnp.concatenate(
        [jnp.concatenate([edge[t, x * C : x * C + C] for t in range(9)], axis=0) for x in range(7)], axis=1
    )
    part = jnp.dot(fwd_ref[...], block, preferred_element_type=f32)
    offset = offset_ref[...]
    for x in range(5):
        preact = offset + sum(
            part[a * C : a * C + C, (x + a) * 128 : (x + a) * 128 + 128] for a in range(3)
        )
        rim_ref[x] = (rim_cot[x * C : x * C + C] * silu_slope(preact)).astype(bf16)

    ups = []
    for x in range(5):
        beside = jnp.concatenate([cot_ref[y, x] for y in range(10)], axis=1).astype(f32)
        upstream = (beside * silu_slope(acc[x] + offset)).astype(bf16)
        up_ref[x] = upstream
        ups.append(upstream[:, 128 : 128 + OWN] if 1 <= x <= 3 else jnp.zeros((C, OWN), bf16))

    left = jnp.concatenate(
        [
            jnp.concatenate([ups[x - a] if 0 <= x - a < 5 else ups[0] for a in range(3)], axis=0)
            for x in range(1, 6)
        ],
        axis=1,
    )
    right = jnp.concatenate(
        [
            jnp.concatenate(
                [shifted[c, x, :, b * 128 + 128 : b * 128 + 128 + OWN] for b in range(3) for c in range(3)], axis=0
            )
            for x in range(1, 6)
        ],
        axis=1,
    )
    total = lax.dot_general(left, right, (((1,), (1,)), ((), ())), preferred_element_type=f32)

    offsets = sum(jnp.sum(ups[x].astype(f32), axis=1, keepdims=True) for x in range(1, 4))
    packed = jnp.concatenate(
        [total[a * C : a * C + C] for a in range(3)] + [jnp.broadcast_to(offsets, (C, C))], axis=1
    )
    for s in range(4):
        for l in range(8):
            at = (s * 8 + l) * 8
            if l < 7:
                sums_ref[at : at + 8] = packed[8 * s : 8 * s + 8, 128 * l : 128 * l + 128]
            else:
                sums_ref[at : at + 8] = jnp.zeros((8, 128), f32)


def grad_kernel_body(up_ref, rim_ref, bwd_ref, grad_ref, shifted, acc):
    lane = lax.broadcasted_iota(jnp.int32, (C, 128), 1)
    for x in range(5):
        rim = rim_ref[x].astype(f32)
        for y in range(10):
            at = slice(y * 128, y * 128 + 128)
            row = up_ref[x, :, at]
            low = jnp.broadcast_to(rim[:, y * EDGE : y * EDGE + 1], (C, 128)).astype(bf16)
            high = jnp.broadcast_to(rim[:, y * EDGE + 3 : y * EDGE + 4], (C, 128)).astype(bf16)
            shifted[0, x, :, at] = jnp.where(lane == 0, low, pltpu.roll(row, 1, 1))
            shifted[1, x, :, at] = row
            shifted[2, x, :, at] = jnp.where(lane == 127, high, pltpu.roll(row, 127, 1))
        part = jnp.dot(bwd_ref[...], row_taps(shifted, x, OWN), preferred_element_type=f32)
        for a in range(3):
            if 0 <= x - a < 3:
                if a == 0:
                    acc[x] = part[:C]
                else:
                    acc[x - a] += part[a * C : a * C + C]

    to = lax.broadcasted_iota(jnp.int32, (256, 256), 0)
    of = lax.broadcasted_iota(jnp.int32, (256, 256), 1)
    perm = jnp.where((to & 7) * C + (to >> 3) == of, 1.0, 0.0).astype(bf16)
    for x in range(3):
        rows = jnp.concatenate(
            [acc[x, :, y * 128 : y * 128 + 128] for y in range(8)], axis=0
        ).astype(bf16)
        moved = jnp.dot(perm, rows, preferred_element_type=f32)
        grad_ref[:, x] = moved.reshape(C, 8, 128).astype(bf16)


def identity():
    return jnp.where(
        lax.broadcasted_iota(jnp.int32, (C, C), 0) == lax.broadcasted_iota(jnp.int32, (C, C), 1), 1.0, 0.0
    )


def modulate_kernel(
    cosmology_ref, lift_ref, bias_ref, weight_ref, sbias_ref, taps_ref, offset_ref,
    fwd_ref, bwd_ref, kernel_ref, modded_ref, styles_ref, inv_ref, lifted_ref, hidden_ref, params_ref, column_ref,
):
    first, second = cosmology_ref[:, 0:1], cosmology_ref[:, 1:2]
    lifted = first * lift_ref[0:1] + second * lift_ref[1:2] + bias_ref[...]
    hidden = lifted * jax.nn.sigmoid(lifted)
    eye = identity()
    column = jnp.sum(weight_ref[...] * hidden, axis=1, keepdims=True)
    styles = jnp.sum(column * eye, axis=0, keepdims=True) + sbias_ref[...] + 1.0
    kernel = jnp.concatenate([taps_ref[t] for t in range(TAPS)] + [jnp.zeros((C, C), f32)], axis=1)
    styles = jnp.concatenate([styles] * TAPS + [jnp.zeros((1, C), f32)], axis=1)
    modded = kernel * styles
    inv = lax.rsqrt(jnp.sum(modded * modded, axis=1, keepdims=True) + demod_eps)
    scaled = (modded * inv).astype(bf16)
    for a in range(3):
        fwd_ref[a * C : a * C + C] = scaled[:, a * 288 : a * 288 + 288]
    turned = scaled.astype(f32).T
    for a in range(3):
        bwd_ref[a * C : a * C + C] = jnp.concatenate(
            [turned[(26 - a * 9 - t) * C : (27 - a * 9 - t) * C] for t in range(9)], axis=1
        ).astype(bf16)
    kernel_ref[...] = kernel
    modded_ref[...] = modded
    styles_ref[...] = styles
    inv_ref[...] = inv
    lifted_ref[...] = lifted
    hidden_ref[...] = hidden
    params_ref[...] = jnp.concatenate([first, second], axis=0)
    column_ref[...] = jnp.sum(offset_ref[...] * eye, axis=1, keepdims=True)


def total_kernel(parts_ref, spread_ref):
    part = jnp.sum(parts_ref[...], axis=0)
    for n in range(spread_ref.shape[0]):
        spread_ref[n] = part


def tail_kernel(
    sums_ref, kernel_ref, modded_ref, styles_ref, inv_ref, lifted_ref, hidden_ref, weight_ref, cosmology_ref,
    kernel_out, offset_out, lift_out, bias_out, style_out, sbias_out,
):
    def total(values):
        return jnp.sum(jnp.sum(values, axis=1, keepdims=True), axis=0, keepdims=True)

    sums = jnp.concatenate(
        [
            jnp.concatenate([sums_ref[(s * 8 + l) * 8 : (s * 8 + l) * 8 + 8] for s in range(4)], axis=0)
            for l in range(7)
        ],
        axis=1,
    )
    kernel, modded, styles, inv = kernel_ref[...], modded_ref[...], styles_ref[...], inv_ref[...]
    eye = identity()
    offset = jnp.sum(sums[:, TAPS * C : TAPS * C + C] * eye, axis=0, keepdims=True)
    projected = jnp.sum(sums * modded, axis=1, keepdims=True)
    mod_grad = inv * (sums - modded * (inv * inv * projected))
    raw = mod_grad * styles
    lanes = jnp.sum(mod_grad * kernel, axis=0, keepdims=True)
    folded = sum(lanes[:, 128 * l : 128 * l + 128] for l in range(7))
    row = sum(folded[:, C * n : C * n + C] for n in range(4))
    column = jnp.sum(row * eye, axis=1, keepdims=True)
    lifted_grad = jnp.sum(weight_ref[...] * column, axis=0, keepdims=True) * silu_slope(lifted_ref[...])
    style_raw = column * hidden_ref[...]
    lift_raw = cosmology_ref[...] * lifted_grad
    squares = sum(total(v * v) for v in (raw, offset, lift_raw, lifted_grad, style_raw, row))
    entries = TAPS * C * C + C + lift_raw.size + lifted_grad.size + style_raw.size + C
    factor = jnp.minimum(1.0, lax.rsqrt(squares / entries + clip_eps))
    raw = raw * factor
    for t in range(TAPS):
        kernel_out[t] = raw[:, C * t : C * t + C]
    offset_out[...] = offset * factor
    lift_out[...] = lift_raw * factor
    bias_out[...] = lifted_grad * factor
    style_out[...] = style_raw * factor
    sbias_out[...] = row * factor


def shifts(axis):
    n = lax.axis_size(axis)
    ahead = [(i, (i + 1) % n) for i in range(n)]
    return ahead, [(j, i) for i, j in ahead]


def summed(sums):
    flat = ("ghi", "gy", "gz")
    parts = lax.all_to_all(sums.reshape(32, 8, 128), flat, 0, 0, tiled=True)
    (spread,) = call(total_kernel, [shape(16, 8, 128, dtype=f32)], 1, limit=4)(parts)
    parts = lax.all_to_all(spread, "glong", 0, 0, tiled=True)
    (spread,) = call(total_kernel, [shape(32, 8, 128, dtype=f32)], 1, limit=4)(parts)
    return lax.all_to_all(spread, flat, 0, 0, tiled=True).reshape(256, 128)


def body(
    field, cotangent, cosmology, lift_weight, lift_bias, style_weight, style_bias, kernel, offset
):
    low, high, mid = pl.pallas_call(
        split_kernel,
        out_shape=[shape(3, 8, C, 128), shape(3, 8, C, 128), shape(1, 8, C, 128)],
        in_specs=[pl.BlockSpec(memory_space=pltpu.HBM)] * 2,
        out_specs=[VMEM] * 3,
        scratch_shapes=[
            pltpu.VMEM((C, 3, 8, 128), bf16), pltpu.VMEM((C, 3, 8, 128), bf16), pltpu.SemaphoreType.DMA((2,)),
        ],
        compiler_params=pltpu.CompilerParams(vmem_limit_bytes=4 * 1024 * 1024),
    )(*(pltpu.with_memory_space_constraint(block, pltpu.HBM) for block in (field, cotangent)))
    ahead, back = shifts(("glong", "ghi"))
    left = lax.ppermute(high, ("glong", "ghi"), ahead)
    right = lax.ppermute(low, ("glong", "ghi"), back)

    taps = jnp.transpose(kernel, (2, 3, 4, 0, 1)).reshape(TAPS, C, C)
    fwd, bwd, packed, modded, styles, inv_norm, lifted, hidden, params, column = call(
        modulate_kernel,
        [
            shape(3 * C, 9 * C), shape(3 * C, 9 * C), shape(C, 896, dtype=f32), shape(C, 896, dtype=f32),
            shape(1, 896, dtype=f32), shape(C, 1, dtype=f32), shape(1, 256, dtype=f32), shape(1, 256, dtype=f32),
            shape(2, 1, dtype=f32), shape(C, 1, dtype=f32),
        ],
        7,
        limit=8,
    )(
        cosmology[None, :], lift_weight, lift_bias[None, :], style_weight.T, style_bias[None, :], taps,
        offset[None, :],
    )

    rows = (low, high, mid, left, right)
    up, down = call(pack_kernel, [shape(19, C, 128), shape(19, C, 128)], 6, limit=8)(*rows, column)
    ahead, back = shifts("gy")
    up = lax.ppermute(up, "gy", ahead)
    down = lax.ppermute(down, "gy", back)

    field_rows, cot_rows, faces = call(
        gather_kernel, [shape(12, 8, C, 128), shape(10, 8, C, 128), shape(4, 48, 256)], 7
    )(*rows, up, down)
    faces = lax.all_to_all(faces, "gz", 0, 0, tiled=True)

    sums, upstream, rim = call(
        conv_kernel,
        [shape(256, 128, dtype=f32), shape(5, C, OUT), shape(5, C, 128)],
        5,
        flops=540_000_000,
        scratch=[
            pltpu.VMEM((8 * C, 12 * 128), bf16),
            pltpu.VMEM((3, 7, C, 12 * 128), bf16),
            pltpu.VMEM((9, 8 * C, 128), bf16),
            pltpu.VMEM((5, C, OUT), f32),
        ],
    )(field_rows, cot_rows, faces, fwd, column)
    (grad_field,) = call(
        grad_kernel_body,
        [shape(C, 3, 8, 128)],
        3,
        flops=170_000_000,
        scratch=[pltpu.VMEM((3, 5, C, OUT), bf16), pltpu.VMEM((3, C, OWN), f32)],
    )(upstream, rim, bwd)

    kernel_out, grad_offset, grad_lift, grad_liftbias, grad_style, grad_stylebias = call(
        tail_kernel,
        [
            shape(TAPS, C, C, dtype=f32), shape(1, C, dtype=f32), shape(2, 256, dtype=f32),
            shape(1, 256, dtype=f32), shape(C, 256, dtype=f32), shape(1, C, dtype=f32),
        ],
        9,
        limit=8,
    )(
        summed(sums), packed, modded, styles, inv_norm, lifted, hidden, style_weight.T, params,
    )
    grad_kernel = jnp.transpose(kernel_out.reshape(3, 3, 3, C, C), (3, 4, 0, 1, 2))
    return (
        grad_field, grad_kernel, grad_offset[0], grad_lift, grad_liftbias[0], grad_style.T, grad_stylebias[0],
    )


def solution(mesh):
    cut = Mesh(mesh.devices.reshape(16, 2, 4, 4), ("glong", "ghi", "gy", "gz"))
    grid = P(None, ("glong", "ghi"), "gy", "gz")
    return jax.shard_map(
        body, mesh=cut, in_specs=(grid,) * 2 + (P(),) * 7, out_specs=(grid,) + (P(),) * 6, check_vma=False
    )
```

```python
import numpy as np
import jax
import jax.numpy as jnp
from jax import lax
from jax.experimental import pallas as pl
from jax.experimental.pallas import tpu as pltpu
from jax.sharding import Mesh, PartitionSpec as P

demod_eps = 1e-06
clip_eps = 1e-06

C = 32
TAPS = 27
EDGE = 6
FIELD_LANES = 12 * 8 * C
COT_LANES = 10 * 8 * C
OUT = 10 * 128
OWN = 8 * 128
f32 = jnp.float32
bf16 = jnp.bfloat16
VMEM = pl.BlockSpec(memory_space=pltpu.VMEM)


def call(kernel, outs, n_in, flops=0, limit=24, scratch=()):
    return pl.pallas_call(
        kernel,
        out_shape=outs,
        in_specs=[VMEM] * n_in,
        out_specs=[VMEM] * len(outs),
        scratch_shapes=list(scratch),
        cost_estimate=pl.CostEstimate(flops=flops, bytes_accessed=1 << 20, transcendentals=0),
        compiler_params=pltpu.CompilerParams(vmem_limit_bytes=limit * 1024 * 1024),
    )


def shape(*dims, dtype=bf16):
    return jax.ShapeDtypeStruct(dims, dtype)


def select(dims, row_axis, lane_axis, lanes):
    row = lax.broadcasted_iota(jnp.int32, dims, row_axis)
    lane = lax.broadcasted_iota(jnp.int32, dims, lane_axis)
    hit = jnp.zeros(dims, f32)
    for n, at in enumerate(lanes):
        if at is not None:
            hit = jnp.where((row == n) & (lane == at), 1.0, hit)
    return hit.astype(bf16)


def split_kernel(field_hbm, cot_hbm, low_ref, high_ref, mid_ref, field_ref, cot_ref, sems):
    fetches = (
        pltpu.make_async_copy(field_hbm, field_ref, sems.at[0]),
        pltpu.make_async_copy(cot_hbm, cot_ref, sems.at[1]),
    )
    for fetch in fetches:
        fetch.start()
    to = lax.broadcasted_iota(jnp.int32, (256, 256), 0)
    of = lax.broadcasted_iota(jnp.int32, (256, 256), 1)
    perm = jnp.where((of & 7) * C + (of >> 3) == to, 1.0, 0.0).astype(bf16)

    def rows(ref, x):
        block = ref[:, x].astype(f32).reshape(C * 8, 128).astype(bf16)
        return jnp.dot(perm, block, preferred_element_type=f32).astype(bf16).reshape(8, C, 128)

    fetches[0].wait()
    f0, f1, f2 = (rows(field_ref, x) for x in range(3))
    low_ref[0], low_ref[1] = f0, f1
    high_ref[0], high_ref[1] = f1, f2
    fetches[1].wait()
    c0, c1, c2 = (rows(cot_ref, x) for x in range(3))
    low_ref[2], high_ref[2], mid_ref[0] = c0, c2, c1


def planes(low_ref, high_ref, mid_ref, left_ref, right_ref):
    field = (
        (left_ref, 0), (left_ref, 1), (low_ref, 0), (low_ref, 1), (high_ref, 1), (right_ref, 0), (right_ref, 1),
    )
    cot = ((left_ref, 2), (low_ref, 2), (mid_ref, 0), (high_ref, 2), (right_ref, 2))
    return field, cot


def pack_kernel(low_ref, high_ref, mid_ref, left_ref, right_ref, _, up_ref, down_ref):
    field, cot = planes(low_ref, high_ref, mid_ref, left_ref, right_ref)
    for n, (ref, at) in enumerate(field):
        up_ref[2 * n : 2 * n + 2] = ref[at, 6:8]
        down_ref[2 * n : 2 * n + 2] = ref[at, 0:2]
    for n, (ref, at) in enumerate(cot):
        up_ref[14 + n] = ref[at, 7]
        down_ref[14 + n] = ref[at, 0]


def gather_kernel(
    low_ref, high_ref, mid_ref, left_ref, right_ref, up_ref, down_ref, field_out, cot_out, faces_ref
):
    field, cot = planes(low_ref, high_ref, mid_ref, left_ref, right_ref)
    for n, (ref, at) in enumerate(field):
        for y in range(12):
            if y < 2:
                row = up_ref[2 * n + y]
            elif y < 10:
                row = ref[at, y - 2]
            else:
                row = down_ref[2 * n + y - 10]
            field_out[y, n] = row
    field_out[:, 7:] = jnp.zeros((12, 1, C, 128), bf16)
    for n, (ref, at) in enumerate(cot):
        for y in range(10):
            cot_out[y, n] = up_ref[14 + n] if y == 0 else down_ref[14 + n] if y == 9 else ref[at, y - 1]
    cot_out[:, 5:] = jnp.zeros((10, 3, C, 128), bf16)

    def faces(lanes, rows):
        pick = select((8, 128), 0, 1, lanes)
        return lax.dot_general(
            pick, rows, (((1,), (1,)), ((), ())), preferred_element_type=f32
        )

    both = faces((126, 127, None, 0, 1, None), field_out[...].reshape(FIELD_LANES, 128))
    beside = faces((None, None, 127, None, None, 0), cot_out[...].reshape(COT_LANES, 128))
    both = jnp.concatenate([both[:, :COT_LANES] + beside, both[:, COT_LANES:]], axis=1)

    def chunk(first):
        return jnp.concatenate(
            [both[first : first + 4, y * 256 : y * 256 + 256] for y in range(12)], axis=0
        ).astype(bf16)

    me = lax.axis_index("gz")
    high = chunk(0)
    faces_ref[me] = high
    faces_ref[lax.rem(me + 1, 4)] = high
    faces_ref[lax.rem(me + 2, 4)] = jnp.zeros_like(high)
    faces_ref[lax.rem(me + 3, 4)] = chunk(3)


def silu_slope(values):
    logistic = jax.nn.sigmoid(values)
    return logistic * (1.0 + values * (1.0 - logistic))


def row_taps(ref, x, width):
    return jnp.concatenate(
        [ref[c, x, :, b * 128 : b * 128 + width] for b in range(3) for c in range(3)], axis=0
    )


def conv_kernel(
    field_ref, cot_ref, faces_ref, fwd_ref, offset_ref, place_ref,
    sums_ref, up_ref, rim_ref,
    halo, shifted, edge, acc,
):
    me = lax.axis_index("gz")
    before, after = lax.rem(me + 3, 4), lax.rem(me + 1, 4)

    def across(rows, place):
        return lax.dot_general(rows, place, (((0,), (0,)), ((), ())), preferred_element_type=f32)

    sides = jnp.concatenate([faces_ref[at] for at in (before, me, after)], axis=0)
    spread = across(sides, place_ref[...])
    rim, rim_cot = spread[:, :128], spread[:, 128:256]
    halo[...] = spread[:, 256:].astype(bf16)
    lane = lax.broadcasted_iota(jnp.int32, (C, 128), 1)
    for x in range(7):
        for y in range(12):
            row = field_ref[y, x]
            at = slice(y * 128, y * 128 + 128)
            ends = halo[x * C : x * C + C, at]
            shifted[0, x, :, at] = jnp.where(lane == 0, ends, pltpu.roll(row, 1, 1))
            shifted[1, x, :, at] = row
            shifted[2, x, :, at] = jnp.where(lane == 127, ends, pltpu.roll(row, 127, 1))
        part = jnp.dot(fwd_ref[...], row_taps(shifted, x, OUT), preferred_element_type=f32)
        for a in range(3):
            if 0 <= x - a < 5:
                if a == 0:
                    acc[x] = part[:C]
                else:
                    acc[x - a] += part[a * C : a * C + C]

    for t in range(9):
        shift = (t // 3) * EDGE + t % 3
        edge[t] = (pltpu.roll(rim, 128 - shift, 1) if shift else rim).astype(bf16)
    block = jnp.concatenate(
        [jnp.concatenate([edge[t, x * C : x * C + C] for t in range(9)], axis=0) for x in range(7)], axis=1
    )
    part = jnp.dot(fwd_ref[...], block, preferred_element_type=f32)
    offset = offset_ref[...]
    for x in range(5):
        preact = offset + sum(
            part[a * C : a * C + C, (x + a) * 128 : (x + a) * 128 + 128] for a in range(3)
        )
        rim_ref[x] = (rim_cot[x * C : x * C + C] * silu_slope(preact)).astype(bf16)

    ups = []
    for x in range(5):
        beside = jnp.concatenate([cot_ref[y, x] for y in range(10)], axis=1).astype(f32)
        upstream = (beside * silu_slope(acc[x] + offset)).astype(bf16)
        up_ref[x] = upstream
        ups.append(upstream[:, 128 : 128 + OWN] if 1 <= x <= 3 else jnp.zeros((C, OWN), bf16))

    left = jnp.concatenate(
        [
            jnp.concatenate([ups[x - a] if 0 <= x - a < 5 else ups[0] for a in range(3)], axis=0)
            for x in range(1, 6)
        ],
        axis=1,
    )
    right = jnp.concatenate(
        [
            jnp.concatenate(
                [shifted[c, x, :, b * 128 + 128 : b * 128 + 128 + OWN] for b in range(3) for c in range(3)], axis=0
            )
            for x in range(1, 6)
        ],
        axis=1,
    )
    total = lax.dot_general(left, right, (((1,), (1,)), ((), ())), preferred_element_type=f32)

    offsets = sum(jnp.sum(ups[x].astype(f32), axis=1, keepdims=True) for x in range(1, 4))
    packed = jnp.concatenate(
        [total[a * C : a * C + C] for a in range(3)] + [jnp.broadcast_to(offsets, (C, C))], axis=1
    )
    for s in range(4):
        for l in range(8):
            at = (s * 8 + l) * 8
            if l < 7:
                sums_ref[at : at + 8] = packed[8 * s : 8 * s + 8, 128 * l : 128 * l + 128]
            else:
                sums_ref[at : at + 8] = jnp.zeros((8, 128), f32)


def grad_kernel_body(up_ref, rim_ref, bwd_ref, grad_ref, done_ref, shifted, acc):
    done_ref[...] = jnp.zeros_like(done_ref)
    lane = lax.broadcasted_iota(jnp.int32, (C, 128), 1)
    for x in range(5):
        rim = rim_ref[x].astype(f32)
        for y in range(10):
            at = slice(y * 128, y * 128 + 128)
            row = up_ref[x, :, at]
            low = jnp.broadcast_to(rim[:, y * EDGE : y * EDGE + 1], (C, 128)).astype(bf16)
            high = jnp.broadcast_to(rim[:, y * EDGE + 3 : y * EDGE + 4], (C, 128)).astype(bf16)
            shifted[0, x, :, at] = jnp.where(lane == 0, low, pltpu.roll(row, 1, 1))
            shifted[1, x, :, at] = row
            shifted[2, x, :, at] = jnp.where(lane == 127, high, pltpu.roll(row, 127, 1))
        part = jnp.dot(bwd_ref[...], row_taps(shifted, x, OWN), preferred_element_type=f32)
        for a in range(3):
            if 0 <= x - a < 3:
                if a == 0:
                    acc[x] = part[:C]
                else:
                    acc[x - a] += part[a * C : a * C + C]

    to = lax.broadcasted_iota(jnp.int32, (256, 256), 0)
    of = lax.broadcasted_iota(jnp.int32, (256, 256), 1)
    perm = jnp.where((to & 7) * C + (to >> 3) == of, 1.0, 0.0).astype(bf16)
    for x in range(3):
        rows = jnp.concatenate(
            [acc[x, :, y * 128 : y * 128 + 128] for y in range(8)], axis=0
        ).astype(bf16)
        moved = jnp.dot(perm, rows, preferred_element_type=f32)
        grad_ref[:, x] = moved.reshape(C, 8, 128).astype(bf16)


def identity():
    return jnp.where(
        lax.broadcasted_iota(jnp.int32, (C, C), 0) == lax.broadcasted_iota(jnp.int32, (C, C), 1), 1.0, 0.0
    )


def fill_places(place_ref):
    row = lax.broadcasted_iota(jnp.int32, (144, 128), 0)
    to = lax.broadcasted_iota(jnp.int32, (144, 128), 1)
    y, k = row >> 2, row & 3

    def place(moves):
        hit = jnp.zeros((144, 128), f32)
        for side, face, lane in moves:
            inside = (y >= side * 12) & (y < side * 12 + 12)
            hit = jnp.where(inside & (k == face) & (to == (y - side * 12) * EDGE + lane), 1.0, hit)
        return hit.astype(bf16)

    place_ref[:, :128] = place(((0, 0, 0), (0, 1, 1), (1, 3, 2), (1, 1, 3), (2, 0, 4), (2, 1, 5)))
    place_ref[:, 128:256] = place(((0, 2, 0), (2, 2, 3)))
    for n in range(12):
        ends = (to == 0) & (row == n * 4 + 1) | (to == 127) & (row == (24 + n) * 4)
        place_ref[:, 256 + n * 128 : 384 + n * 128] = jnp.where(ends, 1.0, 0.0).astype(bf16)


def modulate_kernel(
    cosmology_ref, lift_ref, bias_ref, weight_ref, sbias_ref, taps_ref, offset_ref,
    fwd_ref, bwd_ref, kernel_ref, modded_ref, styles_ref, inv_ref, lifted_ref, hidden_ref, params_ref, column_ref,
    place_ref,
):
    fill_places(place_ref)
    first, second = cosmology_ref[:, 0:1], cosmology_ref[:, 1:2]
    lifted = first * lift_ref[0:1] + second * lift_ref[1:2] + bias_ref[...]
    hidden = lifted * jax.nn.sigmoid(lifted)
    eye = identity()
    column = jnp.sum(weight_ref[...] * hidden, axis=1, keepdims=True)
    styles = jnp.sum(column * eye, axis=0, keepdims=True) + sbias_ref[...] + 1.0
    kernel = jnp.concatenate([taps_ref[t] for t in range(TAPS)] + [jnp.zeros((C, C), f32)], axis=1)
    styles = jnp.concatenate([styles] * TAPS + [jnp.zeros((1, C), f32)], axis=1)
    modded = kernel * styles
    inv = lax.rsqrt(jnp.sum(modded * modded, axis=1, keepdims=True) + demod_eps)
    scaled = (modded * inv).astype(bf16)
    for a in range(3):
        fwd_ref[a * C : a * C + C] = scaled[:, a * 288 : a * 288 + 288]
    turned = scaled.astype(f32).T
    for a in range(3):
        bwd_ref[a * C : a * C + C] = jnp.concatenate(
            [turned[(26 - a * 9 - t) * C : (27 - a * 9 - t) * C] for t in range(9)], axis=1
        ).astype(bf16)
    kernel_ref[...] = kernel
    modded_ref[...] = modded
    styles_ref[...] = styles
    inv_ref[...] = inv
    lifted_ref[...] = lifted
    hidden_ref[...] = hidden
    params_ref[...] = jnp.concatenate([first, second], axis=0)
    column_ref[...] = jnp.sum(offset_ref[...] * eye, axis=1, keepdims=True)


def total_kernel(parts_ref, *rest):
    spread_ref = rest[-1]
    part = jnp.sum(parts_ref[...], axis=0)
    for n in range(spread_ref.shape[0]):
        spread_ref[n] = part


def tail_kernel(
    sums_ref, kernel_ref, modded_ref, styles_ref, inv_ref, lifted_ref, hidden_ref, weight_ref, cosmology_ref,
    kernel_out, offset_out, lift_out, bias_out, style_out, sbias_out,
):
    def total(values):
        return jnp.sum(jnp.sum(values, axis=1, keepdims=True), axis=0, keepdims=True)

    sums = jnp.concatenate(
        [
            jnp.concatenate([sums_ref[(s * 8 + l) * 8 : (s * 8 + l) * 8 + 8] for s in range(4)], axis=0)
            for l in range(7)
        ],
        axis=1,
    )
    kernel, modded, styles, inv = kernel_ref[...], modded_ref[...], styles_ref[...], inv_ref[...]
    eye = identity()
    offset = jnp.sum(sums[:, TAPS * C : TAPS * C + C] * eye, axis=0, keepdims=True)
    projected = jnp.sum(sums * modded, axis=1, keepdims=True)
    mod_grad = inv * (sums - modded * (inv * inv * projected))
    raw = mod_grad * styles
    lanes = jnp.sum(mod_grad * kernel, axis=0, keepdims=True)
    folded = sum(lanes[:, 128 * l : 128 * l + 128] for l in range(7))
    row = sum(folded[:, C * n : C * n + C] for n in range(4))
    column = jnp.sum(row * eye, axis=1, keepdims=True)
    lifted_grad = jnp.sum(weight_ref[...] * column, axis=0, keepdims=True) * silu_slope(lifted_ref[...])
    style_raw = column * hidden_ref[...]
    lift_raw = cosmology_ref[...] * lifted_grad
    squares = sum(total(v * v) for v in (raw, offset, lift_raw, lifted_grad, style_raw, row))
    entries = TAPS * C * C + C + lift_raw.size + lifted_grad.size + style_raw.size + C
    factor = jnp.minimum(1.0, lax.rsqrt(squares / entries + clip_eps))
    raw = raw * factor
    for t in range(TAPS):
        kernel_out[t] = raw[:, C * t : C * t + C]
    offset_out[...] = offset * factor
    lift_out[...] = lift_raw * factor
    bias_out[...] = lifted_grad * factor
    style_out[...] = style_raw * factor
    sbias_out[...] = row * factor


def shifts(axis):
    n = lax.axis_size(axis)
    ahead = [(i, (i + 1) % n) for i in range(n)]
    return ahead, [(j, i) for i, j in ahead]


def summed(sums, first):
    flat = ("ghi", "gy", "gz")
    parts = lax.all_to_all(sums.reshape(32, 8, 128), flat, 0, 0, tiled=True)
    (spread,) = call(total_kernel, [shape(16, 8, 128, dtype=f32)], 1, limit=4)(parts)
    parts = lax.all_to_all(spread, "glong", 0, 0, tiled=True)
    (spread,) = call(total_kernel, [shape(32, 8, 128, dtype=f32)], 2, limit=4)(parts, first)
    return lax.all_to_all(spread, flat, 0, 0, tiled=True).reshape(256, 128)


def body(
    field, cotangent, cosmology, lift_weight, lift_bias, style_weight, style_bias, kernel, offset
):
    low, high, mid = pl.pallas_call(
        split_kernel,
        out_shape=[shape(3, 8, C, 128), shape(3, 8, C, 128), shape(1, 8, C, 128)],
        in_specs=[pl.BlockSpec(memory_space=pltpu.HBM)] * 2,
        out_specs=[VMEM] * 3,
        scratch_shapes=[
            pltpu.VMEM((C, 3, 8, 128), bf16), pltpu.VMEM((C, 3, 8, 128), bf16), pltpu.SemaphoreType.DMA((2,)),
        ],
        compiler_params=pltpu.CompilerParams(vmem_limit_bytes=4 * 1024 * 1024),
    )(*(pltpu.with_memory_space_constraint(block, pltpu.HBM) for block in (field, cotangent)))
    ahead, back = shifts(("glong", "ghi"))
    left = lax.ppermute(high, ("glong", "ghi"), ahead)
    right = lax.ppermute(low, ("glong", "ghi"), back)

    taps = jnp.transpose(kernel, (2, 3, 4, 0, 1)).reshape(TAPS, C, C)
    fwd, bwd, packed, modded, styles, inv_norm, lifted, hidden, params, column, place = call(
        modulate_kernel,
        [
            shape(3 * C, 9 * C), shape(3 * C, 9 * C), shape(C, 896, dtype=f32), shape(C, 896, dtype=f32),
            shape(1, 896, dtype=f32), shape(C, 1, dtype=f32), shape(1, 256, dtype=f32), shape(1, 256, dtype=f32),
            shape(2, 1, dtype=f32), shape(C, 1, dtype=f32), shape(144, 14 * 128),
        ],
        7,
        limit=8,
    )(
        cosmology[None, :], lift_weight, lift_bias[None, :], style_weight.T, style_bias[None, :], taps,
        offset[None, :],
    )

    rows = (low, high, mid, left, right)
    up, down = call(pack_kernel, [shape(19, C, 128), shape(19, C, 128)], 6, limit=8)(*rows, column)
    ahead, back = shifts("gy")
    up = lax.ppermute(up, "gy", ahead)
    down = lax.ppermute(down, "gy", back)

    field_rows, cot_rows, faces = call(
        gather_kernel, [shape(12, 8, C, 128), shape(10, 8, C, 128), shape(4, 48, 256)], 7
    )(*rows, up, down)
    faces = lax.all_to_all(faces, "gz", 0, 0, tiled=True)

    sums, upstream, rim = call(
        conv_kernel,
        [shape(256, 128, dtype=f32), shape(5, C, OUT), shape(5, C, 128)],
        6,
        flops=540_000_000,
        scratch=[
            pltpu.VMEM((8 * C, 12 * 128), bf16),
            pltpu.VMEM((3, 7, C, 12 * 128), bf16),
            pltpu.VMEM((9, 8 * C, 128), bf16),
            pltpu.VMEM((5, C, OUT), f32),
        ],
    )(field_rows, cot_rows, faces, fwd, column, place)
    grad_field, done = call(
        grad_kernel_body,
        [shape(C, 3, 8, 128), shape(8, 128, dtype=f32)],
        3,
        flops=170_000_000,
        scratch=[pltpu.VMEM((3, 5, C, OUT), bf16), pltpu.VMEM((3, C, OWN), f32)],
    )(upstream, rim, bwd)

    kernel_out, grad_offset, grad_lift, grad_liftbias, grad_style, grad_stylebias = call(
        tail_kernel,
        [
            shape(TAPS, C, C, dtype=f32), shape(1, C, dtype=f32), shape(2, 256, dtype=f32),
            shape(1, 256, dtype=f32), shape(C, 256, dtype=f32), shape(1, C, dtype=f32),
        ],
        9,
        limit=8,
    )(
        summed(sums, done), packed, modded, styles, inv_norm, lifted, hidden, style_weight.T, params,
    )
    grad_kernel = jnp.transpose(kernel_out.reshape(3, 3, 3, C, C), (3, 4, 0, 1, 2))
    return (
        grad_field, grad_kernel, grad_offset[0], grad_lift, grad_liftbias[0], grad_style.T, grad_stylebias[0],
    )


def solution(mesh):
    cut = Mesh(mesh.devices.reshape(16, 2, 4, 4), ("glong", "ghi", "gy", "gz"))
    grid = P(None, ("glong", "ghi"), "gy", "gz")
    return jax.shard_map(
        body, mesh=cut, in_specs=(grid,) * 2 + (P(),) * 7, out_specs=(grid,) + (P(),) * 6, check_vma=False
    )
```

```python
import numpy as np
import jax
import jax.numpy as jnp
from jax import lax
from jax.experimental import pallas as pl
from jax.experimental.pallas import tpu as pltpu
from jax.sharding import Mesh, PartitionSpec as P

demod_eps = 1e-06
clip_eps = 1e-06

C = 32
TAPS = 27
EDGE = 6
FIELD_LANES = 12 * 8 * C
COT_LANES = 10 * 8 * C
OWN = 8 * 128
WITH_RIM = 9 * 128
f32 = jnp.float32
bf16 = jnp.bfloat16
VMEM = pl.BlockSpec(memory_space=pltpu.VMEM)


def call(kernel, outs, n_in, flops=0, limit=24, scratch=()):
    return pl.pallas_call(
        kernel,
        out_shape=outs,
        in_specs=[VMEM] * n_in,
        out_specs=[VMEM] * len(outs),
        scratch_shapes=list(scratch),
        cost_estimate=pl.CostEstimate(flops=flops, bytes_accessed=1 << 20, transcendentals=0),
        compiler_params=pltpu.CompilerParams(vmem_limit_bytes=limit * 1024 * 1024),
    )


def shape(*dims, dtype=bf16):
    return jax.ShapeDtypeStruct(dims, dtype)


def select(dims, row_axis, lane_axis, lanes):
    row = lax.broadcasted_iota(jnp.int32, dims, row_axis)
    lane = lax.broadcasted_iota(jnp.int32, dims, lane_axis)
    hit = jnp.zeros(dims, f32)
    for n, at in enumerate(lanes):
        if at is not None:
            hit = jnp.where((row == n) & (lane == at), 1.0, hit)
    return hit.astype(bf16)


def split_kernel(field_hbm, cot_hbm, low_ref, rest_ref, field_ref, cot_ref, sems):
    fetches = (
        pltpu.make_async_copy(field_hbm, field_ref, sems.at[0]),
        pltpu.make_async_copy(cot_hbm, cot_ref, sems.at[1]),
    )
    for fetch in fetches:
        fetch.start()
    to = lax.broadcasted_iota(jnp.int32, (256, 256), 0)
    of = lax.broadcasted_iota(jnp.int32, (256, 256), 1)
    perm = jnp.where((of & 7) * C + (of >> 3) == to, 1.0, 0.0).astype(bf16)

    def rows(ref, x):
        block = ref[:, x].astype(f32).reshape(C * 8, 128).astype(bf16)
        return jnp.dot(perm, block, preferred_element_type=f32).astype(bf16).reshape(8, C, 128)

    fetches[0].wait()
    low_ref[0], low_ref[1], rest_ref[0] = (rows(field_ref, x) for x in range(3))
    fetches[1].wait()
    low_ref[2], rest_ref[1], rest_ref[2] = (rows(cot_ref, x) for x in range(3))


def planes(low_ref, rest_ref, right_ref):
    field = ((low_ref, 0), (low_ref, 1), (rest_ref, 0), (right_ref, 0), (right_ref, 1))
    cot = ((rest_ref, 1), (rest_ref, 2), (right_ref, 2))
    return field, cot


def pack_kernel(low_ref, rest_ref, right_ref, _, down_ref):
    field, cot = planes(low_ref, rest_ref, right_ref)
    for n, (ref, at) in enumerate(field):
        down_ref[2 * n : 2 * n + 2] = ref[at, 0:2]
    for n, (ref, at) in enumerate(cot):
        down_ref[10 + n] = ref[at, 0]


def gather_kernel(low_ref, rest_ref, right_ref, down_ref, field_out, cot_out, faces_ref):
    field, cot = planes(low_ref, rest_ref, right_ref)
    field_out[...] = jnp.zeros_like(field_out)
    cot_out[...] = jnp.zeros_like(cot_out)
    for n, (ref, at) in enumerate(field):
        for y in range(10):
            field_out[y, n] = ref[at, y] if y < 8 else down_ref[2 * n + y - 8]
    for n, (ref, at) in enumerate(cot):
        for y in range(8):
            cot_out[y, n] = ref[at, y + 1] if y < 7 else down_ref[10 + n]

    def faces(lanes, rows):
        pick = select((8, 128), 0, 1, lanes)
        return lax.dot_general(
            pick, rows, (((1,), (1,)), ((), ())), preferred_element_type=f32
        )

    both = faces((126, 127, None, 0, 1, None), field_out[...].reshape(FIELD_LANES, 128))
    beside = faces((None, None, 127, None, None, 0), cot_out[...].reshape(COT_LANES, 128))
    both = jnp.concatenate([both[:, :COT_LANES] + beside, both[:, COT_LANES:]], axis=1)

    def chunk(first):
        return jnp.concatenate(
            [both[first : first + 4, y * 256 : y * 256 + 256] for y in range(12)], axis=0
        ).astype(bf16)

    me = lax.axis_index("gz")
    high = chunk(0)
    faces_ref[me] = high
    faces_ref[lax.rem(me + 1, 4)] = high
    faces_ref[lax.rem(me + 2, 4)] = jnp.zeros_like(high)
    faces_ref[lax.rem(me + 3, 4)] = chunk(3)


def silu_slope(values):
    logistic = jax.nn.sigmoid(values)
    return logistic * (1.0 + values * (1.0 - logistic))


def row_taps(ref, x, width):
    return jnp.concatenate(
        [ref[c, x, :, b * 128 : b * 128 + width] for b in range(3) for c in range(3)], axis=0
    )


def conv_kernel(
    field_ref, cot_ref, faces_ref, fwd_ref, offset_ref, place_ref,
    sums_ref, up_ref, send_ref,
    halo, shifted, edge, acc,
):
    me = lax.axis_index("gz")
    before, after = lax.rem(me + 3, 4), lax.rem(me + 1, 4)

    def across(rows, place):
        return lax.dot_general(rows, place, (((0,), (0,)), ((), ())), preferred_element_type=f32)

    sides = jnp.concatenate([faces_ref[at] for at in (before, me, after)], axis=0)
    spread = across(sides, place_ref[...])
    rim, rim_cot = spread[:, :128], spread[:, 128:256]
    halo[...] = spread[:, 256:].astype(bf16)
    lane = lax.broadcasted_iota(jnp.int32, (C, 128), 1)
    for x in range(5):
        for y in range(10):
            row = field_ref[y, x]
            at = slice(y * 128, y * 128 + 128)
            ends = halo[x * C : x * C + C, at]
            shifted[0, x, :, at] = jnp.where(lane == 0, ends, pltpu.roll(row, 1, 1))
            shifted[1, x, :, at] = row
            shifted[2, x, :, at] = jnp.where(lane == 127, ends, pltpu.roll(row, 127, 1))
        part = jnp.dot(fwd_ref[...], row_taps(shifted, x, OWN), preferred_element_type=f32)
        for a in range(3):
            if 0 <= x - a < 3:
                if a == 0:
                    acc[x] = part[:C]
                else:
                    acc[x - a] += part[a * C : a * C + C]

    for t in range(9):
        shift = (t // 3) * EDGE + t % 3
        edge[t] = (pltpu.roll(rim, 128 - shift, 1) if shift else rim).astype(bf16)
    block = jnp.concatenate(
        [jnp.concatenate([edge[t, x * C : x * C + C] for t in range(9)], axis=0) for x in range(5)], axis=1
    )
    part = jnp.dot(fwd_ref[...], block, preferred_element_type=f32)
    offset = offset_ref[...]
    rims = []
    for x in range(3):
        preact = offset + sum(
            part[a * C : a * C + C, (x + a) * 128 : (x + a) * 128 + 128] for a in range(3)
        )
        rims.append((rim_cot[x * C : x * C + C] * silu_slope(preact)).astype(bf16))

    ups = []
    for x in range(3):
        beside = jnp.concatenate([cot_ref[y, x] for y in range(8)], axis=1).astype(f32)
        upstream = (beside * silu_slope(acc[x] + offset)).astype(bf16)
        ups.append(upstream)
        up_ref[x, :, :OWN] = upstream
        up_ref[x, :, OWN:] = rims[x]
        if x:
            send_ref[x - 1, :, :OWN] = upstream
            send_ref[x - 1, :, OWN:] = rims[x]

    none = jnp.zeros((C, OWN), bf16)
    left = jnp.concatenate(
        [
            jnp.concatenate([ups[x - a] if 0 <= x - a < 3 else none for a in range(3)], axis=0)
            for x in range(5)
        ],
        axis=1,
    )
    right = jnp.concatenate([row_taps(shifted, x, OWN) for x in range(5)], axis=1)
    total = lax.dot_general(left, right, (((1,), (1,)), ((), ())), preferred_element_type=f32)

    offsets = sum(jnp.sum(ups[x].astype(f32), axis=1, keepdims=True) for x in range(3))
    packed = jnp.concatenate(
        [total[a * C : a * C + C] for a in range(3)] + [jnp.broadcast_to(offsets, (C, C))], axis=1
    )
    for s in range(4):
        for l in range(8):
            at = (s * 8 + l) * 8
            if l < 7:
                sums_ref[at : at + 8] = packed[8 * s : 8 * s + 8, 128 * l : 128 * l + 128]
            else:
                sums_ref[at : at + 8] = jnp.zeros((8, 128), f32)


def pack_up_kernel(up_ref, before_ref, last_ref):
    for x in range(5):
        ref, at = (before_ref, x) if x < 2 else (up_ref, x - 2)
        last_ref[x] = ref[at, :, 6 * 128 :]


def grad_kernel_body(up_ref, before_ref, below_ref, bwd_ref, grad_ref, shifted, acc):
    lane = lax.broadcasted_iota(jnp.int32, (C, 128), 1)
    for x in range(5):
        ref, from_x = (before_ref, x) if x < 2 else (up_ref, x - 2)
        rim = ref[from_x, :, OWN:].astype(f32)
        rim_below = below_ref[x, :, 256:].astype(f32)
        for y in range(10):
            at = slice(y * 128, y * 128 + 128)
            if y < 2:
                row = below_ref[x, :, at]
                ends, n = rim_below, (y + 6) * EDGE
            else:
                row = ref[from_x, :, (y - 2) * 128 : (y - 1) * 128]
                ends, n = rim, (y - 2) * EDGE
            low = jnp.broadcast_to(ends[:, n : n + 1], (C, 128)).astype(bf16)
            high = jnp.broadcast_to(ends[:, n + 3 : n + 4], (C, 128)).astype(bf16)
            shifted[0, x, :, at] = jnp.where(lane == 0, low, pltpu.roll(row, 1, 1))
            shifted[1, x, :, at] = row
            shifted[2, x, :, at] = jnp.where(lane == 127, high, pltpu.roll(row, 127, 1))
        part = jnp.dot(bwd_ref[...], row_taps(shifted, x, OWN), preferred_element_type=f32)
        for a in range(3):
            if 0 <= x - a < 3:
                if a == 0:
                    acc[x] = part[:C]
                else:
                    acc[x - a] += part[a * C : a * C + C]

    to = lax.broadcasted_iota(jnp.int32, (256, 256), 0)
    of = lax.broadcasted_iota(jnp.int32, (256, 256), 1)
    perm = jnp.where((to & 7) * C + (to >> 3) == of, 1.0, 0.0).astype(bf16)
    for x in range(3):
        rows = jnp.concatenate(
            [acc[x, :, y * 128 : y * 128 + 128] for y in range(8)], axis=0
        ).astype(bf16)
        moved = jnp.dot(perm, rows, preferred_element_type=f32)
        grad_ref[:, x] = moved.reshape(C, 8, 128).astype(bf16)


def identity():
    return jnp.where(
        lax.broadcasted_iota(jnp.int32, (C, C), 0) == lax.broadcasted_iota(jnp.int32, (C, C), 1), 1.0, 0.0
    )


def fill_places(place_ref):
    row = lax.broadcasted_iota(jnp.int32, (144, 128), 0)
    to = lax.broadcasted_iota(jnp.int32, (144, 128), 1)
    y, k = row >> 2, row & 3

    def place(moves):
        hit = jnp.zeros((144, 128), f32)
        for side, face, lane in moves:
            inside = (y >= side * 12) & (y < side * 12 + 12)
            hit = jnp.where(inside & (k == face) & (to == (y - side * 12) * EDGE + lane), 1.0, hit)
        return hit.astype(bf16)

    place_ref[:, :128] = place(((0, 0, 0), (0, 1, 1), (1, 3, 2), (1, 1, 3), (2, 0, 4), (2, 1, 5)))
    place_ref[:, 128:256] = place(((0, 2, 0), (2, 2, 3)))
    for n in range(12):
        ends = (to == 0) & (row == n * 4 + 1) | (to == 127) & (row == (24 + n) * 4)
        place_ref[:, 256 + n * 128 : 384 + n * 128] = jnp.where(ends, 1.0, 0.0).astype(bf16)


def modulate_kernel(
    cosmology_ref, lift_ref, bias_ref, weight_ref, sbias_ref, taps_ref, offset_ref,
    fwd_ref, bwd_ref, kernel_ref, modded_ref, styles_ref, inv_ref, lifted_ref, hidden_ref, params_ref, column_ref,
    place_ref,
):
    fill_places(place_ref)
    first, second = cosmology_ref[:, 0:1], cosmology_ref[:, 1:2]
    lifted = first * lift_ref[0:1] + second * lift_ref[1:2] + bias_ref[...]
    hidden = lifted * jax.nn.sigmoid(lifted)
    eye = identity()
    column = jnp.sum(weight_ref[...] * hidden, axis=1, keepdims=True)
    styles = jnp.sum(column * eye, axis=0, keepdims=True) + sbias_ref[...] + 1.0
    kernel = jnp.concatenate([taps_ref[t] for t in range(TAPS)] + [jnp.zeros((C, C), f32)], axis=1)
    styles = jnp.concatenate([styles] * TAPS + [jnp.zeros((1, C), f32)], axis=1)
    modded = kernel * styles
    inv = lax.rsqrt(jnp.sum(modded * modded, axis=1, keepdims=True) + demod_eps)
    scaled = (modded * inv).astype(bf16)
    for a in range(3):
        fwd_ref[a * C : a * C + C] = scaled[:, a * 288 : a * 288 + 288]
    turned = scaled.astype(f32).T
    for a in range(3):
        bwd_ref[a * C : a * C + C] = jnp.concatenate(
            [turned[(26 - a * 9 - t) * C : (27 - a * 9 - t) * C] for t in range(9)], axis=1
        ).astype(bf16)
    kernel_ref[...] = kernel
    modded_ref[...] = modded
    styles_ref[...] = styles
    inv_ref[...] = inv
    lifted_ref[...] = lifted
    hidden_ref[...] = hidden
    params_ref[...] = jnp.concatenate([first, second], axis=0)
    column_ref[...] = jnp.sum(offset_ref[...] * eye, axis=1, keepdims=True)


def total_kernel(parts_ref, spread_ref):
    part = jnp.sum(parts_ref[...], axis=0)
    for n in range(spread_ref.shape[0]):
        spread_ref[n] = part


def tail_kernel(
    sums_ref, kernel_ref, modded_ref, styles_ref, inv_ref, lifted_ref, hidden_ref, weight_ref, cosmology_ref,
    kernel_out, offset_out, lift_out, bias_out, style_out, sbias_out,
):
    def total(values):
        return jnp.sum(jnp.sum(values, axis=1, keepdims=True), axis=0, keepdims=True)

    sums = jnp.concatenate(
        [
            jnp.concatenate([sums_ref[(s * 8 + l) * 8 : (s * 8 + l) * 8 + 8] for s in range(4)], axis=0)
            for l in range(7)
        ],
        axis=1,
    )
    kernel, modded, styles, inv = kernel_ref[...], modded_ref[...], styles_ref[...], inv_ref[...]
    eye = identity()
    offset = jnp.sum(sums[:, TAPS * C : TAPS * C + C] * eye, axis=0, keepdims=True)
    projected = jnp.sum(sums * modded, axis=1, keepdims=True)
    mod_grad = inv * (sums - modded * (inv * inv * projected))
    raw = mod_grad * styles
    lanes = jnp.sum(mod_grad * kernel, axis=0, keepdims=True)
    folded = sum(lanes[:, 128 * l : 128 * l + 128] for l in range(7))
    row = sum(folded[:, C * n : C * n + C] for n in range(4))
    column = jnp.sum(row * eye, axis=1, keepdims=True)
    lifted_grad = jnp.sum(weight_ref[...] * column, axis=0, keepdims=True) * silu_slope(lifted_ref[...])
    style_raw = column * hidden_ref[...]
    lift_raw = cosmology_ref[...] * lifted_grad
    squares = sum(total(v * v) for v in (raw, offset, lift_raw, lifted_grad, style_raw, row))
    entries = TAPS * C * C + C + lift_raw.size + lifted_grad.size + style_raw.size + C
    factor = jnp.minimum(1.0, lax.rsqrt(squares / entries + clip_eps))
    raw = raw * factor
    for t in range(TAPS):
        kernel_out[t] = raw[:, C * t : C * t + C]
    offset_out[...] = offset * factor
    lift_out[...] = lift_raw * factor
    bias_out[...] = lifted_grad * factor
    style_out[...] = style_raw * factor
    sbias_out[...] = row * factor


def shifts(axis):
    n = lax.axis_size(axis)
    ahead = [(i, (i + 1) % n) for i in range(n)]
    return ahead, [(j, i) for i, j in ahead]


def summed(sums):
    flat = ("ghi", "gy", "gz")
    parts = lax.all_to_all(sums.reshape(32, 8, 128), flat, 0, 0, tiled=True)
    (spread,) = call(total_kernel, [shape(16, 8, 128, dtype=f32)], 1, limit=4)(parts)
    parts = lax.all_to_all(spread, "glong", 0, 0, tiled=True)
    (spread,) = call(total_kernel, [shape(32, 8, 128, dtype=f32)], 1, limit=4)(parts)
    return lax.all_to_all(spread, flat, 0, 0, tiled=True).reshape(256, 128)


def body(
    field, cotangent, cosmology, lift_weight, lift_bias, style_weight, style_bias, kernel, offset
):
    low, rest = pl.pallas_call(
        split_kernel,
        out_shape=[shape(3, 8, C, 128), shape(3, 8, C, 128)],
        in_specs=[pl.BlockSpec(memory_space=pltpu.HBM)] * 2,
        out_specs=[VMEM] * 2,
        scratch_shapes=[
            pltpu.VMEM((C, 3, 8, 128), bf16), pltpu.VMEM((C, 3, 8, 128), bf16), pltpu.SemaphoreType.DMA((2,)),
        ],
        compiler_params=pltpu.CompilerParams(vmem_limit_bytes=4 * 1024 * 1024),
    )(*(pltpu.with_memory_space_constraint(block, pltpu.HBM) for block in (field, cotangent)))
    x_ahead, back = shifts(("glong", "ghi"))
    right = lax.ppermute(low, ("glong", "ghi"), back)

    taps = jnp.transpose(kernel, (2, 3, 4, 0, 1)).reshape(TAPS, C, C)
    fwd, bwd, packed, modded, styles, inv_norm, lifted, hidden, params, column, place = call(
        modulate_kernel,
        [
            shape(3 * C, 9 * C), shape(3 * C, 9 * C), shape(C, 896, dtype=f32), shape(C, 896, dtype=f32),
            shape(1, 896, dtype=f32), shape(C, 1, dtype=f32), shape(1, 256, dtype=f32), shape(1, 256, dtype=f32),
            shape(2, 1, dtype=f32), shape(C, 1, dtype=f32), shape(144, 14 * 128),
        ],
        7,
        limit=8,
    )(
        cosmology[None, :], lift_weight, lift_bias[None, :], style_weight.T, style_bias[None, :], taps,
        offset[None, :],
    )

    rows = (low, rest, right)
    (down,) = call(pack_kernel, [shape(13, C, 128)], 4, limit=8)(*rows, column)
    y_ahead, back = shifts("gy")
    down = lax.ppermute(down, "gy", back)

    field_rows, cot_rows, faces = call(
        gather_kernel, [shape(12, 8, C, 128), shape(10, 8, C, 128), shape(4, 48, 256)], 4
    )(*rows, down)
    faces = lax.all_to_all(faces, "gz", 0, 0, tiled=True)

    sums, upstream, send = call(
        conv_kernel,
        [shape(256, 128, dtype=f32), shape(3, C, WITH_RIM), shape(2, C, WITH_RIM)],
        6,
        flops=540_000_000,
        scratch=[
            pltpu.VMEM((8 * C, 12 * 128), bf16),
            pltpu.VMEM((3, 5, C, 10 * 128), bf16),
            pltpu.VMEM((9, 8 * C, 128), bf16),
            pltpu.VMEM((3, C, OWN), f32),
        ],
    )(field_rows, cot_rows, faces, fwd, column, place)
    before = lax.ppermute(send, ("glong", "ghi"), x_ahead)
    (last,) = call(pack_up_kernel, [shape(5, C, 3 * 128)], 2, limit=4)(upstream, before)
    below = lax.ppermute(last, "gy", y_ahead)
    (grad_field,) = call(
        grad_kernel_body,
        [shape(C, 3, 8, 128)],
        4,
        flops=170_000_000,
        scratch=[pltpu.VMEM((3, 5, C, 10 * 128), bf16), pltpu.VMEM((3, C, OWN), f32)],
    )(upstream, before, below, bwd)

    kernel_out, grad_offset, grad_lift, grad_liftbias, grad_style, grad_stylebias = call(
        tail_kernel,
        [
            shape(TAPS, C, C, dtype=f32), shape(1, C, dtype=f32), shape(2, 256, dtype=f32),
            shape(1, 256, dtype=f32), shape(C, 256, dtype=f32), shape(1, C, dtype=f32),
        ],
        9,
        limit=8,
    )(
        summed(sums), packed, modded, styles, inv_norm, lifted, hidden, style_weight.T, params,
    )
    grad_kernel = jnp.transpose(kernel_out.reshape(3, 3, 3, C, C), (3, 4, 0, 1, 2))
    return (
        grad_field, grad_kernel, grad_offset[0], grad_lift, grad_liftbias[0], grad_style.T, grad_stylebias[0],
    )


def solution(mesh):
    cut = Mesh(mesh.devices.reshape(16, 2, 4, 4), ("glong", "ghi", "gy", "gz"))
    grid = P(None, ("glong", "ghi"), "gy", "gz")
    return jax.shard_map(
        body, mesh=cut, in_specs=(grid,) * 2 + (P(),) * 7, out_specs=(grid,) + (P(),) * 6, check_vma=False
    )
```

```python
import numpy as np
import jax
import jax.numpy as jnp
from jax import lax
from jax.experimental import pallas as pl
from jax.experimental.pallas import tpu as pltpu
from jax.sharding import Mesh, PartitionSpec as P

demod_eps = 1e-06
clip_eps = 1e-06

C = 32
TAPS = 27
EDGE = 6
FIELD_LANES = 12 * 8 * C
COT_LANES = 10 * 8 * C
OWN = 8 * 128
WITH_RIM = 9 * 128
f32 = jnp.float32
bf16 = jnp.bfloat16
VMEM = pl.BlockSpec(memory_space=pltpu.VMEM)


def call(kernel, outs, n_in, flops=0, limit=24, scratch=()):
    return pl.pallas_call(
        kernel,
        out_shape=outs,
        in_specs=[VMEM] * n_in,
        out_specs=[VMEM] * len(outs),
        scratch_shapes=list(scratch),
        cost_estimate=pl.CostEstimate(flops=flops, bytes_accessed=1 << 20, transcendentals=0),
        compiler_params=pltpu.CompilerParams(vmem_limit_bytes=limit * 1024 * 1024),
    )


def shape(*dims, dtype=bf16):
    return jax.ShapeDtypeStruct(dims, dtype)


def select(dims, row_axis, lane_axis, lanes):
    row = lax.broadcasted_iota(jnp.int32, dims, row_axis)
    lane = lax.broadcasted_iota(jnp.int32, dims, lane_axis)
    hit = jnp.zeros(dims, f32)
    for n, at in enumerate(lanes):
        if at is not None:
            hit = jnp.where((row == n) & (lane == at), 1.0, hit)
    return hit.astype(bf16)


def split_kernel(field_hbm, cot_hbm, low_ref, rest_ref, row_ref, corner_ref, field_ref, cot_ref, sems):
    fetches = (
        pltpu.make_async_copy(field_hbm, field_ref, sems.at[0]),
        pltpu.make_async_copy(cot_hbm, cot_ref, sems.at[1]),
    )
    for fetch in fetches:
        fetch.start()
    to = lax.broadcasted_iota(jnp.int32, (256, 256), 0)
    of = lax.broadcasted_iota(jnp.int32, (256, 256), 1)
    perm = jnp.where((of & 7) * C + (of >> 3) == to, 1.0, 0.0).astype(bf16)

    def rows(ref, x):
        block = ref[:, x].astype(f32).reshape(C * 8, 128).astype(bf16)
        return jnp.dot(perm, block, preferred_element_type=f32).astype(bf16).reshape(8, C, 128)

    fetches[0].wait()
    low_ref[0], low_ref[1], rest_ref[0] = (rows(field_ref, x) for x in range(3))
    fetches[1].wait()
    low_ref[2], rest_ref[1], rest_ref[2] = (rows(cot_ref, x) for x in range(3))
    for n, (ref, at) in enumerate(((low_ref, 0), (low_ref, 1), (rest_ref, 0))):
        row_ref[2 * n : 2 * n + 2] = ref[at, 0:2]
    row_ref[6], row_ref[7] = rest_ref[1, 0], rest_ref[2, 0]
    corner_ref[0:2], corner_ref[2:4], corner_ref[4] = low_ref[0, 0:2], low_ref[1, 0:2], low_ref[2, 0]


def planes(low_ref, rest_ref, right_ref):
    field = ((low_ref, 0), (low_ref, 1), (rest_ref, 0), (right_ref, 0), (right_ref, 1))
    cot = ((rest_ref, 1), (rest_ref, 2), (right_ref, 2))
    return field, cot


def gather_kernel(low_ref, rest_ref, right_ref, row_ref, corner_ref, _, field_out, cot_out, faces_ref):
    field, cot = planes(low_ref, rest_ref, right_ref)
    field_out[...] = jnp.zeros_like(field_out)
    cot_out[...] = jnp.zeros_like(cot_out)
    for n, (ref, at) in enumerate(field):
        for y in range(10):
            if y < 8:
                field_out[y, n] = ref[at, y]
            elif n < 3:
                field_out[y, n] = row_ref[2 * n + y - 8]
            else:
                field_out[y, n] = corner_ref[2 * (n - 3) + y - 8]
    for n, (ref, at) in enumerate(cot):
        for y in range(8):
            if y < 7:
                cot_out[y, n] = ref[at, y + 1]
            else:
                cot_out[y, n] = row_ref[6 + n] if n < 2 else corner_ref[4]

    def faces(lanes, rows):
        pick = select((8, 128), 0, 1, lanes)
        return lax.dot_general(
            pick, rows, (((1,), (1,)), ((), ())), preferred_element_type=f32
        )

    both = faces((126, 127, None, 0, 1, None), field_out[...].reshape(FIELD_LANES, 128))
    beside = faces((None, None, 127, None, None, 0), cot_out[...].reshape(COT_LANES, 128))
    both = jnp.concatenate([both[:, :COT_LANES] + beside, both[:, COT_LANES:]], axis=1)

    def chunk(first):
        return jnp.concatenate(
            [both[first : first + 4, y * 256 : y * 256 + 256] for y in range(12)], axis=0
        ).astype(bf16)

    me = lax.axis_index("gz")
    high = chunk(0)
    faces_ref[me] = high
    faces_ref[lax.rem(me + 1, 4)] = high
    faces_ref[lax.rem(me + 2, 4)] = jnp.zeros_like(high)
    faces_ref[lax.rem(me + 3, 4)] = chunk(3)


def silu_slope(values):
    logistic = jax.nn.sigmoid(values)
    return logistic * (1.0 + values * (1.0 - logistic))


def row_taps(ref, x, width):
    return jnp.concatenate(
        [ref[c, x, :, b * 128 : b * 128 + width] for b in range(3) for c in range(3)], axis=0
    )


def conv_kernel(
    field_ref, cot_ref, faces_ref, fwd_ref, offset_ref, place_ref,
    sums_ref, up_ref, send_ref,
    halo, shifted, edge, acc,
):
    me = lax.axis_index("gz")
    before, after = lax.rem(me + 3, 4), lax.rem(me + 1, 4)

    def across(rows, place):
        return lax.dot_general(rows, place, (((0,), (0,)), ((), ())), preferred_element_type=f32)

    sides = jnp.concatenate([faces_ref[at] for at in (before, me, after)], axis=0)
    spread = across(sides, place_ref[...])
    rim, rim_cot = spread[:, :128], spread[:, 128:256]
    halo[...] = spread[:, 256:].astype(bf16)
    lane = lax.broadcasted_iota(jnp.int32, (C, 128), 1)
    for x in range(5):
        for y in range(10):
            row = field_ref[y, x]
            at = slice(y * 128, y * 128 + 128)
            ends = halo[x * C : x * C + C, at]
            shifted[0, x, :, at] = jnp.where(lane == 0, ends, pltpu.roll(row, 1, 1))
            shifted[1, x, :, at] = row
            shifted[2, x, :, at] = jnp.where(lane == 127, ends, pltpu.roll(row, 127, 1))
        part = jnp.dot(fwd_ref[...], row_taps(shifted, x, OWN), preferred_element_type=f32)
        for a in range(3):
            if 0 <= x - a < 3:
                if a == 0:
                    acc[x] = part[:C]
                else:
                    acc[x - a] += part[a * C : a * C + C]

    for t in range(9):
        shift = (t // 3) * EDGE + t % 3
        edge[t] = (pltpu.roll(rim, 128 - shift, 1) if shift else rim).astype(bf16)
    block = jnp.concatenate(
        [jnp.concatenate([edge[t, x * C : x * C + C] for t in range(9)], axis=0) for x in range(5)], axis=1
    )
    part = jnp.dot(fwd_ref[...], block, preferred_element_type=f32)
    offset = offset_ref[...]
    rims = []
    for x in range(3):
        preact = offset + sum(
            part[a * C : a * C + C, (x + a) * 128 : (x + a) * 128 + 128] for a in range(3)
        )
        rims.append((rim_cot[x * C : x * C + C] * silu_slope(preact)).astype(bf16))

    ups = []
    for x in range(3):
        beside = jnp.concatenate([cot_ref[y, x] for y in range(8)], axis=1).astype(f32)
        upstream = (beside * silu_slope(acc[x] + offset)).astype(bf16)
        ups.append(upstream)
        up_ref[x, :, :OWN] = upstream
        up_ref[x, :, OWN:] = rims[x]
        if x:
            send_ref[x - 1, :, :OWN] = upstream
            send_ref[x - 1, :, OWN:] = rims[x]

    none = jnp.zeros((C, OWN), bf16)
    left = jnp.concatenate(
        [
            jnp.concatenate([ups[x - a] if 0 <= x - a < 3 else none for a in range(3)], axis=0)
            for x in range(5)
        ],
        axis=1,
    )
    right = jnp.concatenate([row_taps(shifted, x, OWN) for x in range(5)], axis=1)
    total = lax.dot_general(left, right, (((1,), (1,)), ((), ())), preferred_element_type=f32)

    offsets = sum(jnp.sum(ups[x].astype(f32), axis=1, keepdims=True) for x in range(3))
    packed = jnp.concatenate(
        [total[a * C : a * C + C] for a in range(3)] + [jnp.broadcast_to(offsets, (C, C))], axis=1
    )
    for s in range(4):
        for l in range(8):
            at = (s * 8 + l) * 8
            if l < 7:
                sums_ref[at : at + 8] = packed[8 * s : 8 * s + 8, 128 * l : 128 * l + 128]
            else:
                sums_ref[at : at + 8] = jnp.zeros((8, 128), f32)


def pack_up_kernel(up_ref, before_ref, last_ref):
    for x in range(5):
        ref, at = (before_ref, x) if x < 2 else (up_ref, x - 2)
        last_ref[x] = ref[at, :, 6 * 128 :]


def grad_kernel_body(up_ref, before_ref, below_ref, bwd_ref, grad_ref, shifted, acc):
    lane = lax.broadcasted_iota(jnp.int32, (C, 128), 1)
    for x in range(5):
        ref, from_x = (before_ref, x) if x < 2 else (up_ref, x - 2)
        rim = ref[from_x, :, OWN:].astype(f32)
        rim_below = below_ref[x, :, 256:].astype(f32)
        for y in range(10):
            at = slice(y * 128, y * 128 + 128)
            if y < 2:
                row = below_ref[x, :, at]
                ends, n = rim_below, (y + 6) * EDGE
            else:
                row = ref[from_x, :, (y - 2) * 128 : (y - 1) * 128]
                ends, n = rim, (y - 2) * EDGE
            low = jnp.broadcast_to(ends[:, n : n + 1], (C, 128)).astype(bf16)
            high = jnp.broadcast_to(ends[:, n + 3 : n + 4], (C, 128)).astype(bf16)
            shifted[0, x, :, at] = jnp.where(lane == 0, low, pltpu.roll(row, 1, 1))
            shifted[1, x, :, at] = row
            shifted[2, x, :, at] = jnp.where(lane == 127, high, pltpu.roll(row, 127, 1))
        part = jnp.dot(bwd_ref[...], row_taps(shifted, x, OWN), preferred_element_type=f32)
        for a in range(3):
            if 0 <= x - a < 3:
                if a == 0:
                    acc[x] = part[:C]
                else:
                    acc[x - a] += part[a * C : a * C + C]

    to = lax.broadcasted_iota(jnp.int32, (256, 256), 0)
    of = lax.broadcasted_iota(jnp.int32, (256, 256), 1)
    perm = jnp.where((to & 7) * C + (to >> 3) == of, 1.0, 0.0).astype(bf16)
    for x in range(3):
        rows = jnp.concatenate(
            [acc[x, :, y * 128 : y * 128 + 128] for y in range(8)], axis=0
        ).astype(bf16)
        moved = jnp.dot(perm, rows, preferred_element_type=f32)
        grad_ref[:, x] = moved.reshape(C, 8, 128).astype(bf16)


def identity():
    return jnp.where(
        lax.broadcasted_iota(jnp.int32, (C, C), 0) == lax.broadcasted_iota(jnp.int32, (C, C), 1), 1.0, 0.0
    )


def fill_places(place_ref):
    row = lax.broadcasted_iota(jnp.int32, (144, 128), 0)
    to = lax.broadcasted_iota(jnp.int32, (144, 128), 1)
    y, k = row >> 2, row & 3

    def place(moves):
        hit = jnp.zeros((144, 128), f32)
        for side, face, lane in moves:
            inside = (y >= side * 12) & (y < side * 12 + 12)
            hit = jnp.where(inside & (k == face) & (to == (y - side * 12) * EDGE + lane), 1.0, hit)
        return hit.astype(bf16)

    place_ref[:, :128] = place(((0, 0, 0), (0, 1, 1), (1, 3, 2), (1, 1, 3), (2, 0, 4), (2, 1, 5)))
    place_ref[:, 128:256] = place(((0, 2, 0), (2, 2, 3)))
    for n in range(12):
        ends = (to == 0) & (row == n * 4 + 1) | (to == 127) & (row == (24 + n) * 4)
        place_ref[:, 256 + n * 128 : 384 + n * 128] = jnp.where(ends, 1.0, 0.0).astype(bf16)


def modulate_kernel(
    cosmology_ref, lift_ref, bias_ref, weight_ref, sbias_ref, taps_ref, offset_ref,
    fwd_ref, bwd_ref, kernel_ref, modded_ref, styles_ref, inv_ref, lifted_ref, hidden_ref, params_ref, column_ref,
    place_ref,
):
    fill_places(place_ref)
    first, second = cosmology_ref[:, 0:1], cosmology_ref[:, 1:2]
    lifted = first * lift_ref[0:1] + second * lift_ref[1:2] + bias_ref[...]
    hidden = lifted * jax.nn.sigmoid(lifted)
    eye = identity()
    column = jnp.sum(weight_ref[...] * hidden, axis=1, keepdims=True)
    styles = jnp.sum(column * eye, axis=0, keepdims=True) + sbias_ref[...] + 1.0
    kernel = jnp.concatenate([taps_ref[t] for t in range(TAPS)] + [jnp.zeros((C, C), f32)], axis=1)
    styles = jnp.concatenate([styles] * TAPS + [jnp.zeros((1, C), f32)], axis=1)
    modded = kernel * styles
    inv = lax.rsqrt(jnp.sum(modded * modded, axis=1, keepdims=True) + demod_eps)
    scaled = (modded * inv).astype(bf16)
    for a in range(3):
        fwd_ref[a * C : a * C + C] = scaled[:, a * 288 : a * 288 + 288]
    turned = scaled.astype(f32).T
    for a in range(3):
        bwd_ref[a * C : a * C + C] = jnp.concatenate(
            [turned[(26 - a * 9 - t) * C : (27 - a * 9 - t) * C] for t in range(9)], axis=1
        ).astype(bf16)
    kernel_ref[...] = kernel
    modded_ref[...] = modded
    styles_ref[...] = styles
    inv_ref[...] = inv
    lifted_ref[...] = lifted
    hidden_ref[...] = hidden
    params_ref[...] = jnp.concatenate([first, second], axis=0)
    column_ref[...] = jnp.sum(offset_ref[...] * eye, axis=1, keepdims=True)


def total_kernel(parts_ref, spread_ref):
    part = jnp.sum(parts_ref[...], axis=0)
    for n in range(spread_ref.shape[0]):
        spread_ref[n] = part


def tail_kernel(
    sums_ref, kernel_ref, modded_ref, styles_ref, inv_ref, lifted_ref, hidden_ref, weight_ref, cosmology_ref,
    kernel_out, offset_out, lift_out, bias_out, style_out, sbias_out,
):
    def total(values):
        return jnp.sum(jnp.sum(values, axis=1, keepdims=True), axis=0, keepdims=True)

    sums = jnp.concatenate(
        [
            jnp.concatenate([sums_ref[(s * 8 + l) * 8 : (s * 8 + l) * 8 + 8] for s in range(4)], axis=0)
            for l in range(7)
        ],
        axis=1,
    )
    kernel, modded, styles, inv = kernel_ref[...], modded_ref[...], styles_ref[...], inv_ref[...]
    eye = identity()
    offset = jnp.sum(sums[:, TAPS * C : TAPS * C + C] * eye, axis=0, keepdims=True)
    projected = jnp.sum(sums * modded, axis=1, keepdims=True)
    mod_grad = inv * (sums - modded * (inv * inv * projected))
    raw = mod_grad * styles
    lanes = jnp.sum(mod_grad * kernel, axis=0, keepdims=True)
    folded = sum(lanes[:, 128 * l : 128 * l + 128] for l in range(7))
    row = sum(folded[:, C * n : C * n + C] for n in range(4))
    column = jnp.sum(row * eye, axis=1, keepdims=True)
    lifted_grad = jnp.sum(weight_ref[...] * column, axis=0, keepdims=True) * silu_slope(lifted_ref[...])
    style_raw = column * hidden_ref[...]
    lift_raw = cosmology_ref[...] * lifted_grad
    squares = sum(total(v * v) for v in (raw, offset, lift_raw, lifted_grad, style_raw, row))
    entries = TAPS * C * C + C + lift_raw.size + lifted_grad.size + style_raw.size + C
    factor = jnp.minimum(1.0, lax.rsqrt(squares / entries + clip_eps))
    raw = raw * factor
    for t in range(TAPS):
        kernel_out[t] = raw[:, C * t : C * t + C]
    offset_out[...] = offset * factor
    lift_out[...] = lift_raw * factor
    bias_out[...] = lifted_grad * factor
    style_out[...] = style_raw * factor
    sbias_out[...] = row * factor


def shifts(axis):
    n = lax.axis_size(axis)
    ahead = [(i, (i + 1) % n) for i in range(n)]
    return ahead, [(j, i) for i, j in ahead]


def summed(sums):
    flat = ("ghi", "gy", "gz")
    parts = lax.all_to_all(sums.reshape(32, 8, 128), flat, 0, 0, tiled=True)
    (spread,) = call(total_kernel, [shape(16, 8, 128, dtype=f32)], 1, limit=4)(parts)
    parts = lax.all_to_all(spread, "glong", 0, 0, tiled=True)
    (spread,) = call(total_kernel, [shape(32, 8, 128, dtype=f32)], 1, limit=4)(parts)
    return lax.all_to_all(spread, flat, 0, 0, tiled=True).reshape(256, 128)


def body(
    field, cotangent, cosmology, lift_weight, lift_bias, style_weight, style_bias, kernel, offset
):
    low, rest, row, corner = pl.pallas_call(
        split_kernel,
        out_shape=[shape(3, 8, C, 128), shape(3, 8, C, 128), shape(8, C, 128), shape(5, C, 128)],
        in_specs=[pl.BlockSpec(memory_space=pltpu.HBM)] * 2,
        out_specs=[VMEM] * 4,
        scratch_shapes=[
            pltpu.VMEM((C, 3, 8, 128), bf16), pltpu.VMEM((C, 3, 8, 128), bf16), pltpu.SemaphoreType.DMA((2,)),
        ],
        compiler_params=pltpu.CompilerParams(vmem_limit_bytes=4 * 1024 * 1024),
    )(*(pltpu.with_memory_space_constraint(block, pltpu.HBM) for block in (field, cotangent)))
    x_ahead, back = shifts(("glong", "ghi"))
    right = lax.ppermute(low, ("glong", "ghi"), back)

    taps = jnp.transpose(kernel, (2, 3, 4, 0, 1)).reshape(TAPS, C, C)
    fwd, bwd, packed, modded, styles, inv_norm, lifted, hidden, params, column, place = call(
        modulate_kernel,
        [
            shape(3 * C, 9 * C), shape(3 * C, 9 * C), shape(C, 896, dtype=f32), shape(C, 896, dtype=f32),
            shape(1, 896, dtype=f32), shape(C, 1, dtype=f32), shape(1, 256, dtype=f32), shape(1, 256, dtype=f32),
            shape(2, 1, dtype=f32), shape(C, 1, dtype=f32), shape(144, 14 * 128),
        ],
        7,
        limit=8,
    )(
        cosmology[None, :], lift_weight, lift_bias[None, :], style_weight.T, style_bias[None, :], taps,
        offset[None, :],
    )

    diagonal = [(4 * i + j, 4 * ((i + 31) % 32) + (j + 3) % 4) for i in range(32) for j in range(4)]
    corner = lax.ppermute(corner, ("glong", "ghi", "gy"), diagonal)
    y_ahead, back = shifts("gy")
    row = lax.ppermute(row, "gy", back)

    field_rows, cot_rows, faces = call(
        gather_kernel, [shape(12, 8, C, 128), shape(10, 8, C, 128), shape(4, 48, 256)], 6
    )(low, rest, right, row, corner, column)
    faces = lax.all_to_all(faces, "gz", 0, 0, tiled=True)

    sums, upstream, send = call(
        conv_kernel,
        [shape(256, 128, dtype=f32), shape(3, C, WITH_RIM), shape(2, C, WITH_RIM)],
        6,
        flops=540_000_000,
        scratch=[
            pltpu.VMEM((8 * C, 12 * 128), bf16),
            pltpu.VMEM((3, 5, C, 10 * 128), bf16),
            pltpu.VMEM((9, 8 * C, 128), bf16),
            pltpu.VMEM((3, C, OWN), f32),
        ],
    )(field_rows, cot_rows, faces, fwd, column, place)
    before = lax.ppermute(send, ("glong", "ghi"), x_ahead)
    (last,) = call(pack_up_kernel, [shape(5, C, 3 * 128)], 2, limit=4)(upstream, before)
    below = lax.ppermute(last, "gy", y_ahead)
    (grad_field,) = call(
        grad_kernel_body,
        [shape(C, 3, 8, 128)],
        4,
        flops=170_000_000,
        scratch=[pltpu.VMEM((3, 5, C, 10 * 128), bf16), pltpu.VMEM((3, C, OWN), f32)],
    )(upstream, before, below, bwd)

    kernel_out, grad_offset, grad_lift, grad_liftbias, grad_style, grad_stylebias = call(
        tail_kernel,
        [
            shape(TAPS, C, C, dtype=f32), shape(1, C, dtype=f32), shape(2, 256, dtype=f32),
            shape(1, 256, dtype=f32), shape(C, 256, dtype=f32), shape(1, C, dtype=f32),
        ],
        9,
        limit=8,
    )(
        summed(sums), packed, modded, styles, inv_norm, lifted, hidden, style_weight.T, params,
    )
    grad_kernel = jnp.transpose(kernel_out.reshape(3, 3, 3, C, C), (3, 4, 0, 1, 2))
    return (
        grad_field, grad_kernel, grad_offset[0], grad_lift, grad_liftbias[0], grad_style.T, grad_stylebias[0],
    )


def solution(mesh):
    cut = Mesh(mesh.devices.reshape(16, 2, 4, 4), ("glong", "ghi", "gy", "gz"))
    grid = P(None, ("glong", "ghi"), "gy", "gz")
    return jax.shard_map(
        body, mesh=cut, in_specs=(grid,) * 2 + (P(),) * 7, out_specs=(grid,) + (P(),) * 6, check_vma=False
    )
```

```python
import numpy as np
import jax
import jax.numpy as jnp
from jax import lax
from jax.experimental import pallas as pl
from jax.experimental.pallas import tpu as pltpu
from jax.sharding import Mesh, PartitionSpec as P

demod_eps = 1e-06
clip_eps = 1e-06

C = 32
TAPS = 27
EDGE = 6
FIELD_LANES = 12 * 8 * C
COT_LANES = 10 * 8 * C
OWN = 8 * 128
WITH_RIM = 9 * 128
f32 = jnp.float32
bf16 = jnp.bfloat16
VMEM = pl.BlockSpec(memory_space=pltpu.VMEM)


def call(kernel, outs, n_in, flops=0, limit=24, scratch=()):
    return pl.pallas_call(
        kernel,
        out_shape=outs,
        in_specs=[VMEM] * n_in,
        out_specs=[VMEM] * len(outs),
        scratch_shapes=list(scratch),
        cost_estimate=pl.CostEstimate(flops=flops, bytes_accessed=1 << 20, transcendentals=0),
        compiler_params=pltpu.CompilerParams(vmem_limit_bytes=limit * 1024 * 1024),
    )


def shape(*dims, dtype=bf16):
    return jax.ShapeDtypeStruct(dims, dtype)


def select(dims, row_axis, lane_axis, lanes):
    row = lax.broadcasted_iota(jnp.int32, dims, row_axis)
    lane = lax.broadcasted_iota(jnp.int32, dims, lane_axis)
    hit = jnp.zeros(dims, f32)
    for n, at in enumerate(lanes):
        if at is not None:
            hit = jnp.where((row == n) & (lane == at), 1.0, hit)
    return hit.astype(bf16)


def split_kernel(field_hbm, cot_hbm, low_ref, rest_ref, row_ref, corner_ref, field_ref, cot_ref, sems):
    fetches = (
        pltpu.make_async_copy(field_hbm, field_ref, sems.at[0]),
        pltpu.make_async_copy(cot_hbm, cot_ref, sems.at[1]),
    )
    for fetch in fetches:
        fetch.start()
    to = lax.broadcasted_iota(jnp.int32, (256, 256), 0)
    of = lax.broadcasted_iota(jnp.int32, (256, 256), 1)
    perm = jnp.where((of & 7) * C + (of >> 3) == to, 1.0, 0.0).astype(bf16)

    def rows(ref, x):
        block = ref[:, x].astype(f32).reshape(C * 8, 128).astype(bf16)
        return jnp.dot(perm, block, preferred_element_type=f32).astype(bf16).reshape(8, C, 128)

    fetches[0].wait()
    low_ref[0], low_ref[1], rest_ref[0] = (rows(field_ref, x) for x in range(3))
    fetches[1].wait()
    low_ref[2], rest_ref[1], rest_ref[2] = (rows(cot_ref, x) for x in range(3))
    for n, (ref, at) in enumerate(((low_ref, 0), (low_ref, 1), (rest_ref, 0))):
        row_ref[2 * n : 2 * n + 2] = ref[at, 0:2]
    row_ref[6], row_ref[7] = rest_ref[1, 0], rest_ref[2, 0]
    corner_ref[0:2], corner_ref[2:4], corner_ref[4] = low_ref[0, 0:2], low_ref[1, 0:2], low_ref[2, 0]
    corner_ref[5:9] = jnp.zeros((4, C, 128), bf16)


def planes(low_ref, rest_ref, right_ref):
    field = ((low_ref, 0), (low_ref, 1), (rest_ref, 0), (right_ref, 0), (right_ref, 1))
    cot = ((rest_ref, 1), (rest_ref, 2), (right_ref, 2))
    return field, cot


def gather_kernel(low_ref, rest_ref, right_ref, row_ref, corner_ref, _, field_out, cot_out, faces_ref):
    field, cot = planes(low_ref, rest_ref, right_ref)
    field_out[...] = jnp.zeros_like(field_out)
    cot_out[...] = jnp.zeros_like(cot_out)
    for n, (ref, at) in enumerate(field):
        for y in range(10):
            if y < 8:
                field_out[y, n] = ref[at, y]
            elif n < 3:
                field_out[y, n] = row_ref[2 * n + y - 8]
            else:
                field_out[y, n] = corner_ref[2 * (n - 3) + y - 8]
    for n, (ref, at) in enumerate(cot):
        for y in range(8):
            if y < 7:
                cot_out[y, n] = ref[at, y + 1]
            else:
                cot_out[y, n] = row_ref[6 + n] if n < 2 else corner_ref[4]

    def faces(lanes, rows):
        pick = select((8, 128), 0, 1, lanes)
        return lax.dot_general(
            pick, rows, (((1,), (1,)), ((), ())), preferred_element_type=f32
        )

    both = faces((126, 127, None, 0, 1, None), field_out[...].reshape(FIELD_LANES, 128))
    beside = faces((None, None, 127, None, None, 0), cot_out[...].reshape(COT_LANES, 128))
    both = jnp.concatenate([both[:, :COT_LANES] + beside, both[:, COT_LANES:]], axis=1)

    def chunk(first):
        return jnp.concatenate(
            [both[first : first + 4, y * 256 : y * 256 + 256] for y in range(12)], axis=0
        ).astype(bf16)

    me = lax.axis_index("gz")
    high = chunk(0)
    faces_ref[me] = high
    faces_ref[lax.rem(me + 1, 4)] = high
    faces_ref[lax.rem(me + 2, 4)] = jnp.zeros_like(high)
    faces_ref[lax.rem(me + 3, 4)] = chunk(3)


def silu_slope(values):
    logistic = jax.nn.sigmoid(values)
    return logistic * (1.0 + values * (1.0 - logistic))


def row_taps(ref, x, width):
    return jnp.concatenate(
        [ref[c, x, :, b * 128 : b * 128 + width] for b in range(3) for c in range(3)], axis=0
    )


def conv_kernel(
    field_ref, cot_ref, faces_ref, fwd_ref, offset_ref, place_ref,
    sums_ref, up_ref, send_ref,
    halo, shifted, edge, acc,
):
    me = lax.axis_index("gz")
    before, after = lax.rem(me + 3, 4), lax.rem(me + 1, 4)

    def across(rows, place):
        return lax.dot_general(rows, place, (((0,), (0,)), ((), ())), preferred_element_type=f32)

    sides = jnp.concatenate([faces_ref[at] for at in (before, me, after)], axis=0)
    spread = across(sides, place_ref[...])
    rim, rim_cot = spread[:, :128], spread[:, 128:256]
    halo[...] = spread[:, 256:].astype(bf16)
    lane = lax.broadcasted_iota(jnp.int32, (C, 128), 1)
    for x in range(5):
        for y in range(10):
            row = field_ref[y, x]
            at = slice(y * 128, y * 128 + 128)
            ends = halo[x * C : x * C + C, at]
            shifted[0, x, :, at] = jnp.where(lane == 0, ends, pltpu.roll(row, 1, 1))
            shifted[1, x, :, at] = row
            shifted[2, x, :, at] = jnp.where(lane == 127, ends, pltpu.roll(row, 127, 1))
        part = jnp.dot(fwd_ref[...], row_taps(shifted, x, OWN), preferred_element_type=f32)
        for a in range(3):
            if 0 <= x - a < 3:
                if a == 0:
                    acc[x] = part[:C]
                else:
                    acc[x - a] += part[a * C : a * C + C]

    for t in range(9):
        shift = (t // 3) * EDGE + t % 3
        edge[t] = (pltpu.roll(rim, 128 - shift, 1) if shift else rim).astype(bf16)
    block = jnp.concatenate(
        [jnp.concatenate([edge[t, x * C : x * C + C] for t in range(9)], axis=0) for x in range(5)], axis=1
    )
    part = jnp.dot(fwd_ref[...], block, preferred_element_type=f32)
    offset = offset_ref[...]
    rims = []
    for x in range(3):
        preact = offset + sum(
            part[a * C : a * C + C, (x + a) * 128 : (x + a) * 128 + 128] for a in range(3)
        )
        rims.append((rim_cot[x * C : x * C + C] * silu_slope(preact)).astype(bf16))

    ups = []
    for x in range(3):
        beside = jnp.concatenate([cot_ref[y, x] for y in range(8)], axis=1).astype(f32)
        upstream = (beside * silu_slope(acc[x] + offset)).astype(bf16)
        ups.append(upstream)
        up_ref[x, :, :OWN] = upstream
        up_ref[x, :, OWN:] = rims[x]
        if x:
            send_ref[x - 1, :, :OWN] = upstream
            send_ref[x - 1, :, OWN:] = rims[x]

    none = jnp.zeros((C, OWN), bf16)
    left = jnp.concatenate(
        [
            jnp.concatenate([ups[x - a] if 0 <= x - a < 3 else none for a in range(3)], axis=0)
            for x in range(5)
        ],
        axis=1,
    )
    right = jnp.concatenate([row_taps(shifted, x, OWN) for x in range(5)], axis=1)
    total = lax.dot_general(left, right, (((1,), (1,)), ((), ())), preferred_element_type=f32)

    offsets = sum(jnp.sum(ups[x].astype(f32), axis=1, keepdims=True) for x in range(3))
    packed = jnp.concatenate(
        [total[a * C : a * C + C] for a in range(3)] + [jnp.broadcast_to(offsets, (C, C))], axis=1
    )
    for s in range(4):
        for l in range(8):
            at = (s * 8 + l) * 8
            if l < 7:
                sums_ref[at : at + 8] = packed[8 * s : 8 * s + 8, 128 * l : 128 * l + 128]
            else:
                sums_ref[at : at + 8] = jnp.zeros((8, 128), f32)


def pack_up_kernel(up_ref, before_ref, last_ref):
    for x in range(5):
        ref, at = (before_ref, x) if x < 2 else (up_ref, x - 2)
        last_ref[x] = ref[at, :, 6 * 128 :]


def grad_kernel_body(up_ref, before_ref, below_ref, bwd_ref, grad_ref, shifted, acc):
    lane = lax.broadcasted_iota(jnp.int32, (C, 128), 1)
    for x in range(5):
        ref, from_x = (before_ref, x) if x < 2 else (up_ref, x - 2)
        rim = ref[from_x, :, OWN:].astype(f32)
        rim_below = below_ref[x, :, 256:].astype(f32)
        for y in range(10):
            at = slice(y * 128, y * 128 + 128)
            if y < 2:
                row = below_ref[x, :, at]
                ends, n = rim_below, (y + 6) * EDGE
            else:
                row = ref[from_x, :, (y - 2) * 128 : (y - 1) * 128]
                ends, n = rim, (y - 2) * EDGE
            low = jnp.broadcast_to(ends[:, n : n + 1], (C, 128)).astype(bf16)
            high = jnp.broadcast_to(ends[:, n + 3 : n + 4], (C, 128)).astype(bf16)
            shifted[0, x, :, at] = jnp.where(lane == 0, low, pltpu.roll(row, 1, 1))
            shifted[1, x, :, at] = row
            shifted[2, x, :, at] = jnp.where(lane == 127, high, pltpu.roll(row, 127, 1))
        part = jnp.dot(bwd_ref[...], row_taps(shifted, x, OWN), preferred_element_type=f32)
        for a in range(3):
            if 0 <= x - a < 3:
                if a == 0:
                    acc[x] = part[:C]
                else:
                    acc[x - a] += part[a * C : a * C + C]

    to = lax.broadcasted_iota(jnp.int32, (256, 256), 0)
    of = lax.broadcasted_iota(jnp.int32, (256, 256), 1)
    perm = jnp.where((to & 7) * C + (to >> 3) == of, 1.0, 0.0).astype(bf16)
    for x in range(3):
        rows = jnp.concatenate(
            [acc[x, :, y * 128 : y * 128 + 128] for y in range(8)], axis=0
        ).astype(bf16)
        moved = jnp.dot(perm, rows, preferred_element_type=f32)
        grad_ref[:, x] = moved.reshape(C, 8, 128).astype(bf16)


def identity():
    return jnp.where(
        lax.broadcasted_iota(jnp.int32, (C, C), 0) == lax.broadcasted_iota(jnp.int32, (C, C), 1), 1.0, 0.0
    )


def fill_places(place_ref):
    row = lax.broadcasted_iota(jnp.int32, (144, 128), 0)
    to = lax.broadcasted_iota(jnp.int32, (144, 128), 1)
    y, k = row >> 2, row & 3

    def place(moves):
        hit = jnp.zeros((144, 128), f32)
        for side, face, lane in moves:
            inside = (y >= side * 12) & (y < side * 12 + 12)
            hit = jnp.where(inside & (k == face) & (to == (y - side * 12) * EDGE + lane), 1.0, hit)
        return hit.astype(bf16)

    place_ref[:, :128] = place(((0, 0, 0), (0, 1, 1), (1, 3, 2), (1, 1, 3), (2, 0, 4), (2, 1, 5)))
    place_ref[:, 128:256] = place(((0, 2, 0), (2, 2, 3)))
    for n in range(12):
        ends = (to == 0) & (row == n * 4 + 1) | (to == 127) & (row == (24 + n) * 4)
        place_ref[:, 256 + n * 128 : 384 + n * 128] = jnp.where(ends, 1.0, 0.0).astype(bf16)


def modulate_kernel(
    cosmology_ref, lift_ref, bias_ref, weight_ref, sbias_ref, taps_ref, offset_ref,
    fwd_ref, bwd_ref, kernel_ref, modded_ref, styles_ref, inv_ref, lifted_ref, hidden_ref, params_ref, column_ref,
    place_ref,
):
    fill_places(place_ref)
    first, second = cosmology_ref[:, 0:1], cosmology_ref[:, 1:2]
    lifted = first * lift_ref[0:1] + second * lift_ref[1:2] + bias_ref[...]
    hidden = lifted * jax.nn.sigmoid(lifted)
    eye = identity()
    column = jnp.sum(weight_ref[...] * hidden, axis=1, keepdims=True)
    styles = jnp.sum(column * eye, axis=0, keepdims=True) + sbias_ref[...] + 1.0
    kernel = jnp.concatenate([taps_ref[t] for t in range(TAPS)] + [jnp.zeros((C, C), f32)], axis=1)
    styles = jnp.concatenate([styles] * TAPS + [jnp.zeros((1, C), f32)], axis=1)
    modded = kernel * styles
    inv = lax.rsqrt(jnp.sum(modded * modded, axis=1, keepdims=True) + demod_eps)
    scaled = (modded * inv).astype(bf16)
    for a in range(3):
        fwd_ref[a * C : a * C + C] = scaled[:, a * 288 : a * 288 + 288]
    turned = scaled.astype(f32).T
    for a in range(3):
        bwd_ref[a * C : a * C + C] = jnp.concatenate(
            [turned[(26 - a * 9 - t) * C : (27 - a * 9 - t) * C] for t in range(9)], axis=1
        ).astype(bf16)
    kernel_ref[...] = kernel
    modded_ref[...] = modded
    styles_ref[...] = styles
    inv_ref[...] = inv
    lifted_ref[...] = lifted
    hidden_ref[...] = hidden
    params_ref[...] = jnp.concatenate([first, second], axis=0)
    column_ref[...] = jnp.sum(offset_ref[...] * eye, axis=1, keepdims=True)


def total_kernel(parts_ref, spread_ref):
    part = jnp.sum(parts_ref[...], axis=0)
    for n in range(spread_ref.shape[0]):
        spread_ref[n] = part


def tail_kernel(
    sums_ref, kernel_ref, modded_ref, styles_ref, inv_ref, lifted_ref, hidden_ref, weight_ref, cosmology_ref,
    kernel_out, offset_out, lift_out, bias_out, style_out, sbias_out,
):
    def total(values):
        return jnp.sum(jnp.sum(values, axis=1, keepdims=True), axis=0, keepdims=True)

    sums = jnp.concatenate(
        [
            jnp.concatenate([sums_ref[(s * 8 + l) * 8 : (s * 8 + l) * 8 + 8] for s in range(4)], axis=0)
            for l in range(7)
        ],
        axis=1,
    )
    kernel, modded, styles, inv = kernel_ref[...], modded_ref[...], styles_ref[...], inv_ref[...]
    eye = identity()
    offset = jnp.sum(sums[:, TAPS * C : TAPS * C + C] * eye, axis=0, keepdims=True)
    projected = jnp.sum(sums * modded, axis=1, keepdims=True)
    mod_grad = inv * (sums - modded * (inv * inv * projected))
    raw = mod_grad * styles
    lanes = jnp.sum(mod_grad * kernel, axis=0, keepdims=True)
    folded = sum(lanes[:, 128 * l : 128 * l + 128] for l in range(7))
    row = sum(folded[:, C * n : C * n + C] for n in range(4))
    column = jnp.sum(row * eye, axis=1, keepdims=True)
    lifted_grad = jnp.sum(weight_ref[...] * column, axis=0, keepdims=True) * silu_slope(lifted_ref[...])
    style_raw = column * hidden_ref[...]
    lift_raw = cosmology_ref[...] * lifted_grad
    squares = sum(total(v * v) for v in (raw, offset, lift_raw, lifted_grad, style_raw, row))
    entries = TAPS * C * C + C + lift_raw.size + lifted_grad.size + style_raw.size + C
    factor = jnp.minimum(1.0, lax.rsqrt(squares / entries + clip_eps))
    raw = raw * factor
    for t in range(TAPS):
        kernel_out[t] = raw[:, C * t : C * t + C]
    offset_out[...] = offset * factor
    lift_out[...] = lift_raw * factor
    bias_out[...] = lifted_grad * factor
    style_out[...] = style_raw * factor
    sbias_out[...] = row * factor


def shifts(axis):
    n = lax.axis_size(axis)
    ahead = [(i, (i + 1) % n) for i in range(n)]
    return ahead, [(j, i) for i, j in ahead]


def summed(sums):
    flat = ("ghi", "gy", "gz")
    parts = lax.all_to_all(sums.reshape(32, 8, 128), flat, 0, 0, tiled=True)
    (spread,) = call(total_kernel, [shape(16, 8, 128, dtype=f32)], 1, limit=4)(parts)
    parts = lax.all_to_all(spread, "glong", 0, 0, tiled=True)
    (spread,) = call(total_kernel, [shape(32, 8, 128, dtype=f32)], 1, limit=4)(parts)
    return lax.all_to_all(spread, flat, 0, 0, tiled=True).reshape(256, 128)


def body(
    field, cotangent, cosmology, lift_weight, lift_bias, style_weight, style_bias, kernel, offset
):
    low, rest, row, corner = pl.pallas_call(
        split_kernel,
        out_shape=[shape(3, 8, C, 128), shape(3, 8, C, 128), shape(8, C, 128), shape(9, C, 128)],
        in_specs=[pl.BlockSpec(memory_space=pltpu.HBM)] * 2,
        out_specs=[VMEM] * 4,
        scratch_shapes=[
            pltpu.VMEM((C, 3, 8, 128), bf16), pltpu.VMEM((C, 3, 8, 128), bf16), pltpu.SemaphoreType.DMA((2,)),
        ],
        compiler_params=pltpu.CompilerParams(vmem_limit_bytes=4 * 1024 * 1024),
    )(*(pltpu.with_memory_space_constraint(block, pltpu.HBM) for block in (field, cotangent)))
    x_ahead, back = shifts(("glong", "ghi"))
    right = lax.ppermute(low, ("glong", "ghi"), back)

    taps = jnp.transpose(kernel, (2, 3, 4, 0, 1)).reshape(TAPS, C, C)
    fwd, bwd, packed, modded, styles, inv_norm, lifted, hidden, params, column, place = call(
        modulate_kernel,
        [
            shape(3 * C, 9 * C), shape(3 * C, 9 * C), shape(C, 896, dtype=f32), shape(C, 896, dtype=f32),
            shape(1, 896, dtype=f32), shape(C, 1, dtype=f32), shape(1, 256, dtype=f32), shape(1, 256, dtype=f32),
            shape(2, 1, dtype=f32), shape(C, 1, dtype=f32), shape(144, 14 * 128),
        ],
        7,
        limit=8,
    )(
        cosmology[None, :], lift_weight, lift_bias[None, :], style_weight.T, style_bias[None, :], taps,
        offset[None, :],
    )

    diagonal = [(4 * i + j, 4 * ((i + 31) % 32) + (j + 3) % 4) for i in range(32) for j in range(4)]
    corner = lax.ppermute(corner, ("glong", "ghi", "gy"), diagonal)
    y_ahead, back = shifts("gy")
    row = lax.ppermute(row, "gy", back)

    field_rows, cot_rows, faces = call(
        gather_kernel, [shape(12, 8, C, 128), shape(10, 8, C, 128), shape(4, 48, 256)], 6
    )(low, rest, right, row, corner, column)
    faces = lax.all_to_all(faces, "gz", 0, 0, tiled=True)

    sums, upstream, send = call(
        conv_kernel,
        [shape(256, 128, dtype=f32), shape(3, C, WITH_RIM), shape(2, C, WITH_RIM)],
        6,
        flops=540_000_000,
        scratch=[
            pltpu.VMEM((8 * C, 12 * 128), bf16),
            pltpu.VMEM((3, 5, C, 10 * 128), bf16),
            pltpu.VMEM((9, 8 * C, 128), bf16),
            pltpu.VMEM((3, C, OWN), f32),
        ],
    )(field_rows, cot_rows, faces, fwd, column, place)
    before = lax.ppermute(send, ("glong", "ghi"), x_ahead)
    (last,) = call(pack_up_kernel, [shape(5, C, 3 * 128)], 2, limit=4)(upstream, before)
    below = lax.ppermute(last, "gy", y_ahead)
    (grad_field,) = call(
        grad_kernel_body,
        [shape(C, 3, 8, 128)],
        4,
        flops=170_000_000,
        scratch=[pltpu.VMEM((3, 5, C, 10 * 128), bf16), pltpu.VMEM((3, C, OWN), f32)],
    )(upstream, before, below, bwd)

    kernel_out, grad_offset, grad_lift, grad_liftbias, grad_style, grad_stylebias = call(
        tail_kernel,
        [
            shape(TAPS, C, C, dtype=f32), shape(1, C, dtype=f32), shape(2, 256, dtype=f32),
            shape(1, 256, dtype=f32), shape(C, 256, dtype=f32), shape(1, C, dtype=f32),
        ],
        9,
        limit=8,
    )(
        summed(sums), packed, modded, styles, inv_norm, lifted, hidden, style_weight.T, params,
    )
    grad_kernel = jnp.transpose(kernel_out.reshape(3, 3, 3, C, C), (3, 4, 0, 1, 2))
    return (
        grad_field, grad_kernel, grad_offset[0], grad_lift, grad_liftbias[0], grad_style.T, grad_stylebias[0],
    )


def solution(mesh):
    cut = Mesh(mesh.devices.reshape(16, 2, 4, 4), ("glong", "ghi", "gy", "gz"))
    grid = P(None, ("glong", "ghi"), "gy", "gz")
    return jax.shard_map(
        body, mesh=cut, in_specs=(grid,) * 2 + (P(),) * 7, out_specs=(grid,) + (P(),) * 6, check_vma=False
    )
```
